32 devices in a mesh: gx: 4 (over y, core), gy: 8 (over z, x).
Axes of the slice: x: 2, y: 2, z: 4, core: 2. Of those that a mesh axis runs over, the one named last changes fastest.
Arguments:
- cotangent: float32 [6, 8, 512, 512], P(None, None, 'gy', 'gx'), may hold values from -6 to 6
- permeability: float32 [6, 512, 512], P(None, 'gy', 'gx'), may hold values from 0.2 to 5
- well_mask: int32 [512, 512], P('gy', 'gx'), may hold values 0 or 1
- diag_block: bfloat16 [6, 8, 8, 512, 512], P(None, None, None, 'gy', 'gx'), may hold values from -2 to 2
- flux_block: bfloat16 [6, 8, 8, 512, 512], P(None, None, None, 'gy', 'gx'), may hold values from -0.875 to 0.875
- cell_list: int32 [8, 4, 4096], P('gy', 'gx'), may hold values from 0 to 49151, as said below
- block_count: int32 [8, 4], P('gy', 'gx'), may hold values from 16 to 32, as said below
- helper_of: int32 [8, 4, 32], P('gy', 'gx'), may hold values from 0 to 31, as said below
- flash_inverse: bfloat16 [8, 4, 32, 8, 8, 128], P('gy', 'gx'), may hold values from -2 to 2
- flash_coupling: bfloat16 [8, 4, 32, 8, 8, 128], P('gy', 'gx'), may hold values from -2 to 2
- phase_state: bfloat16 [8, 4, 32, 8, 128], P('gy', 'gx'), may hold values from 0.049804688 to 1
Outputs:
- adjoint: float32 [6, 8, 512, 512], P(None, None, 'gy', 'gx')
- interaction_grad: float32 [8, 8], replicated
The draws below stay inside these ranges and needn't reach their ends.
Inputs may be any that keep to these rules, and one draw needn't show every extreme that they name: `cell_list`: within one brick the 4096 entries are distinct cells of that brick. `block_count`: some brick has 32 live blocks. `helper_of`: each brick's row is a permutation of all helpers; helper h is the device at gx index h // 8 and gy index h % 8.
All inputs are finite; a program needn't handle non-finite values. No bound on the sum of `well_mask` on one device may be relied on, other than what follows from the above.
Results may differ from the reference program's by a relative error of at most 0.0075.
Values may be sent and summed in bfloat16 or wider, within the bound.
No kernel may reach another device: no remote copies, remote signals or barrier semaphores. Data moves between devices by JAX's collectives and lax.ppermute only.
A program may use at most 192 MiB of HBM per device.

```python
import math
import jax
import jax.numpy as jnp
from jax import lax

NC = 8
BLK = 128
LAYERS = 6
CY = 64
CX = 128
NY = 512
NX = 512
BRICKS_Y = 8
BRICKS_X = 4
BLK_MOST = 32
SLOTS = 4096
CELLS = 49152


def draw_cell_list(key, part):
    brick_keys = jax.random.split(jax.random.fold_in(key, 11), BRICKS_Y * BRICKS_X)

    def one_brick(brick_key):
        return jax.random.permutation(brick_key, LAYERS * CY * CX)[:SLOTS].astype(jnp.int32)
    return jax.vmap(one_brick)(brick_keys).reshape(BRICKS_Y, BRICKS_X, SLOTS)


def draw_block_count(key, part):
    count_key = jax.random.fold_in(key, 23)
    first_key, second_key = jax.random.split(count_key)
    counts = jax.random.randint(first_key, (BRICKS_Y * BRICKS_X,), BLK_MOST // 2, BLK_MOST + 1)
    chosen = jax.random.randint(second_key, (), 0, BRICKS_Y * BRICKS_X)
    counts = counts.at[chosen].set(BLK_MOST)
    return counts.reshape(BRICKS_Y, BRICKS_X).astype(jnp.int32)


def draw_helper_of(key, part):
    brick_keys = jax.random.split(jax.random.fold_in(key, 37), BRICKS_Y * BRICKS_X)

    def one_brick(brick_key):
        return jax.random.permutation(brick_key, BLK_MOST).astype(jnp.int32)
    return jax.vmap(one_brick)(brick_keys).reshape(BRICKS_Y, BRICKS_X, BLK_MOST)


def plant(values, own_key, low, high):
    longest = values.shape.index(max(values.shape))
    spots = []
    for shift in (0, 1):
        where = [jax.random.randint(jax.random.fold_in(own_key, axis), (), 0, length) for axis, length in enumerate(values.shape)]
        where[longest] = (where[longest] + shift) % values.shape[longest]
        spots.append(tuple(where))
    return values.at[spots[0]].set(low).at[spots[1]].set(high)


def levels(key, extent, cuts, low, largest):
    loudness, own = 1.0, jax.random.fold_in(key, 6)
    for position, parts in cuts:
        heights = jnp.exp(jax.random.uniform(jax.random.fold_in(own, position), (parts,), jnp.float32, low / len(cuts), largest / len(cuts)))
        loudness = loudness * jnp.repeat(heights, extent[position] // parts).reshape([-1 if axis == position else 1 for axis in range(len(extent))])
    return loudness


def gaussian(own_key, shape, deviation, limit, pieces=(), held_as=jnp.bfloat16):
    values = jax.random.normal(own_key, shape, jnp.float32) * deviation
    if len(pieces) > 0:
        values = levels(own_key, shape, pieces, -0.22, 0.18) * values
    return jnp.clip(values, min=-limit, max=limit).astype(held_as)


def setup_inputs(seed: int = 0) -> dict:
    key_of = jax.random.split(jax.random.key(seed), 12)
    cotangent = gaussian(key_of[0], (LAYERS, NC, NY, NX), 1.0, 6.0, ((2, 8), (3, 4)), jnp.float32)
    permeability = jnp.clip(jnp.exp(math.log(5.0) - 3.218876 * jax.random.uniform(key_of[1], (LAYERS, NY, NX), jnp.float32) ** levels(key_of[1], (LAYERS, NY, NX), ((1, 8), (2, 4)), -0.2, 0.2)), 0.2, 5.0)
    well_mask = plant((jax.random.randint(key_of[2], (NY, NX), 0, 16) < 1).astype(jnp.int32), jax.random.fold_in(key_of[2], 1), 0, 1)
    diag_block = gaussian(key_of[3], (LAYERS, NC, NC, NY, NX), NC ** -0.5, 2.0, ((3, 8), (4, 4)))
    flux_block = gaussian(key_of[4], (LAYERS, NC, NC, NY, NX), (6 * NC) ** -0.5, 0.875, ((3, 8), (4, 4)))
    cell_list = draw_cell_list(jax.random.fold_in(key_of[11], 71), 0)
    block_count = draw_block_count(jax.random.fold_in(key_of[11], 71), 0)
    helper_of = draw_helper_of(jax.random.fold_in(key_of[11], 71), 0)
    flash_inverse = gaussian(key_of[8], (BRICKS_Y, BRICKS_X, BLK_MOST, NC, NC, BLK), NC ** -0.5, 2.0, ((0, 8), (1, 4)))
    flash_coupling = gaussian(key_of[9], (BRICKS_Y, BRICKS_X, BLK_MOST, NC, NC, BLK), NC ** -0.5, 2.0, ((0, 8), (1, 4)))
    phase_state = jnp.clip(0.049804688 + 0.9501953 * jax.random.uniform(key_of[10], (BRICKS_Y, BRICKS_X, BLK_MOST, NC, BLK), jnp.float32) ** levels(key_of[10], (BRICKS_Y, BRICKS_X, BLK_MOST, NC, BLK), ((0, 8), (1, 4)), -0.2, 0.2), 0.049804688, 1.0).astype(jnp.bfloat16)
    return dict(cotangent=cotangent, permeability=permeability, well_mask=well_mask, diag_block=diag_block, flux_block=flux_block, cell_list=cell_list, block_count=block_count, helper_of=helper_of, flash_inverse=flash_inverse, flash_coupling=flash_coupling, phase_state=phase_state)


OFFSETS = ((1, 0, 0), (-1, 0, 0), (0, 1, 0), (0, -1, 0), (0, 0, 1), (0, 0, -1))

def transmissibility(padded_perm, layers, rows_y, cols_x):
    centre = padded_perm[1:1 + layers, 1:1 + rows_y, 1:1 + cols_x]
    result = []
    for step_z, step_y, step_x in OFFSETS:
        beside = padded_perm[1 + step_z:1 + step_z + layers, 1 + step_y:1 + step_y + rows_y, 1 + step_x:1 + step_x + cols_x]
        result.append(2.0 * centre * beside / (centre + beside))
    return result

def neighbour_sum(padded, trans_list, layers, rows_y, cols_x):
    summed = jnp.zeros((layers, padded.shape[1], rows_y, cols_x), jnp.float32)
    for weights, (step_z, step_y, step_x) in zip(trans_list, OFFSETS):
        beside = padded[1 + step_z:1 + step_z + layers, :, 1 + step_y:1 + step_y + rows_y, 1 + step_x:1 + step_x + cols_x]
        summed = summed + weights[:, None] * beside
    return summed

def blocks_transposed(blocks, source_field):

    def layer_term(layer_pair):
        return lax.optimization_barrier(jnp.sum(layer_pair[0].astype(jnp.float32) * layer_pair[1][:, None], axis=0))
    return lax.map(layer_term, (blocks, source_field))

def apply_transposed(source_field, well_field, trans_list, diag_block, flux_block):
    layers, components, rows_y, cols_x = source_field.shape
    masked = source_field * (1.0 - well_field)
    padded = jnp.pad(masked, ((1, 1), (0, 0), (1, 1), (1, 1)))
    summed = neighbour_sum(padded, trans_list, layers, rows_y, cols_x)
    return blocks_transposed(diag_block, masked) - blocks_transposed(flux_block, summed) + well_field * source_field

def flash_terms(inverse, coupling, chosen, phase_rows):
    multiplier = jnp.einsum('nrck,nrk->nck', inverse.astype(jnp.float32), chosen.astype(jnp.float32))
    correction = (-jnp.einsum('nrck,nrk->nck', coupling.astype(jnp.float32), multiplier)).astype(jnp.bfloat16)
    state_wide = phase_rows.astype(jnp.float32)
    partial_sum = jnp.einsum('nik,njk->ij', multiplier * state_wide, state_wide)
    return (correction, partial_sum)

def reference(cotangent, permeability, well_mask, diag_block, flux_block, cell_list, block_count, helper_of, flash_inverse, flash_coupling, phase_state):
    well_field = well_mask.astype(jnp.float32)
    layers, components, total_y, total_x = cotangent.shape
    trans_list = transmissibility(jnp.pad(permeability, 1), layers, total_y, total_x)
    first_apply = apply_transposed(cotangent, well_field, trans_list, diag_block, flux_block)
    bricks = first_apply.reshape(layers, components, BRICKS_Y, CY, BRICKS_X, CX).transpose(2, 4, 1, 0, 3, 5).reshape(BRICKS_Y, BRICKS_X, components, CELLS)
    gather_index = jnp.broadcast_to(cell_list[:, :, None, :], (BRICKS_Y, BRICKS_X, components, SLOTS))
    picked = jnp.take_along_axis(bricks, gather_index, axis=3)
    picked = picked.reshape(BRICKS_Y, BRICKS_X, components, BLK_MOST, BLK).transpose(0, 1, 3, 2, 4)
    live_slots = jnp.arange(BLK_MOST, dtype=jnp.int32)[None, None, :] < block_count[:, :, None]
    picked = jnp.where(live_slots[:, :, :, None, None], picked, 0.0).astype(jnp.bfloat16)
    brick_y = jnp.arange(BRICKS_Y, dtype=jnp.int32)[:, None, None]
    brick_x = jnp.arange(BRICKS_X, dtype=jnp.int32)[None, :, None]
    source = jnp.broadcast_to(brick_x * BRICKS_Y + brick_y, (BRICKS_Y, BRICKS_X, BLK_MOST)).astype(jnp.int32)
    helper_y = (helper_of % BRICKS_Y).astype(jnp.int32)
    helper_x = (helper_of // BRICKS_Y).astype(jnp.int32)
    at_helper = jnp.zeros((BRICKS_Y, BRICKS_X, BLK_MOST, components, BLK), jnp.bfloat16).at[helper_y, helper_x, source].set(picked)

    def helper_row(row_group):
        inverse, coupling, chosen, phase_rows = row_group
        correction, partial_sum = flash_terms(inverse.reshape(-1, components, components, BLK), coupling.reshape(-1, components, components, BLK), chosen.reshape(-1, components, BLK), phase_rows.reshape(-1, components, BLK))
        return (correction.reshape(BRICKS_X, BLK_MOST, components, BLK), partial_sum)
    corrections_h, partials = lax.map(helper_row, (flash_inverse, flash_coupling, at_helper, phase_state))
    grad_scale = 1.0 / math.sqrt(BLK * BLK_MOST * BLK_MOST)
    interaction_grad = -grad_scale * lax.optimization_barrier(jnp.sum(partials, axis=0))
    corrections = corrections_h[helper_y, helper_x, source]
    values = corrections.transpose(0, 1, 3, 2, 4).reshape(BRICKS_Y, BRICKS_X, components, SLOTS).astype(jnp.float32)

    def add_cells(cells_row, where_cells, amount):
        return cells_row.at[:, where_cells].add(amount)
    updated = jax.vmap(jax.vmap(add_cells))(bricks, cell_list, values)
    second = updated.reshape(BRICKS_Y, BRICKS_X, components, layers, CY, CX).transpose(3, 2, 0, 4, 1, 5).reshape(layers, components, total_y, total_x)
    adjoint = apply_transposed(second, well_field, trans_list, diag_block, flux_block)
    return (adjoint, interaction_grad)
```

```python
import functools
import math

import jax
import jax.numpy as jnp
from jax import lax
from jax.experimental import pallas as pl
from jax.experimental.pallas import tpu as pltpu
from jax.sharding import PartitionSpec as P

F32 = jnp.float32
BF16 = jnp.bfloat16
AXES = ("gx", "gy")
MIB = 1024 * 1024
CHUNK = 512


def params(mib):
    return pltpu.CompilerParams(vmem_limit_bytes=mib * MIB)


def cost(flops, moved):
    return pl.CostEstimate(flops=int(flops), bytes_accessed=int(moved), transcendentals=0)


def product_kernel(inverse_ref, coupling_ref, out_ref):
    blocks, comps = inverse_ref.shape[:2]

    def one(b, carry):
        inverse = inverse_ref[b].astype(F32)
        coupling = coupling_ref[b].astype(F32)
        for r in range(comps):
            row = inverse[r, 0:1] * coupling[0]
            for m in range(1, comps):
                row += inverse[r, m : m + 1] * coupling[m]
            out_ref[b, r] = row.astype(BF16)
        return carry

    lax.fori_loop(0, blocks, one, 0)


def flash_product(inverse, coupling):
    return pl.pallas_call(
        product_kernel,
        out_shape=jax.ShapeDtypeStruct(inverse.shape, BF16),
        compiler_params=params(24),
        cost_estimate=cost(16 * inverse.size, 6 * inverse.size),
    )(inverse, coupling)


def write_edges(field, clear, perm_ref, low_y, high_y, low_x, high_x):
    layers, rows, cols = perm_ref.shape
    comps = low_y.shape[0] // layers - 1
    lane = lax.broadcasted_iota(jnp.int32, (rows, cols), 1)
    left = jnp.zeros((rows, cols), F32)
    right = jnp.zeros((rows, cols), F32)
    for k in range(layers):
        for c in range(comps + 1):
            if c < comps:
                value, at = field(k, c) * clear, k * comps + c
            else:
                value, at = perm_ref[k], layers * comps + k
            low_y[at : at + 1, :] = value[0:1]
            high_y[at : at + 1, :] = value[rows - 1 : rows]
            left = jnp.where(lane == at, value[:, 0:1], left)
            right = jnp.where(lane == at, value[:, cols - 1 : cols], right)
    low_x[...] = left
    high_x[...] = right


def edges_kernel(field_ref, mask_ref, perm_ref, low_y, high_y, low_x, high_x):
    clear = 1.0 - mask_ref[...].astype(F32)
    write_edges(lambda k, c: field_ref[k, c], clear, perm_ref, low_y, high_y, low_x, high_x)


def edge_shapes(layers, comps, rows, cols):
    along_y = jax.ShapeDtypeStruct((layers * (comps + 1), cols), F32)
    along_x = jax.ShapeDtypeStruct((rows, cols), F32)
    return [along_y, along_y, along_x, along_x]


def edges(field, mask, perm):
    return pl.pallas_call(
        edges_kernel,
        out_shape=edge_shapes(*field.shape),
        compiler_params=params(24),
        cost_estimate=cost(4 * field.size, 4 * field.size),
    )(field, mask, perm)


def exchange(sides):
    low_y, high_y, low_x, high_x = sides

    def both(low, high, axis):
        count = lax.axis_size(axis)
        up = [(i, i + 1) for i in range(count - 1)]
        down = [(j, i) for i, j in up]
        return lax.ppermute(high, axis, up), lax.ppermute(low, axis, down)

    return (*both(low_y, high_y, "gy"), *both(low_x, high_x, "gx"))


TILE = 16


def diag_kernel(field_ref, mask_ref, block_ref, out_ref):
    comps, rows = field_ref.shape[1:3]
    for y in range(0, rows, TILE):
        here = slice(y, y + TILE)
        well = mask_ref[here].astype(F32)
        values = [field_ref[0, c, here] for c in range(comps)]
        total = [well * value for value in values]
        for r in range(comps):
            source = values[r] * (1.0 - well)
            for c in range(comps):
                total[c] += block_ref[0, r, c, here].astype(F32) * source
        for c in range(comps):
            out_ref[0, c, here] = total[c]


def diag_part(field, mask, block):
    layers, comps, rows, cols = field.shape
    layer = pl.BlockSpec((1, comps, rows, cols), lambda k: (k, 0, 0, 0))
    return pl.pallas_call(
        diag_kernel,
        grid=(layers,),
        in_specs=[
            layer,
            pl.BlockSpec((rows, cols), lambda k: (0, 0)),
            pl.BlockSpec((1, comps, comps, rows, cols), lambda k: (k, 0, 0, 0, 0)),
        ],
        out_specs=layer,
        out_shape=jax.ShapeDtypeStruct(field.shape, F32),
        compiler_params=params(24),
        cost_estimate=cost(2 * block.size, 2 * block.size + 8 * field.size),
    )(field, mask, block)


def flux_kernel(want_rounded, before_ref, field_ref, mask_ref, perm_ref, low_y, high_y, low_x, high_x, block_ref, *rest):
    if want_rounded:
        out_ref, rounded_ref, padded, padded_perm = rest
    else:
        out_ref, padded, padded_perm = rest
    layers, comps, rows, cols = field_ref.shape
    top = 8
    k = pl.program_id(0)
    above = jnp.minimum(k + 1, layers - 1)
    below = jnp.maximum(k - 1, 0)
    clear = 1.0 - mask_ref[...].astype(F32)
    for c in range(comps):
        padded[c, top : top + rows] = field_ref[k, c] * clear
        padded[c, top - 1 : top] = low_y[pl.ds(k * comps + c, 1)]
        padded[c, top + rows : top + rows + 1] = high_y[pl.ds(k * comps + c, 1)]
    padded_perm[top : top + rows] = perm_ref[k]
    padded_perm[top - 1 : top] = low_y[pl.ds(layers * comps + k, 1)]
    padded_perm[top + rows : top + rows + 1] = high_y[pl.ds(layers * comps + k, 1)]
    lane = lax.broadcasted_iota(jnp.int32, (TILE, cols), 1)
    is_first, is_last = lane == 0, lane == cols - 1
    turn_field = lax.rem(cols - k * comps, cols)
    turn_perm = lax.rem(cols - (layers * comps + k), cols)

    def weight(centre, beside):
        return 2.0 * centre * beside / (centre + beside)

    for y in range(0, rows, TILE):
        here = slice(y, y + TILE)
        at = top + y
        free = 1.0 - mask_ref[here].astype(F32)
        low_field, high_field = (pltpu.roll(ref[here], turn_field, 1) for ref in (low_x, high_x))
        low_perm, high_perm = (pltpu.roll(ref[here], turn_perm, 1) for ref in (low_x, high_x))

        def beside_x(value, low, high):
            return (
                jnp.where(is_first, low, pltpu.roll(value, 1, 1)),
                jnp.where(is_last, high, pltpu.roll(value, cols - 1, 1)),
            )

        centre = perm_ref[k, here]
        perm_left, perm_right = beside_x(centre, low_perm[:, 0:1], high_perm[:, 0:1])
        weights = [
            jnp.where(k < layers - 1, weight(centre, perm_ref[above, here]), 0.0) * free,
            jnp.where(k > 0, weight(centre, perm_ref[below, here]), 0.0) * free,
            weight(centre, padded_perm[at + 1 : at + 1 + TILE]),
            weight(centre, padded_perm[at - 1 : at - 1 + TILE]),
            weight(centre, perm_right),
            weight(centre, perm_left),
        ]
        total = [None] * comps
        for r in range(comps):
            own = padded[r, at : at + TILE]
            left, right = beside_x(own, low_field[:, r : r + 1], high_field[:, r : r + 1])
            summed = (
                weights[0] * field_ref[above, r, here]
                + weights[1] * field_ref[below, r, here]
                + weights[2] * padded[r, at + 1 : at + 1 + TILE]
                + weights[3] * padded[r, at - 1 : at - 1 + TILE]
                + weights[4] * right
                + weights[5] * left
            )
            for c in range(comps):
                term = block_ref[0, r, c, here].astype(F32) * summed
                total[c] = term if r == 0 else total[c] + term
        for c in range(comps):
            value = before_ref[0, c, here] - total[c]
            out_ref[0, c, here] = value
            if want_rounded:
                rounded_ref[c * rows + y : c * rows + y + TILE, :] = value.astype(BF16)


def flux_part(before, field, mask, perm, halos, block, want_rounded):
    layers, comps, rows, cols = field.shape
    layer = pl.BlockSpec((1, comps, rows, cols), lambda k: (k, 0, 0, 0))

    def whole(array):
        return pl.BlockSpec(array.shape, lambda k: (0,) * array.ndim)

    out_specs = [layer]
    out_shape = [jax.ShapeDtypeStruct(field.shape, F32)]
    if want_rounded:
        out_specs.append(pl.BlockSpec((comps * rows, cols), lambda k: (0, k)))
        out_shape.append(jax.ShapeDtypeStruct((comps * rows, layers * cols), BF16))
    return pl.pallas_call(
        functools.partial(flux_kernel, want_rounded),
        grid=(layers,),
        in_specs=[
            layer,
            whole(field),
            whole(mask),
            whole(perm),
            *(whole(halo) for halo in halos),
            pl.BlockSpec((1, comps, comps, rows, cols), lambda k: (k, 0, 0, 0, 0)),
        ],
        out_specs=out_specs,
        out_shape=out_shape,
        scratch_shapes=[
            pltpu.VMEM((comps, rows + 16, cols), F32),
            pltpu.VMEM((rows + 16, cols), F32),
        ],
        compiler_params=params(24),
        cost_estimate=cost(4 * block.size, 2 * block.size + 12 * field.size),
    )(before, field, mask, perm, *halos, block)


def split_cells(cells, rows, cols):
    layer = cells // (rows * cols)
    y = (cells // cols) % rows
    return layer * cols + cells % cols, y


def one_hot(column, count, slots):
    number = lax.broadcasted_iota(jnp.int32, (count, slots), 0)
    return jnp.where(number == column, 1.0, 0.0).astype(BF16)


def gather_kernel(rows, cols, helper_ref, count_ref, cells_ref, rounded_ref, picked_ref, sent_ref):
    chunks, _, slots = cells_ref.shape
    width = picked_ref.shape[-1]
    comps = picked_ref.shape[1]
    per_chunk = slots // width
    row_number = lax.broadcasted_iota(jnp.int32, (rows, slots), 0)

    def one(i, carry):
        column, y = split_cells(cells_ref[i], rows, cols)
        chosen = one_hot(column, rounded_ref.shape[1], slots)
        found = jnp.dot(rounded_ref[...], chosen, preferred_element_type=F32)
        at_row = row_number == y
        values = [
            jnp.sum(jnp.where(at_row, found[c * rows : (c + 1) * rows], 0.0), axis=0, keepdims=True)
            for c in range(comps)
        ]
        values = jnp.concatenate(values, axis=0)
        for j in range(per_chunk):
            b = i * per_chunk + j
            live = jnp.where(b < count_ref[0, 0], 1.0, 0.0)
            value = (values[:, j * width : (j + 1) * width] * live).astype(BF16)
            picked_ref[b] = value
            sent_ref[helper_ref[0, 0, b]] = value
        return carry

    lax.fori_loop(0, chunks, one, 0)


def gather(rounded, cells, helper, count, comps, rows, cols, width):
    blocks = helper.shape[-1]
    shape = jax.ShapeDtypeStruct((blocks, comps, width), BF16)
    smem = pl.BlockSpec(memory_space=pltpu.SMEM)
    vmem = pl.BlockSpec(memory_space=pltpu.VMEM)
    return pl.pallas_call(
        functools.partial(gather_kernel, rows, cols),
        in_specs=[smem, smem, vmem, vmem],
        out_specs=[vmem, vmem],
        out_shape=[shape, shape],
        compiler_params=params(32),
        cost_estimate=cost(2 * rounded.size * cells.size, 2 * rounded.size),
    )(helper, count, cells, rounded)


def scatter_kernel(
    helper_ref, cells_ref, picked_ref, home_ref, first_ref, mask_ref, perm_ref, second_ref, low_y, high_y, low_x, high_x, added
):
    layers, comps, rows, cols = first_ref.shape
    chunks, _, slots = cells_ref.shape
    width = picked_ref.shape[-1]
    per_chunk = slots // width
    row_number = lax.broadcasted_iota(jnp.int32, (rows, slots), 0)
    added[...] = jnp.zeros_like(added)

    def one(i, carry):
        column, y = split_cells(cells_ref[i], rows, cols)
        chosen = one_hot(column, added.shape[1], slots)
        parts = []
        for j in range(per_chunk):
            b = i * per_chunk + j
            home = home_ref[helper_ref[0, 0, b]].astype(F32)
            value = picked_ref[b].astype(F32)
            part = home[0] * value[0:1]
            for r in range(1, comps):
                part += home[r] * value[r : r + 1]
            parts.append((-part).astype(BF16).astype(F32))
        correction = jnp.concatenate(parts, axis=1)
        at_row = row_number == y
        spread = jnp.concatenate(
            [jnp.where(at_row, correction[c : c + 1], 0.0).astype(BF16) for c in range(comps)], axis=0
        )
        added[...] += lax.dot_general(spread, chosen, (((1,), (1,)), ((), ())), preferred_element_type=F32)
        return carry

    lax.fori_loop(0, chunks, one, 0)
    for k in range(layers):
        for c in range(comps):
            second_ref[k, c] = first_ref[k, c] + added[c * rows : (c + 1) * rows, k * cols : (k + 1) * cols]
    clear = 1.0 - mask_ref[...].astype(F32)
    write_edges(lambda k, c: second_ref[k, c], clear, perm_ref, low_y, high_y, low_x, high_x)


def scatter(first, picked, home, helper, cells, mask, perm):
    layers, comps, rows, cols = first.shape
    smem = pl.BlockSpec(memory_space=pltpu.SMEM)
    vmem = pl.BlockSpec(memory_space=pltpu.VMEM)
    return pl.pallas_call(
        scatter_kernel,
        in_specs=[smem] + [vmem] * 6,
        out_specs=[vmem] * 5,
        out_shape=[jax.ShapeDtypeStruct(first.shape, F32), *edge_shapes(*first.shape)],
        scratch_shapes=[pltpu.VMEM((comps * rows, layers * cols), F32)],
        compiler_params=params(40),
        cost_estimate=cost(2 * first.size * cells.size, 8 * first.size),
    )(helper, cells, picked, home, first, mask, perm)


def grad_kernel(inverse_ref, state_ref, picked_ref, out_ref):
    blocks, comps = inverse_ref.shape[:2]
    width = inverse_ref.shape[-1]

    def one(b, totals):
        inverse = inverse_ref[b].astype(F32)
        value = picked_ref[b].astype(F32)
        state = state_ref[b].astype(F32)
        part = inverse[0] * value[0:1]
        for r in range(1, comps):
            part += inverse[r] * value[r : r + 1]
        part *= state
        return tuple(totals[j] + part * state[j : j + 1] for j in range(comps))

    totals = lax.fori_loop(0, blocks, one, (jnp.zeros((comps, width), F32),) * comps)
    lane = lax.broadcasted_iota(jnp.int32, (comps, width), 1)
    result = jnp.zeros((comps, width), F32)
    for j in range(comps):
        result = jnp.where(lane == j, jnp.sum(totals[j], axis=1, keepdims=True), result)
    out_ref[...] = result


def grad_part(inverse, state, picked):
    return pl.pallas_call(
        grad_kernel,
        out_shape=jax.ShapeDtypeStruct((inverse.shape[1], inverse.shape[-1]), F32),
        compiler_params=params(24),
        cost_estimate=cost(4 * inverse.size, 2 * inverse.size),
    )(inverse, state, picked)


def shards(
    cotangent,
    permeability,
    well_mask,
    diag_block,
    flux_block,
    cell_list,
    block_count,
    helper_of,
    flash_inverse,
    flash_coupling,
    phase_state,
):
    layers, comps, rows, cols = cotangent.shape
    blocks, width = helper_of.shape[-1], flash_inverse.shape[-1]
    inverse = flash_inverse.reshape(blocks, comps, comps, width)
    coupling = flash_coupling.reshape(blocks, comps, comps, width)
    state = phase_state.reshape(blocks, comps, width)
    cells = cell_list.reshape(-1, 1, min(CHUNK, cell_list.shape[-1]))

    def to_partners(array):
        return lax.all_to_all(array, AXES, split_axis=0, concat_axis=0, tiled=True)

    home = to_partners(flash_product(inverse, coupling))
    halos = exchange(edges(cotangent, well_mask, permeability))
    before = diag_part(cotangent, well_mask, diag_block)
    first, rounded = flux_part(before, cotangent, well_mask, permeability, halos, flux_block, True)
    picked, sent = gather(rounded, cells, helper_of, block_count, comps, rows, cols, width)
    second, *sides = scatter(first, picked, home, helper_of, cells, well_mask, permeability)
    halos = exchange(sides)
    before = diag_part(second, well_mask, diag_block)
    (adjoint,) = flux_part(before, second, well_mask, permeability, halos, flux_block, False)

    partial_sum = grad_part(inverse, state, to_partners(sent))
    devices = lax.axis_size("gx") * lax.axis_size("gy")
    grad_scale = 1.0 / math.sqrt(width * devices * devices)
    gathered = lax.all_gather(partial_sum, AXES)
    interaction_grad = -grad_scale * jnp.sum(gathered, axis=0)[:, :comps]
    return (adjoint, interaction_grad)


def solution(mesh):
    return jax.shard_map(
        shards,
        mesh=mesh,
        in_specs=(
            P(None, None, "gy", "gx"),
            P(None, "gy", "gx"),
            P("gy", "gx"),
            P(None, None, None, "gy", "gx"),
            P(None, None, None, "gy", "gx"),
            P("gy", "gx", None),
            P("gy", "gx"),
            P("gy", "gx", None),
            P("gy", "gx", None, None, None, None),
            P("gy", "gx", None, None, None, None),
            P("gy", "gx", None, None, None),
        ),
        out_specs=(P(None, None, "gy", "gx"), P()),
        check_vma=False,
    )
```

```python
import functools
import math

import jax
import jax.numpy as jnp
from jax import lax
from jax.experimental import pallas as pl
from jax.experimental.pallas import tpu as pltpu
from jax.sharding import PartitionSpec as P

F32 = jnp.float32
BF16 = jnp.bfloat16
AXES = ("gx", "gy")
MIB = 1024 * 1024
CHUNK = 512


def params(mib):
    return pltpu.CompilerParams(vmem_limit_bytes=mib * MIB)


def cost(flops, moved):
    return pl.CostEstimate(flops=int(flops), bytes_accessed=int(moved), transcendentals=0)


def product_kernel(inverse_ref, coupling_ref, out_ref):
    blocks, comps = inverse_ref.shape[:2]

    def one(b, carry):
        inverse = inverse_ref[b].astype(F32)
        coupling = coupling_ref[b].astype(F32)
        for r in range(comps):
            row = inverse[r, 0:1] * coupling[0]
            for m in range(1, comps):
                row += inverse[r, m : m + 1] * coupling[m]
            out_ref[b, r] = row.astype(BF16)
        return carry

    lax.fori_loop(0, blocks, one, 0)


def flash_product(inverse, coupling):
    return pl.pallas_call(
        product_kernel,
        out_shape=jax.ShapeDtypeStruct(inverse.shape, BF16),
        compiler_params=params(24),
        cost_estimate=cost(16 * inverse.size, 6 * inverse.size),
    )(inverse, coupling)


def round_up(number, step):
    return -(-number // step) * step


def write_edges(field, comps, clear, perm_ref, side_y, send_y, send_x):
    layers, rows, cols = perm_ref.shape
    lane = lax.broadcasted_iota(jnp.int32, (rows, cols), 1)
    pair = lane // 2
    along_x = jnp.zeros((rows, cols), F32)
    side_y[...] = jnp.zeros_like(side_y)
    for k in range(layers):
        for c in range(comps + 1):
            if c < comps:
                value, at = field(k, c) * clear, k * comps + c
            else:
                value, at = perm_ref[k], layers * comps + k
            side_y[0, at : at + 1, :] = value[0:1]
            side_y[1, at : at + 1, :] = value[rows - 1 : rows]
            along_x = jnp.where(pair == at, pltpu.roll(value, (2 * at + 1) % cols, 1), along_x)
    count_y, count_x = send_y.shape[0], send_x.shape[0]
    me_y = lax.axis_index("gy")
    along_x = along_x.astype(BF16)
    for i in range(count_x):
        send_x[i] = along_x
    low, high = side_y[0].astype(BF16), side_y[1].astype(BF16)
    for i in range(count_y):
        send_y[i] = jnp.where(i < me_y, low, high)


def edges_kernel(field_ref, mask_ref, perm_ref, send_y, send_x, side_y):
    clear = 1.0 - mask_ref[...].astype(F32)
    write_edges(lambda k, c: field_ref[k, c], field_ref.shape[1], clear, perm_ref, side_y, send_y, send_x)


def edge_rows(layers, comps):
    return round_up(layers * (comps + 1), 16)


def edge_shapes(layers, comps, rows, cols):
    along_y = (lax.axis_size("gy"), edge_rows(layers, comps), cols)
    along_x = (lax.axis_size("gx"), rows, cols)
    return [jax.ShapeDtypeStruct(shape, BF16) for shape in (along_y, along_x)]


def edge_scratch(layers, comps, cols):
    return pltpu.VMEM((2, edge_rows(layers, comps), cols), F32)


def edges(field, mask, perm):
    layers, comps, rows, cols = field.shape
    return pl.pallas_call(
        edges_kernel,
        out_shape=edge_shapes(*field.shape),
        scratch_shapes=[edge_scratch(layers, comps, cols)],
        compiler_params=params(24),
        cost_estimate=cost(4 * field.size, 4 * field.size),
    )(field, mask, perm)


def exchange(sides):
    send_y, send_x = sides

    def swap(array, axis):
        return lax.all_to_all(array, axis, split_axis=0, concat_axis=0, tiled=True)

    return swap(send_y, "gy"), swap(send_x, "gx")


TILE = 16


def diag_kernel(field_ref, mask_ref, block_ref, out_ref):
    comps, rows = field_ref.shape[1:3]
    for y in range(0, rows, TILE):
        here = slice(y, y + TILE)
        well = mask_ref[here].astype(F32)
        values = [field_ref[0, c, here] for c in range(comps)]
        total = [well * value for value in values]
        for r in range(comps):
            source = values[r] * (1.0 - well)
            for c in range(comps):
                total[c] += block_ref[0, r, c, here].astype(F32) * source
        for c in range(comps):
            out_ref[0, c, here] = total[c]


def diag_part(field, mask, block, mib):
    layers, comps, rows, cols = field.shape
    layer = pl.BlockSpec((1, comps, rows, cols), lambda k: (k, 0, 0, 0))
    return pl.pallas_call(
        diag_kernel,
        grid=(layers,),
        in_specs=[
            layer,
            pl.BlockSpec((rows, cols), lambda k: (0, 0)),
            pl.BlockSpec((1, comps, comps, rows, cols), lambda k: (k, 0, 0, 0, 0)),
        ],
        out_specs=layer,
        out_shape=jax.ShapeDtypeStruct(field.shape, F32),
        compiler_params=params(mib),
        cost_estimate=cost(2 * block.size, 2 * block.size + 8 * field.size),
    )(field, mask, block)


def reciprocal(value):
    guess = pl.reciprocal(value, approx=True)
    return guess * (2.0 - value * guess)


def flux_kernel(want_rounded, before_ref, field_ref, mask_ref, perm_ref, from_y, from_x, block_ref, *rest):
    out_ref = rest[0]
    rounded_ref = rest[1] if want_rounded else None
    padded, padded_perm, edge_x, place, beside_edge, perm_edge = rest[-6:]
    layers, comps, rows, cols = field_ref.shape
    top = 8
    k = pl.program_id(0)
    above = jnp.minimum(k + 1, layers - 1)
    below = jnp.maximum(k - 1, 0)
    me_x, me_y = lax.axis_index("gx"), lax.axis_index("gy")
    count_x, count_y = from_x.shape[0], from_y.shape[0]
    lane = lax.broadcasted_iota(jnp.int32, (rows, cols), 1)

    @pl.when(k == 0)
    def _():
        low = from_x[jnp.maximum(me_x - 1, 0)].astype(F32)
        high = from_x[jnp.minimum(me_x + 1, count_x - 1)].astype(F32)
        low = jnp.where(me_x > 0, low, 0.0)
        high = jnp.where(me_x < count_x - 1, high, 0.0)
        edge_x[...] = jnp.where(lane % 2 == 0, low, high)
        number = lax.broadcasted_iota(jnp.int32, (cols, cols), 0)
        spot = lax.broadcasted_iota(jnp.int32, (cols, cols), 1)
        for r in range(comps):
            taken = ((number == 2 * r) & (spot == 0)) | ((number == 2 * r + 1) & (spot == cols - 1))
            place[:, r * cols : (r + 1) * cols] = jnp.where(taken, 1.0, 0.0).astype(BF16)

    turned = pltpu.roll(edge_x[...], lax.rem(cols - 2 * comps * k, cols), 1).astype(BF16)
    beside_edge[...] = jnp.dot(turned, place[...], preferred_element_type=F32)
    at_low = 2 * (layers * comps + k)
    perm_low = pltpu.roll(edge_x[...], lax.rem(cols - at_low, cols), 1)
    perm_high = pltpu.roll(edge_x[...], lax.rem(2 * cols - at_low - 2, cols), 1)
    perm_edge[...] = jnp.where(lane == 0, perm_low, perm_high)

    clear = 1.0 - mask_ref[...].astype(F32)
    low_y = from_y[jnp.maximum(me_y - 1, 0), pl.ds(pl.multiple_of(16 * (k // 2), 16), 16)].astype(F32)
    high_y = from_y[jnp.minimum(me_y + 1, count_y - 1), pl.ds(pl.multiple_of(16 * (k // 2), 16), 16)].astype(F32)
    has_low, has_high = me_y > 0, me_y < count_y - 1
    odd = k % 2 == 1
    low_y = jnp.where(has_low, jnp.where(odd, low_y[comps:], low_y[:comps]), 0.0)
    high_y = jnp.where(has_high, jnp.where(odd, high_y[comps:], high_y[:comps]), 0.0)
    perm_rows = slice(layers * comps, layers * comps + 16)
    perm_y_low = from_y[jnp.maximum(me_y - 1, 0), perm_rows].astype(F32)
    perm_y_high = from_y[jnp.minimum(me_y + 1, count_y - 1), perm_rows].astype(F32)
    mine = lax.broadcasted_iota(jnp.int32, (16, cols), 0) == k
    perm_y_low = jnp.sum(jnp.where(mine & has_low, perm_y_low, 0.0), axis=0, keepdims=True)
    perm_y_high = jnp.sum(jnp.where(mine & has_high, perm_y_high, 0.0), axis=0, keepdims=True)
    for c in range(comps):
        padded[c, top : top + rows] = field_ref[k, c] * clear
        padded[c, top - 1 : top] = low_y[c : c + 1]
        padded[c, top + rows : top + rows + 1] = high_y[c : c + 1]
    padded_perm[top : top + rows] = perm_ref[k]
    padded_perm[top - 1 : top] = perm_y_low
    padded_perm[top + rows : top + rows + 1] = perm_y_high
    lane = lax.broadcasted_iota(jnp.int32, (TILE, cols), 1)
    is_first, is_last = lane == 0, lane == cols - 1
    inner = jnp.where(is_first | is_last, 0.0, 1.0)

    def weight(centre, beside):
        return 2.0 * centre * beside * reciprocal(centre + beside)

    for y in range(0, rows, TILE):
        here = slice(y, y + TILE)
        at = top + y
        free = 1.0 - mask_ref[here].astype(F32)
        centre = perm_ref[k, here]
        perm_beside = perm_edge[here]
        perm_left = jnp.where(is_first, perm_beside, pltpu.roll(centre, 1, 1))
        perm_right = jnp.where(is_last, perm_beside, pltpu.roll(centre, cols - 1, 1))
        to_left, to_right = weight(centre, perm_left), weight(centre, perm_right)
        weights = [
            jnp.where(k < layers - 1, weight(centre, perm_ref[above, here]), 0.0) * free,
            jnp.where(k > 0, weight(centre, perm_ref[below, here]), 0.0) * free,
            weight(centre, padded_perm[at + 1 : at + 1 + TILE]),
            weight(centre, padded_perm[at - 1 : at - 1 + TILE]),
            jnp.where(is_last, 0.0, to_right),
            jnp.where(is_first, 0.0, to_left),
            jnp.where(is_first, to_left, to_right) * (1.0 - inner),
        ]
        total = [None] * comps
        for r in range(comps):
            own = padded[r, at : at + TILE]
            summed = (
                weights[0] * field_ref[above, r, here]
                + weights[1] * field_ref[below, r, here]
                + weights[2] * padded[r, at + 1 : at + 1 + TILE]
                + weights[3] * padded[r, at - 1 : at - 1 + TILE]
                + weights[4] * pltpu.roll(own, cols - 1, 1)
                + weights[5] * pltpu.roll(own, 1, 1)
                + weights[6] * beside_edge[here, r * cols : (r + 1) * cols]
            )
            for c in range(comps):
                term = block_ref[0, r, c, here].astype(F32) * summed
                total[c] = term if r == 0 else total[c] + term
        for c in range(comps):
            value = before_ref[0, c, here] - total[c]
            out_ref[0, c, here] = value
            if want_rounded:
                rounded_ref[c * rows + y : c * rows + y + TILE, :] = value.astype(BF16)


def flux_part(before, field, mask, perm, halos, block, want_rounded, mib):
    layers, comps, rows, cols = field.shape
    layer = pl.BlockSpec((1, comps, rows, cols), lambda k: (k, 0, 0, 0))

    def whole(array):
        return pl.BlockSpec(array.shape, lambda k: (0,) * array.ndim)

    out_specs = [layer]
    out_shape = [jax.ShapeDtypeStruct(field.shape, F32)]
    if want_rounded:
        out_specs.append(pl.BlockSpec((comps * rows, cols), lambda k: (0, k)))
        out_shape.append(jax.ShapeDtypeStruct((comps * rows, layers * cols), BF16))
    return pl.pallas_call(
        functools.partial(flux_kernel, want_rounded),
        grid=(layers,),
        in_specs=[
            layer,
            whole(field),
            whole(mask),
            whole(perm),
            *(whole(halo) for halo in halos),
            pl.BlockSpec((1, comps, comps, rows, cols), lambda k: (k, 0, 0, 0, 0)),
        ],
        out_specs=out_specs,
        out_shape=out_shape,
        scratch_shapes=[
            pltpu.VMEM((comps, rows + 16, cols), F32),
            pltpu.VMEM((rows + 16, cols), F32),
            pltpu.VMEM((rows, cols), F32),
            pltpu.VMEM((cols, comps * cols), BF16),
            pltpu.VMEM((rows, comps * cols), F32),
            pltpu.VMEM((rows, cols), F32),
        ],
        compiler_params=params(mib),
        cost_estimate=cost(4 * block.size, 2 * block.size + 12 * field.size),
    )(before, field, mask, perm, *halos, block)


def split_cells(cells, rows, cols):
    layer = cells // (rows * cols)
    y = (cells // cols) % rows
    return layer * cols + cells % cols, y


def one_hot(column, count, slots):
    number = lax.broadcasted_iota(jnp.int32, (count, slots), 0)
    return jnp.where(number == column, 1.0, 0.0).astype(BF16)


def gather_kernel(rows, cols, helper_ref, count_ref, cells_ref, rounded_ref, picked_ref, sent_ref):
    chunks, _, slots = cells_ref.shape
    width = picked_ref.shape[-1]
    comps = picked_ref.shape[1]
    per_chunk = slots // width
    row_number = lax.broadcasted_iota(jnp.int32, (rows, slots), 0)

    def one(i, carry):
        column, y = split_cells(cells_ref[i], rows, cols)
        chosen = one_hot(column, rounded_ref.shape[1], slots)
        found = jnp.dot(rounded_ref[...], chosen, preferred_element_type=F32)
        at_row = row_number == y
        values = [
            jnp.sum(jnp.where(at_row, found[c * rows : (c + 1) * rows], 0.0), axis=0, keepdims=True)
            for c in range(comps)
        ]
        values = jnp.concatenate(values, axis=0)
        for j in range(per_chunk):
            b = i * per_chunk + j
            live = jnp.where(b < count_ref[0, 0], 1.0, 0.0)
            value = (values[:, j * width : (j + 1) * width] * live).astype(BF16)
            picked_ref[b] = value
            sent_ref[helper_ref[0, 0, b]] = value
        return carry

    lax.fori_loop(0, chunks, one, 0)


def gather(rounded, cells, helper, count, comps, rows, cols, width):
    blocks = helper.shape[-1]
    shape = jax.ShapeDtypeStruct((blocks, comps, width), BF16)
    smem = pl.BlockSpec(memory_space=pltpu.SMEM)
    vmem = pl.BlockSpec(memory_space=pltpu.VMEM)
    return pl.pallas_call(
        functools.partial(gather_kernel, rows, cols),
        in_specs=[smem, smem, vmem, vmem],
        out_specs=[vmem, vmem],
        out_shape=[shape, shape],
        compiler_params=params(32),
        cost_estimate=cost(2 * rounded.size * cells.size, 2 * rounded.size),
    )(helper, count, cells, rounded)


def scatter_kernel(
    helper_ref, cells_ref, picked_ref, home_ref, first_ref, mask_ref, perm_ref, second_ref, send_y, send_x, added, side_y
):
    layers, comps, rows, cols = first_ref.shape
    chunks, _, slots = cells_ref.shape
    width = picked_ref.shape[-1]
    per_chunk = slots // width
    row_number = lax.broadcasted_iota(jnp.int32, (rows, slots), 0)
    added[...] = jnp.zeros_like(added)

    def one(i, carry):
        column, y = split_cells(cells_ref[i], rows, cols)
        chosen = one_hot(column, added.shape[1], slots)
        parts = []
        for j in range(per_chunk):
            b = i * per_chunk + j
            home = home_ref[helper_ref[0, 0, b]].astype(F32)
            value = picked_ref[b].astype(F32)
            part = home[0] * value[0:1]
            for r in range(1, comps):
                part += home[r] * value[r : r + 1]
            parts.append((-part).astype(BF16).astype(F32))
        correction = jnp.concatenate(parts, axis=1)
        at_row = row_number == y
        spread = jnp.concatenate(
            [jnp.where(at_row, correction[c : c + 1], 0.0).astype(BF16) for c in range(comps)], axis=0
        )
        added[...] += lax.dot_general(spread, chosen, (((1,), (1,)), ((), ())), preferred_element_type=F32)
        return carry

    lax.fori_loop(0, chunks, one, 0)
    for k in range(layers):
        for c in range(comps):
            second_ref[k, c] = first_ref[k, c] + added[c * rows : (c + 1) * rows, k * cols : (k + 1) * cols]
    clear = 1.0 - mask_ref[...].astype(F32)
    write_edges(lambda k, c: second_ref[k, c], comps, clear, perm_ref, side_y, send_y, send_x)


def scatter(first, picked, home, helper, cells, mask, perm):
    layers, comps, rows, cols = first.shape
    smem = pl.BlockSpec(memory_space=pltpu.SMEM)
    vmem = pl.BlockSpec(memory_space=pltpu.VMEM)
    return pl.pallas_call(
        scatter_kernel,
        in_specs=[smem] + [vmem] * 6,
        out_specs=[vmem] * 3,
        out_shape=[jax.ShapeDtypeStruct(first.shape, F32), *edge_shapes(*first.shape)],
        scratch_shapes=[pltpu.VMEM((comps * rows, layers * cols), F32), edge_scratch(layers, comps, cols)],
        compiler_params=params(40),
        cost_estimate=cost(2 * first.size * cells.size, 8 * first.size),
    )(helper, cells, picked, home, first, mask, perm)


def grad_kernel(inverse_ref, state_ref, picked_ref, out_ref):
    blocks, comps = inverse_ref.shape[:2]
    width = inverse_ref.shape[-1]

    def one(b, totals):
        inverse = inverse_ref[b].astype(F32)
        value = picked_ref[b].astype(F32)
        state = state_ref[b].astype(F32)
        part = inverse[0] * value[0:1]
        for r in range(1, comps):
            part += inverse[r] * value[r : r + 1]
        part *= state
        return tuple(totals[j] + part * state[j : j + 1] for j in range(comps))

    totals = lax.fori_loop(0, blocks, one, (jnp.zeros((comps, width), F32),) * comps)
    lane = lax.broadcasted_iota(jnp.int32, (comps, width), 1)
    result = jnp.zeros((comps, width), F32)
    for j in range(comps):
        result = jnp.where(lane == j, jnp.sum(totals[j], axis=1, keepdims=True), result)
    out_ref[...] = result


def grad_part(inverse, state, picked):
    return pl.pallas_call(
        grad_kernel,
        out_shape=jax.ShapeDtypeStruct((inverse.shape[1], inverse.shape[-1]), F32),
        compiler_params=params(24),
        cost_estimate=cost(4 * inverse.size, 2 * inverse.size),
    )(inverse, state, picked)


def shards(
    cotangent,
    permeability,
    well_mask,
    diag_block,
    flux_block,
    cell_list,
    block_count,
    helper_of,
    flash_inverse,
    flash_coupling,
    phase_state,
):
    layers, comps, rows, cols = cotangent.shape
    blocks, width = helper_of.shape[-1], flash_inverse.shape[-1]
    inverse = flash_inverse.reshape(blocks, comps, comps, width)
    coupling = flash_coupling.reshape(blocks, comps, comps, width)
    state = phase_state.reshape(blocks, comps, width)
    cells = cell_list.reshape(-1, 1, min(CHUNK, cell_list.shape[-1]))

    def to_partners(array):
        return lax.all_to_all(array, AXES, split_axis=0, concat_axis=0, tiled=True)

    home = to_partners(flash_product(inverse, coupling))
    halos = exchange(edges(cotangent, well_mask, permeability))
    before = diag_part(cotangent, well_mask, diag_block, 56)
    first, rounded = flux_part(before, cotangent, well_mask, permeability, halos, flux_block, True, 56)
    picked, sent = gather(rounded, cells, helper_of, block_count, comps, rows, cols, width)
    second, *sides = scatter(first, picked, home, helper_of, cells, well_mask, permeability)
    halos = exchange(sides)
    before = diag_part(second, well_mask, diag_block, 24)
    (adjoint,) = flux_part(before, second, well_mask, permeability, halos, flux_block, False, 24)

    partial_sum = grad_part(inverse, state, to_partners(sent))
    devices = lax.axis_size("gx") * lax.axis_size("gy")
    grad_scale = 1.0 / math.sqrt(width * devices * devices)
    for axis in ("gy", "gx"):
        copies = jnp.broadcast_to(partial_sum[None], (lax.axis_size(axis), *partial_sum.shape))
        partial_sum = jnp.sum(lax.all_to_all(copies, axis, split_axis=0, concat_axis=0), axis=0)
    interaction_grad = -grad_scale * partial_sum[:, :comps]
    return (adjoint, interaction_grad)


def solution(mesh):
    return jax.shard_map(
        shards,
        mesh=mesh,
        in_specs=(
            P(None, None, "gy", "gx"),
            P(None, "gy", "gx"),
            P("gy", "gx"),
            P(None, None, None, "gy", "gx"),
            P(None, None, None, "gy", "gx"),
            P("gy", "gx", None),
            P("gy", "gx"),
            P("gy", "gx", None),
            P("gy", "gx", None, None, None, None),
            P("gy", "gx", None, None, None, None),
            P("gy", "gx", None, None, None),
        ),
        out_specs=(P(None, None, "gy", "gx"), P()),
        check_vma=False,
    )
```

```python
import functools
import math

import jax
import jax.numpy as jnp
from jax import lax
from jax.experimental import pallas as pl
from jax.experimental.pallas import tpu as pltpu
from jax.sharding import PartitionSpec as P

F32 = jnp.float32
BF16 = jnp.bfloat16
AXES = ("gx", "gy")
MIB = 1024 * 1024
CHUNK = 512


def params(mib):
    return pltpu.CompilerParams(vmem_limit_bytes=mib * MIB)


def cost(flops, moved):
    return pl.CostEstimate(flops=int(flops), bytes_accessed=int(moved), transcendentals=0)


def round_up(number, step):
    return -(-number // step) * step


def write_edges(field, comps, clear, perm_ref, side_y, sends):
    send_y_0, send_y_1, send_x = sends
    layers, rows, cols = perm_ref.shape
    lane = lax.broadcasted_iota(jnp.int32, (rows, cols), 1)
    pair = lane // 2
    along_x = jnp.zeros((rows, cols), F32)
    side_y[...] = jnp.zeros_like(side_y)
    for k in range(layers):
        for c in range(comps + 1):
            if c < comps:
                value, at = field(k, c) * clear, k * comps + c
            else:
                value, at = perm_ref[k], layers * comps + k
            side_y[0, at : at + 1, :] = value[0:1]
            side_y[1, at : at + 1, :] = value[rows - 1 : rows]
            along_x = jnp.where(pair == at, pltpu.roll(value, (2 * at + 1) % cols, 1), along_x)
    even = lax.axis_index("gy") % 2 == 0
    send_x[...] = along_x.astype(BF16)
    low, high = side_y[0].astype(BF16), side_y[1].astype(BF16)
    send_y_0[...] = jnp.where(even, high, low)
    send_y_1[...] = jnp.where(even, low, high)


def fetch(copies):
    for copy in copies:
        copy.start()
    for copy in copies:
        copy.wait()


def opening_kernel(
    inverse_hbm, coupling_hbm, field_hbm, mask_hbm, perm_hbm,
    product_ref, send_y_0, send_y_1, send_x,
    inverse_ref, coupling_ref, field_ref, mask_ref, perm_ref, side_y, sems,
):
    sources = (inverse_hbm, coupling_hbm, field_hbm, mask_hbm, perm_hbm)
    targets = (inverse_ref, coupling_ref, field_ref, mask_ref, perm_ref)
    copies = [pltpu.make_async_copy(a, b, sems.at[i]) for i, (a, b) in enumerate(zip(sources, targets))]
    for copy in copies:
        copy.start()
    blocks, comps = inverse_ref.shape[:2]
    copies[0].wait()
    copies[1].wait()

    def one(b, carry):
        inverse = inverse_ref[b].astype(F32)
        coupling = coupling_ref[b].astype(F32)
        for r in range(comps):
            row = inverse[r, 0:1] * coupling[0]
            for m in range(1, comps):
                row += inverse[r, m : m + 1] * coupling[m]
            product_ref[b, r] = row.astype(BF16)
        return carry

    lax.fori_loop(0, blocks, one, 0)
    for copy in copies[2:]:
        copy.wait()
    clear = 1.0 - mask_ref[...].astype(F32)
    sends = (send_y_0, send_y_1, send_x)
    write_edges(lambda k, c: field_ref[k, c], comps, clear, perm_ref, side_y, sends)


def edge_rows(layers, comps):
    return round_up(layers * (comps + 1), 16)


def edge_shapes(layers, comps, rows, cols):
    along_y = (edge_rows(layers, comps), cols)
    return [jax.ShapeDtypeStruct(shape, BF16) for shape in (along_y, along_y, (rows, cols))]


def edge_scratch(layers, comps, cols):
    return pltpu.VMEM((2, edge_rows(layers, comps), cols), F32)


def opening(inverse, coupling, field, mask, perm):
    layers, comps, rows, cols = field.shape
    hbm = pl.BlockSpec(memory_space=pltpu.HBM)
    vmem = pl.BlockSpec(memory_space=pltpu.VMEM)
    arrays = (inverse, coupling, field, mask, perm)
    return pl.pallas_call(
        opening_kernel,
        in_specs=[hbm] * 5,
        out_specs=[vmem] * 4,
        out_shape=[jax.ShapeDtypeStruct(inverse.shape, BF16), *edge_shapes(*field.shape)],
        scratch_shapes=[
            *(pltpu.VMEM(array.shape, array.dtype) for array in arrays),
            edge_scratch(layers, comps, cols),
            pltpu.SemaphoreType.DMA((5,)),
        ],
        compiler_params=params(56),
        cost_estimate=cost(16 * inverse.size + 4 * field.size, 6 * inverse.size + 4 * field.size),
    )(*arrays)


def exchange(send_y_0, send_y_1, send_x):
    def swaps(axis, first, second):
        count = lax.axis_size(axis)
        results = []
        for start, array in ((0, first), (1, second)):
            pairs = [(i, i + 1) for i in range(start, count - 1, 2)]
            results.append(lax.ppermute(array, axis, pairs + [(j, i) for i, j in pairs]))
        return results

    return (*swaps("gy", send_y_0, send_y_1), *swaps("gx", send_x, send_x))


TILE = 16
AHEAD = 3


def reciprocal(value):
    guess = pl.reciprocal(value, approx=True)
    return guess * (2.0 - value * guess)


def weight(centre, beside):
    return 2.0 * centre * beside * reciprocal(centre + beside)


def apply_kernel(want_rounded, field_hbm, mask_hbm, perm_hbm, y_0, y_1, x_0, x_1, diag_hbm, flux_hbm, *rest):
    if want_rounded:
        out_hbm, rounded_hbm, *rest, rounded_ref, rounded_sems = rest
    else:
        out_hbm, *rest = rest
    *rest, out_ref, out_sems = rest
    (field_ref, mask_ref, perm_ref, diag_ref, flux_ref, padded, padded_perm, edge_x, place, beside_edge, perm_edge, sems) = rest
    layers, comps, rows, cols = field_ref.shape
    top = 8

    def blocks(k):
        return (
            pltpu.make_async_copy(diag_hbm.at[k], diag_ref.at[k], sems.at[3 + k]),
            pltpu.make_async_copy(flux_hbm.at[k], flux_ref.at[k], sems.at[3 + layers + k]),
        )

    def out_copies(k):
        copies = [pltpu.make_async_copy(out_ref.at[k], out_hbm.at[k], out_sems.at[k])]
        if want_rounded:
            columns = pl.ds(pl.multiple_of(k * cols, cols), cols)
            source, target = rounded_ref.at[:, columns], rounded_hbm.at[:, columns]
            copies.append(pltpu.make_async_copy(source, target, rounded_sems.at[k]))
        return copies

    smalls = [
        pltpu.make_async_copy(field_hbm, field_ref, sems.at[0]),
        pltpu.make_async_copy(mask_hbm, mask_ref, sems.at[1]),
        pltpu.make_async_copy(perm_hbm, perm_ref, sems.at[2]),
    ]
    for copy in smalls:
        copy.start()
    for k in range(min(AHEAD, layers)):
        for copy in blocks(k):
            copy.start()

    lane = lax.broadcasted_iota(jnp.int32, (rows, cols), 1)
    number = lax.broadcasted_iota(jnp.int32, (cols, cols), 0)
    spot = lax.broadcasted_iota(jnp.int32, (cols, cols), 1)
    for r in range(comps):
        taken = ((number == 2 * r) & (spot == 0)) | ((number == 2 * r + 1) & (spot == cols - 1))
        place[:, r * cols : (r + 1) * cols] = jnp.where(taken, 1.0, 0.0).astype(BF16)
    even_x = lax.axis_index("gx") % 2 == 0
    even_y = lax.axis_index("gy") % 2 == 0
    side_0, side_1 = x_0[...].astype(F32), x_1[...].astype(F32)
    edge_x[...] = jnp.where((lane % 2 == 0) == even_x, side_1, side_0)
    for copy in smalls:
        copy.wait()
    clear = 1.0 - mask_ref[...].astype(F32)

    def layer(k, carry):
        above = jnp.minimum(k + 1, layers - 1)
        below = jnp.maximum(k - 1, 0)

        @pl.when(k + AHEAD < layers)
        def _():
            for copy in blocks(k + AHEAD):
                copy.start()

        turned = pltpu.roll(edge_x[...], lax.rem(cols - 2 * comps * k, cols), 1).astype(BF16)
        beside_edge[...] = jnp.dot(turned, place[...], preferred_element_type=F32)
        at_low = 2 * (layers * comps + k)
        perm_low = pltpu.roll(edge_x[...], lax.rem(cols - at_low, cols), 1)
        perm_high = pltpu.roll(edge_x[...], lax.rem(2 * cols - at_low - 2, cols), 1)
        perm_edge[...] = jnp.where(lane == 0, perm_low, perm_high)

        odd = k % 2 == 1
        here = pl.ds(pl.multiple_of(16 * (k // 2), 16), 16)
        side_0, side_1 = y_0[here].astype(F32), y_1[here].astype(F32)
        side_0 = jnp.where(odd, side_0[comps:], side_0[:comps])
        side_1 = jnp.where(odd, side_1[comps:], side_1[:comps])
        low_y, high_y = jnp.where(even_y, side_1, side_0), jnp.where(even_y, side_0, side_1)
        here = slice(layers * comps, layers * comps + 16)
        mine = lax.broadcasted_iota(jnp.int32, (16, cols), 0) == k
        perm_0 = jnp.sum(jnp.where(mine, y_0[here].astype(F32), 0.0), axis=0, keepdims=True)
        perm_1 = jnp.sum(jnp.where(mine, y_1[here].astype(F32), 0.0), axis=0, keepdims=True)
        for c in range(comps):
            padded[c, top : top + rows] = field_ref[k, c] * clear
            padded[c, top - 1 : top] = low_y[c : c + 1]
            padded[c, top + rows : top + rows + 1] = high_y[c : c + 1]
        padded_perm[top : top + rows] = perm_ref[k]
        padded_perm[top - 1 : top] = jnp.where(even_y, perm_1, perm_0)
        padded_perm[top + rows : top + rows + 1] = jnp.where(even_y, perm_0, perm_1)
        for copy in blocks(k):
            copy.wait()

        narrow = lax.broadcasted_iota(jnp.int32, (TILE, cols), 1)
        is_first, is_last = narrow == 0, narrow == cols - 1
        for y in range(0, rows, TILE):
            here = slice(y, y + TILE)
            at = top + y
            well = mask_ref[here].astype(F32)
            free = 1.0 - well
            centre = perm_ref[k, here]
            perm_beside = perm_edge[here]
            perm_left = jnp.where(is_first, perm_beside, pltpu.roll(centre, 1, 1))
            perm_right = jnp.where(is_last, perm_beside, pltpu.roll(centre, cols - 1, 1))
            to_left, to_right = weight(centre, perm_left), weight(centre, perm_right)
            weights = [
                jnp.where(k < layers - 1, weight(centre, perm_ref[above, here]), 0.0) * free,
                jnp.where(k > 0, weight(centre, perm_ref[below, here]), 0.0) * free,
                weight(centre, padded_perm[at + 1 : at + 1 + TILE]),
                weight(centre, padded_perm[at - 1 : at - 1 + TILE]),
                jnp.where(is_last, 0.0, to_right),
                jnp.where(is_first, 0.0, to_left),
                jnp.where(is_first, to_left, jnp.where(is_last, to_right, 0.0)),
            ]
            total = [None] * comps
            for r in range(comps):
                own = padded[r, at : at + TILE]
                summed = (
                    weights[0] * field_ref[above, r, here]
                    + weights[1] * field_ref[below, r, here]
                    + weights[2] * padded[r, at + 1 : at + 1 + TILE]
                    + weights[3] * padded[r, at - 1 : at - 1 + TILE]
                    + weights[4] * pltpu.roll(own, cols - 1, 1)
                    + weights[5] * pltpu.roll(own, 1, 1)
                    + weights[6] * beside_edge[here, r * cols : (r + 1) * cols]
                )
                for c in range(comps):
                    term = diag_ref[k, r, c, here].astype(F32) * own - flux_ref[k, r, c, here].astype(F32) * summed
                    total[c] = term if r == 0 else total[c] + term
            for c in range(comps):
                value = total[c] + well * field_ref[k, c, here]
                out_ref[k, c, here] = value
                if want_rounded:
                    columns = pl.ds(pl.multiple_of(k * cols, cols), cols)
                    rounded_ref[c * rows + y : c * rows + y + TILE, columns] = value.astype(BF16)
        for copy in out_copies(k):
            copy.start()
        return carry

    lax.fori_loop(0, layers, layer, 0)
    for k in range(layers):
        for copy in out_copies(k):
            copy.wait()


def apply_transposed(field, mask, perm, halos, diag, flux, want_rounded, mib):
    layers, comps, rows, cols = field.shape
    hbm = pl.BlockSpec(memory_space=pltpu.HBM)
    vmem = pl.BlockSpec(memory_space=pltpu.VMEM)
    out_shape = [jax.ShapeDtypeStruct(field.shape, F32)]
    extra = []
    if want_rounded:
        out_shape.append(jax.ShapeDtypeStruct((comps * rows, layers * cols), BF16))
        extra = [pltpu.VMEM(out_shape[1].shape, BF16), pltpu.SemaphoreType.DMA((layers,))]
    return pl.pallas_call(
        functools.partial(apply_kernel, want_rounded),
        in_specs=[pl.BlockSpec(memory_space=pl.ANY), hbm, hbm, *[vmem] * 4, hbm, hbm],
        out_specs=[hbm] * len(out_shape),
        out_shape=out_shape,
        scratch_shapes=[
            pltpu.VMEM(field.shape, F32),
            pltpu.VMEM(mask.shape, mask.dtype),
            pltpu.VMEM(perm.shape, F32),
            pltpu.VMEM(diag.shape, BF16),
            pltpu.VMEM(flux.shape, BF16),
            pltpu.VMEM((comps, rows + 16, cols), F32),
            pltpu.VMEM((rows + 16, cols), F32),
            pltpu.VMEM((rows, cols), F32),
            pltpu.VMEM((cols, comps * cols), BF16),
            pltpu.VMEM((rows, comps * cols), F32),
            pltpu.VMEM((rows, cols), F32),
            pltpu.SemaphoreType.DMA((3 + 2 * layers,)),
            pltpu.VMEM(field.shape, F32),
            pltpu.SemaphoreType.DMA((layers,)),
            *extra,
        ],
        compiler_params=params(mib),
        cost_estimate=cost(8 * diag.size, 4 * diag.size + 8 * field.size),
    )(field, mask, perm, *halos, diag, flux)


def split_cells(cells, rows, cols):
    layer = cells // (rows * cols)
    y = (cells // cols) % rows
    return layer * cols + cells % cols, y


def one_hot(column, count, slots):
    number = lax.broadcasted_iota(jnp.int32, (count, slots), 0)
    return jnp.where(number == column, 1.0, 0.0).astype(BF16)


def gather_kernel(rows, cols, helper_ref, count_ref, cells_ref, rounded_ref, picked_ref, sent_ref):
    chunks, _, slots = cells_ref.shape
    width = picked_ref.shape[-1]
    comps = picked_ref.shape[1]
    per_chunk = slots // width
    row_number = lax.broadcasted_iota(jnp.int32, (rows, slots), 0)

    def one(i, carry):
        column, y = split_cells(cells_ref[i], rows, cols)
        chosen = one_hot(column, rounded_ref.shape[1], slots)
        found = jnp.dot(rounded_ref[...], chosen, preferred_element_type=F32)
        at_row = row_number == y
        values = [
            jnp.sum(jnp.where(at_row, found[c * rows : (c + 1) * rows], 0.0), axis=0, keepdims=True)
            for c in range(comps)
        ]
        values = jnp.concatenate(values, axis=0)
        for j in range(per_chunk):
            b = i * per_chunk + j
            live = jnp.where(b < count_ref[0, 0], 1.0, 0.0)
            value = (values[:, j * width : (j + 1) * width] * live).astype(BF16)
            picked_ref[b] = value
            sent_ref[helper_ref[0, 0, b]] = value
        return carry

    lax.fori_loop(0, chunks, one, 0)


def gather(rounded, cells, helper, count, comps, rows, cols, width):
    blocks = helper.shape[-1]
    shape = jax.ShapeDtypeStruct((blocks, comps, width), BF16)
    smem = pl.BlockSpec(memory_space=pltpu.SMEM)
    vmem = pl.BlockSpec(memory_space=pltpu.VMEM)
    return pl.pallas_call(
        functools.partial(gather_kernel, rows, cols),
        in_specs=[smem, smem, vmem, vmem],
        out_specs=[vmem, vmem],
        out_shape=[shape, shape],
        compiler_params=params(32),
        cost_estimate=cost(2 * rounded.size * cells.size, 2 * rounded.size),
    )(helper, count, cells, rounded)


def scatter_kernel(
    helper_ref, cells_ref, picked_ref, home_ref, first_ref, mask_ref, perm_ref,
    second_ref, send_y_0, send_y_1, send_x, added, side_y,
):
    layers, comps, rows, cols = first_ref.shape
    chunks, _, slots = cells_ref.shape
    width = picked_ref.shape[-1]
    per_chunk = slots // width
    row_number = lax.broadcasted_iota(jnp.int32, (rows, slots), 0)
    added[...] = jnp.zeros_like(added)

    def one(i, carry):
        column, y = split_cells(cells_ref[i], rows, cols)
        chosen = one_hot(column, added.shape[1], slots)
        parts = []
        for j in range(per_chunk):
            b = i * per_chunk + j
            home = home_ref[helper_ref[0, 0, b]].astype(F32)
            value = picked_ref[b].astype(F32)
            part = home[0] * value[0:1]
            for r in range(1, comps):
                part += home[r] * value[r : r + 1]
            parts.append((-part).astype(BF16).astype(F32))
        correction = jnp.concatenate(parts, axis=1)
        at_row = row_number == y
        spread = jnp.concatenate(
            [jnp.where(at_row, correction[c : c + 1], 0.0).astype(BF16) for c in range(comps)], axis=0
        )
        added[...] += lax.dot_general(spread, chosen, (((1,), (1,)), ((), ())), preferred_element_type=F32)
        return carry

    lax.fori_loop(0, chunks, one, 0)
    for k in range(layers):
        for c in range(comps):
            second_ref[k, c] = first_ref[k, c] + added[c * rows : (c + 1) * rows, k * cols : (k + 1) * cols]
    clear = 1.0 - mask_ref[...].astype(F32)
    sends = (send_y_0, send_y_1, send_x)
    write_edges(lambda k, c: second_ref[k, c], comps, clear, perm_ref, side_y, sends)


def scatter(first, picked, home, helper, cells, mask, perm):
    layers, comps, rows, cols = first.shape
    smem = pl.BlockSpec(memory_space=pltpu.SMEM)
    vmem = pl.BlockSpec(memory_space=pltpu.VMEM)
    return pl.pallas_call(
        scatter_kernel,
        in_specs=[smem] + [vmem] * 6,
        out_specs=[vmem] * 4,
        out_shape=[jax.ShapeDtypeStruct(first.shape, F32), *edge_shapes(*first.shape)],
        scratch_shapes=[pltpu.VMEM((comps * rows, layers * cols), F32), edge_scratch(layers, comps, cols)],
        compiler_params=params(40),
        cost_estimate=cost(2 * first.size * cells.size, 8 * first.size),
    )(helper, cells, picked, home, first, mask, perm)


GROUPS = 4


def grad_kernel(inverse_ref, state_ref, picked_ref, out_ref):
    blocks, comps = inverse_ref.shape[:2]
    width = inverse_ref.shape[-1]

    def one(b, totals):
        inverse = inverse_ref[b].astype(F32)
        value = picked_ref[b].astype(F32)
        state = state_ref[b].astype(F32)
        part = inverse[0] * value[0:1]
        for r in range(1, comps):
            part += inverse[r] * value[r : r + 1]
        part *= state
        return tuple(totals[j] + part * state[j : j + 1] for j in range(comps))

    share = blocks // GROUPS
    for g in range(GROUPS):
        totals = lax.fori_loop(g * share, (g + 1) * share, one, (jnp.zeros((comps, width), F32),) * comps)
        for j in range(comps):
            out_ref[g, j] = totals[j]


def grad_part(inverse, state, picked):
    comps, width = inverse.shape[1], inverse.shape[-1]
    return pl.pallas_call(
        grad_kernel,
        out_shape=jax.ShapeDtypeStruct((GROUPS, comps, comps, width), F32),
        compiler_params=params(24),
        cost_estimate=cost(4 * inverse.size, 2 * inverse.size),
    )(inverse, state, picked)


def shards(
    cotangent,
    permeability,
    well_mask,
    diag_block,
    flux_block,
    cell_list,
    block_count,
    helper_of,
    flash_inverse,
    flash_coupling,
    phase_state,
):
    layers, comps, rows, cols = cotangent.shape
    blocks, width = helper_of.shape[-1], flash_inverse.shape[-1]
    inverse = flash_inverse.reshape(blocks, comps, comps, width)
    coupling = flash_coupling.reshape(blocks, comps, comps, width)
    state = phase_state.reshape(blocks, comps, width)
    cells = cell_list.reshape(-1, 1, min(CHUNK, cell_list.shape[-1]))

    def to_partners(array):
        return lax.all_to_all(array, AXES, split_axis=0, concat_axis=0, tiled=True)

    product, *sides = opening(inverse, coupling, cotangent, well_mask, permeability)
    home = to_partners(product)
    halos = exchange(*sides)
    first, rounded = apply_transposed(cotangent, well_mask, permeability, halos, diag_block, flux_block, True, 56)
    rounded, home = lax.optimization_barrier((rounded, home))
    picked, sent = gather(rounded, cells, helper_of, block_count, comps, rows, cols, width)
    at_helper = to_partners(sent)
    second, *sides = scatter(first, picked, home, helper_of, cells, well_mask, permeability)
    halos = exchange(*sides)
    (adjoint,) = apply_transposed(second, well_mask, permeability, halos, diag_block, flux_block, False, 32)

    totals = lax.psum(grad_part(inverse, state, at_helper), AXES)
    devices = lax.axis_size("gx") * lax.axis_size("gy")
    grad_scale = 1.0 / math.sqrt(width * devices * devices)
    interaction_grad = -grad_scale * jnp.sum(totals, axis=(0, 3)).T
    return (adjoint, interaction_grad)


def solution(mesh):
    return jax.shard_map(
        shards,
        mesh=mesh,
        in_specs=(
            P(None, None, "gy", "gx"),
            P(None, "gy", "gx"),
            P("gy", "gx"),
            P(None, None, None, "gy", "gx"),
            P(None, None, None, "gy", "gx"),
            P("gy", "gx", None),
            P("gy", "gx"),
            P("gy", "gx", None),
            P("gy", "gx", None, None, None, None),
            P("gy", "gx", None, None, None, None),
            P("gy", "gx", None, None, None),
        ),
        out_specs=(P(None, None, "gy", "gx"), P()),
        check_vma=False,
    )
```

```python
import functools
import math

import jax
import jax.numpy as jnp
from jax import lax
from jax.experimental import pallas as pl
from jax.experimental.pallas import tpu as pltpu
from jax.sharding import PartitionSpec as P

F32 = jnp.float32
BF16 = jnp.bfloat16
AXES = ("gx", "gy")
MIB = 1024 * 1024
CHUNK = 512


def params(mib):
    return pltpu.CompilerParams(vmem_limit_bytes=mib * MIB)


def cost(flops, moved):
    return pl.CostEstimate(flops=int(flops), bytes_accessed=int(moved), transcendentals=0)


def round_up(number, step):
    return -(-number // step) * step


def write_edges(field, comps, clear, perm_ref, side_y, sends):
    send_y_0, send_y_1, send_x = sends
    layers, rows, cols = perm_ref.shape
    lane = lax.broadcasted_iota(jnp.int32, (rows, cols), 1)
    pair = lane // 2
    along_x = jnp.zeros((rows, cols), F32)
    side_y[...] = jnp.zeros_like(side_y)
    for k in range(layers):
        for c in range(comps + 1):
            if c < comps:
                value, at = field(k, c) * clear, k * comps + c
            else:
                value, at = perm_ref[k], layers * comps + k
            side_y[0, at : at + 1, :] = value[0:1]
            side_y[1, at : at + 1, :] = value[rows - 1 : rows]
            along_x = jnp.where(pair == at, pltpu.roll(value, (2 * at + 1) % cols, 1), along_x)
    even = lax.axis_index("gy") % 2 == 0
    send_x[...] = along_x.astype(BF16)
    low, high = side_y[0].astype(BF16), side_y[1].astype(BF16)
    send_y_0[...] = jnp.where(even, high, low)
    send_y_1[...] = jnp.where(even, low, high)


def fetch(copies):
    for copy in copies:
        copy.start()
    for copy in copies:
        copy.wait()


def opening_kernel(
    inverse_hbm, coupling_hbm, field_hbm, mask_hbm, perm_hbm,
    product_ref, send_y_0, send_y_1, send_x,
    inverse_ref, coupling_ref, field_ref, mask_ref, perm_ref, side_y, sems,
):
    sources = (inverse_hbm, coupling_hbm, field_hbm, mask_hbm, perm_hbm)
    targets = (inverse_ref, coupling_ref, field_ref, mask_ref, perm_ref)
    copies = [pltpu.make_async_copy(a, b, sems.at[i]) for i, (a, b) in enumerate(zip(sources, targets))]
    for copy in copies:
        copy.start()
    blocks, comps = inverse_ref.shape[:2]
    copies[0].wait()
    copies[1].wait()

    def one(b, carry):
        inverse = inverse_ref[b].astype(F32)
        coupling = coupling_ref[b].astype(F32)
        for r in range(comps):
            row = inverse[r, 0:1] * coupling[0]
            for m in range(1, comps):
                row += inverse[r, m : m + 1] * coupling[m]
            product_ref[b, r] = row.astype(BF16)
        return carry

    lax.fori_loop(0, blocks, one, 0)
    for copy in copies[2:]:
        copy.wait()
    clear = 1.0 - mask_ref[...].astype(F32)
    sends = (send_y_0, send_y_1, send_x)
    write_edges(lambda k, c: field_ref[k, c], comps, clear, perm_ref, side_y, sends)


def edge_rows(layers, comps):
    return round_up(layers * (comps + 1), 16)


def edge_shapes(layers, comps, rows, cols):
    along_y = (edge_rows(layers, comps), cols)
    return [jax.ShapeDtypeStruct(shape, BF16) for shape in (along_y, along_y, (rows, cols))]


def edge_scratch(layers, comps, cols):
    return pltpu.VMEM((2, edge_rows(layers, comps), cols), F32)


def opening(inverse, coupling, field, mask, perm):
    layers, comps, rows, cols = field.shape
    hbm = pl.BlockSpec(memory_space=pltpu.HBM)
    vmem = pl.BlockSpec(memory_space=pltpu.VMEM)
    arrays = (inverse, coupling, field, mask, perm)
    return pl.pallas_call(
        opening_kernel,
        in_specs=[hbm] * 5,
        out_specs=[vmem] * 4,
        out_shape=[jax.ShapeDtypeStruct(inverse.shape, BF16), *edge_shapes(*field.shape)],
        scratch_shapes=[
            *(pltpu.VMEM(array.shape, array.dtype) for array in arrays),
            edge_scratch(layers, comps, cols),
            pltpu.SemaphoreType.DMA((5,)),
        ],
        compiler_params=params(24),
        cost_estimate=cost(16 * inverse.size + 4 * field.size, 160 * field.size),
    )(*(pltpu.with_memory_space_constraint(array, pltpu.HBM) for array in arrays))


def exchange(send_y_0, send_y_1, send_x):
    def swaps(axis, first, second):
        count = lax.axis_size(axis)
        results = []
        for start, array in ((0, first), (1, second)):
            pairs = [(i, i + 1) for i in range(start, count - 1, 2)]
            results.append(lax.ppermute(array, axis, pairs + [(j, i) for i, j in pairs]))
        return results

    return (*swaps("gy", send_y_0, send_y_1), *swaps("gx", send_x, send_x))


TILE = 16


def reciprocal(value):
    guess = pl.reciprocal(value, approx=True)
    return guess * (2.0 - value * guess)


def weight(centre, beside):
    return 2.0 * centre * beside * reciprocal(centre + beside)


def apply_kernel(want_rounded, field_ref, mask_ref, perm_ref, y_0, y_1, x_0, x_1, diag_ref, flux_ref, *rest):
    if want_rounded:
        out_ref, rounded_ref, *rest = rest
    else:
        out_hbm, *rest, out_ref, out_sems = rest
    padded, padded_perm, edge_x, place, beside_edge, perm_edge = rest
    layers, comps, rows, cols = field_ref.shape
    top = 8

    def out_copy(k):
        return pltpu.make_async_copy(out_ref.at[k], out_hbm.at[k], out_sems.at[k])

    lane = lax.broadcasted_iota(jnp.int32, (rows, cols), 1)
    number = lax.broadcasted_iota(jnp.int32, (cols, cols), 0)
    spot = lax.broadcasted_iota(jnp.int32, (cols, cols), 1)
    for r in range(comps):
        taken = ((number == 2 * r) & (spot == 0)) | ((number == 2 * r + 1) & (spot == cols - 1))
        place[:, r * cols : (r + 1) * cols] = jnp.where(taken, 1.0, 0.0).astype(BF16)
    even_x = lax.axis_index("gx") % 2 == 0
    even_y = lax.axis_index("gy") % 2 == 0
    side_0, side_1 = x_0[...].astype(F32), x_1[...].astype(F32)
    edge_x[...] = jnp.where((lane % 2 == 0) == even_x, side_1, side_0)
    clear = 1.0 - mask_ref[...].astype(F32)

    def layer(k, carry):
        above = jnp.minimum(k + 1, layers - 1)
        below = jnp.maximum(k - 1, 0)

        turned = pltpu.roll(edge_x[...], lax.rem(cols - 2 * comps * k, cols), 1).astype(BF16)
        beside_edge[...] = jnp.dot(turned, place[...], preferred_element_type=F32)
        at_low = 2 * (layers * comps + k)
        perm_low = pltpu.roll(edge_x[...], lax.rem(cols - at_low, cols), 1)
        perm_high = pltpu.roll(edge_x[...], lax.rem(2 * cols - at_low - 2, cols), 1)
        perm_edge[...] = jnp.where(lane == 0, perm_low, perm_high)

        odd = k % 2 == 1
        here = pl.ds(pl.multiple_of(16 * (k // 2), 16), 16)
        side_0, side_1 = y_0[here].astype(F32), y_1[here].astype(F32)
        side_0 = jnp.where(odd, side_0[comps:], side_0[:comps])
        side_1 = jnp.where(odd, side_1[comps:], side_1[:comps])
        low_y, high_y = jnp.where(even_y, side_1, side_0), jnp.where(even_y, side_0, side_1)
        here = slice(layers * comps, layers * comps + 16)
        mine = lax.broadcasted_iota(jnp.int32, (16, cols), 0) == k
        perm_0 = jnp.sum(jnp.where(mine, y_0[here].astype(F32), 0.0), axis=0, keepdims=True)
        perm_1 = jnp.sum(jnp.where(mine, y_1[here].astype(F32), 0.0), axis=0, keepdims=True)
        for c in range(comps):
            padded[c, top : top + rows] = field_ref[k, c] * clear
            padded[c, top - 1 : top] = low_y[c : c + 1]
            padded[c, top + rows : top + rows + 1] = high_y[c : c + 1]
        padded_perm[top : top + rows] = perm_ref[k]
        padded_perm[top - 1 : top] = jnp.where(even_y, perm_1, perm_0)
        padded_perm[top + rows : top + rows + 1] = jnp.where(even_y, perm_0, perm_1)
        narrow = lax.broadcasted_iota(jnp.int32, (TILE, cols), 1)
        is_first, is_last = narrow == 0, narrow == cols - 1
        for y in range(0, rows, TILE):
            here = slice(y, y + TILE)
            at = top + y
            well = mask_ref[here].astype(F32)
            free = 1.0 - well
            centre = perm_ref[k, here]
            perm_beside = perm_edge[here]
            perm_left = jnp.where(is_first, perm_beside, pltpu.roll(centre, 1, 1))
            perm_right = jnp.where(is_last, perm_beside, pltpu.roll(centre, cols - 1, 1))
            to_left, to_right = weight(centre, perm_left), weight(centre, perm_right)
            weights = [
                jnp.where(k < layers - 1, weight(centre, perm_ref[above, here]), 0.0) * free,
                jnp.where(k > 0, weight(centre, perm_ref[below, here]), 0.0) * free,
                weight(centre, padded_perm[at + 1 : at + 1 + TILE]),
                weight(centre, padded_perm[at - 1 : at - 1 + TILE]),
                jnp.where(is_last, 0.0, to_right),
                jnp.where(is_first, 0.0, to_left),
                jnp.where(is_first, to_left, jnp.where(is_last, to_right, 0.0)),
            ]
            total = [None] * comps
            for r in range(comps):
                own = padded[r, at : at + TILE]
                summed = (
                    weights[0] * field_ref[above, r, here]
                    + weights[1] * field_ref[below, r, here]
                    + weights[2] * padded[r, at + 1 : at + 1 + TILE]
                    + weights[3] * padded[r, at - 1 : at - 1 + TILE]
                    + weights[4] * pltpu.roll(own, cols - 1, 1)
                    + weights[5] * pltpu.roll(own, 1, 1)
                    + weights[6] * beside_edge[here, r * cols : (r + 1) * cols]
                )
                for c in range(comps):
                    term = diag_ref[k, r, c, here].astype(F32) * own - flux_ref[k, r, c, here].astype(F32) * summed
                    total[c] = term if r == 0 else total[c] + term
            for c in range(comps):
                value = total[c] + well * field_ref[k, c, here]
                out_ref[k, c, here] = value
                if want_rounded:
                    columns = pl.ds(pl.multiple_of(k * cols, cols), cols)
                    rounded_ref[c * rows + y : c * rows + y + TILE, columns] = value.astype(BF16)
        if not want_rounded:
            out_copy(k).start()
        return carry

    lax.fori_loop(0, layers, layer, 0)
    if not want_rounded:
        for k in range(layers):
            out_copy(k).wait()


def apply_transposed(field, mask, perm, halos, diag, flux, want_rounded):
    layers, comps, rows, cols = field.shape
    vmem = pl.BlockSpec(memory_space=pltpu.VMEM)
    out_shape = [jax.ShapeDtypeStruct(field.shape, F32)]
    if want_rounded:
        out_specs, tail = [vmem, vmem], []
        out_shape.append(jax.ShapeDtypeStruct((comps * rows, layers * cols), BF16))
    else:
        out_specs = [pl.BlockSpec(memory_space=pltpu.HBM)]
        tail = [pltpu.VMEM(field.shape, F32), pltpu.SemaphoreType.DMA((layers,))]
    return pl.pallas_call(
        functools.partial(apply_kernel, want_rounded),
        in_specs=[vmem] * 9,
        out_specs=out_specs,
        out_shape=out_shape,
        scratch_shapes=[
            pltpu.VMEM((comps, rows + 16, cols), F32),
            pltpu.VMEM((rows + 16, cols), F32),
            pltpu.VMEM((rows, cols), F32),
            pltpu.VMEM((cols, comps * cols), BF16),
            pltpu.VMEM((rows, comps * cols), F32),
            pltpu.VMEM((rows, cols), F32),
            *tail,
        ],
        compiler_params=params(24),
        cost_estimate=cost(8 * diag.size, 4 * diag.size + 8 * field.size),
    )(field, mask, perm, *halos, diag, flux)


def split_cells(cells, rows, cols):
    layer = cells // (rows * cols)
    y = (cells // cols) % rows
    return layer * cols + cells % cols, y


def one_hot(column, count, slots):
    number = lax.broadcasted_iota(jnp.int32, (count, slots), 0)
    return jnp.where(number == column, 1.0, 0.0).astype(BF16)


def gather_kernel(rows, cols, helper_ref, count_ref, cells_ref, rounded_ref, picked_ref, sent_ref):
    chunks, _, slots = cells_ref.shape
    width = picked_ref.shape[-1]
    comps = picked_ref.shape[1]
    per_chunk = slots // width
    row_number = lax.broadcasted_iota(jnp.int32, (rows, slots), 0)

    def one(i, carry):
        column, y = split_cells(cells_ref[i], rows, cols)
        chosen = one_hot(column, rounded_ref.shape[1], slots)
        found = jnp.dot(rounded_ref[...], chosen, preferred_element_type=F32)
        at_row = row_number == y
        values = [
            jnp.sum(jnp.where(at_row, found[c * rows : (c + 1) * rows], 0.0), axis=0, keepdims=True)
            for c in range(comps)
        ]
        values = jnp.concatenate(values, axis=0)
        for j in range(per_chunk):
            b = i * per_chunk + j
            live = jnp.where(b < count_ref[0, 0], 1.0, 0.0)
            value = (values[:, j * width : (j + 1) * width] * live).astype(BF16)
            picked_ref[b] = value
            sent_ref[helper_ref[0, 0, b]] = value
        return carry

    lax.fori_loop(0, chunks, one, 0)


def gather(rounded, cells, helper, count, comps, rows, cols, width):
    blocks = helper.shape[-1]
    shape = jax.ShapeDtypeStruct((blocks, comps, width), BF16)
    smem = pl.BlockSpec(memory_space=pltpu.SMEM)
    vmem = pl.BlockSpec(memory_space=pltpu.VMEM)
    return pl.pallas_call(
        functools.partial(gather_kernel, rows, cols),
        in_specs=[smem, smem, vmem, vmem],
        out_specs=[vmem, vmem],
        out_shape=[shape, shape],
        compiler_params=params(32),
        cost_estimate=cost(2 * rounded.size * cells.size, 2 * rounded.size),
    )(helper, count, cells, rounded)


def scatter_kernel(
    helper_ref, cells_ref, picked_ref, home_ref, first_ref, mask_ref, perm_ref,
    second_ref, send_y_0, send_y_1, send_x, added, side_y,
):
    layers, comps, rows, cols = first_ref.shape
    chunks, _, slots = cells_ref.shape
    width = picked_ref.shape[-1]
    per_chunk = slots // width
    row_number = lax.broadcasted_iota(jnp.int32, (rows, slots), 0)
    added[...] = jnp.zeros_like(added)

    def one(i, carry):
        column, y = split_cells(cells_ref[i], rows, cols)
        chosen = one_hot(column, added.shape[1], slots)
        parts = []
        for j in range(per_chunk):
            b = i * per_chunk + j
            home = home_ref[helper_ref[0, 0, b]].astype(F32)
            value = picked_ref[b].astype(F32)
            part = home[0] * value[0:1]
            for r in range(1, comps):
                part += home[r] * value[r : r + 1]
            parts.append((-part).astype(BF16).astype(F32))
        correction = jnp.concatenate(parts, axis=1)
        at_row = row_number == y
        spread = jnp.concatenate(
            [jnp.where(at_row, correction[c : c + 1], 0.0).astype(BF16) for c in range(comps)], axis=0
        )
        added[...] += lax.dot_general(spread, chosen, (((1,), (1,)), ((), ())), preferred_element_type=F32)
        return carry

    lax.fori_loop(0, chunks, one, 0)
    for k in range(layers):
        for c in range(comps):
            second_ref[k, c] = first_ref[k, c] + added[c * rows : (c + 1) * rows, k * cols : (k + 1) * cols]
    clear = 1.0 - mask_ref[...].astype(F32)
    sends = (send_y_0, send_y_1, send_x)
    write_edges(lambda k, c: second_ref[k, c], comps, clear, perm_ref, side_y, sends)


def scatter(first, picked, home, helper, cells, mask, perm):
    layers, comps, rows, cols = first.shape
    smem = pl.BlockSpec(memory_space=pltpu.SMEM)
    vmem = pl.BlockSpec(memory_space=pltpu.VMEM)
    return pl.pallas_call(
        scatter_kernel,
        in_specs=[smem] + [vmem] * 6,
        out_specs=[vmem] * 4,
        out_shape=[jax.ShapeDtypeStruct(first.shape, F32), *edge_shapes(*first.shape)],
        scratch_shapes=[pltpu.VMEM((comps * rows, layers * cols), F32), edge_scratch(layers, comps, cols)],
        compiler_params=params(24),
        cost_estimate=cost(2 * first.size * cells.size, 160 * first.size),
    )(helper, cells, picked, home, first, mask, perm)


def grad_kernel(inverse_ref, state_ref, picked_ref, out_ref):
    blocks, comps = inverse_ref.shape[:2]
    width = inverse_ref.shape[-1]

    def one(b, totals):
        inverse = inverse_ref[b].astype(F32)
        value = picked_ref[b].astype(F32)
        state = state_ref[b].astype(F32)
        part = inverse[0] * value[0:1]
        for r in range(1, comps):
            part += inverse[r] * value[r : r + 1]
        part *= state
        return tuple(totals[j] + part * state[j : j + 1] for j in range(comps))

    totals = lax.fori_loop(0, blocks, one, (jnp.zeros((comps, width), F32),) * comps)
    lane = lax.broadcasted_iota(jnp.int32, (comps, width), 1)
    result = jnp.zeros((comps, width), F32)
    for j in range(comps):
        result = jnp.where(lane == j, jnp.sum(totals[j], axis=1, keepdims=True), result)
    for i in range(out_ref.shape[0]):
        out_ref[i] = result


def grad_part(inverse, state, picked, copies):
    comps, width = inverse.shape[1], inverse.shape[-1]
    return pl.pallas_call(
        grad_kernel,
        out_shape=jax.ShapeDtypeStruct((copies, comps, width), F32),
        compiler_params=params(24),
        cost_estimate=cost(4 * inverse.size, 2 * inverse.size),
    )(inverse, state, picked)


def total_kernel(scale, parts_ref, out_ref):
    total = parts_ref[0]
    for i in range(1, parts_ref.shape[0]):
        total += parts_ref[i]
    out_ref[...] = (total * scale)[:, : out_ref.shape[1]]


def grad_total(parts, scale):
    return pl.pallas_call(
        functools.partial(total_kernel, scale),
        out_shape=jax.ShapeDtypeStruct((parts.shape[1],) * 2, F32),
        cost_estimate=cost(parts.size, 4 * parts.size),
    )(parts)


def shards(
    cotangent,
    permeability,
    well_mask,
    diag_block,
    flux_block,
    cell_list,
    block_count,
    helper_of,
    flash_inverse,
    flash_coupling,
    phase_state,
):
    layers, comps, rows, cols = cotangent.shape
    blocks, width = helper_of.shape[-1], flash_inverse.shape[-1]
    inverse = flash_inverse.reshape(blocks, comps, comps, width)
    coupling = flash_coupling.reshape(blocks, comps, comps, width)
    state = phase_state.reshape(blocks, comps, width)
    cells = cell_list.reshape(-1, 1, min(CHUNK, cell_list.shape[-1]))

    def to_partners(array):
        return lax.all_to_all(array, AXES, split_axis=0, concat_axis=0, tiled=True)

    product, *sides = opening(inverse, coupling, cotangent, well_mask, permeability)
    home = to_partners(product)
    halos = exchange(*sides)
    first, rounded = apply_transposed(cotangent, well_mask, permeability, halos, diag_block, flux_block, True)
    rounded, home = lax.optimization_barrier((rounded, home))
    picked, sent = gather(rounded, cells, helper_of, block_count, comps, rows, cols, width)
    at_helper = to_partners(sent)
    second, *sides = scatter(first, picked, home, helper_of, cells, well_mask, permeability)
    halos = exchange(*sides)
    at_helper, *halos = lax.optimization_barrier((at_helper, *halos))
    devices = lax.axis_size("gx") * lax.axis_size("gy")
    parts = to_partners(grad_part(inverse, state, at_helper, devices))
    (adjoint,) = apply_transposed(second, well_mask, permeability, halos, diag_block, flux_block, False)
    interaction_grad = grad_total(parts, -1.0 / math.sqrt(width * devices * devices))
    return (adjoint, interaction_grad)


def solution(mesh):
    return jax.shard_map(
        shards,
        mesh=mesh,
        in_specs=(
            P(None, None, "gy", "gx"),
            P(None, "gy", "gx"),
            P("gy", "gx"),
            P(None, None, None, "gy", "gx"),
            P(None, None, None, "gy", "gx"),
            P("gy", "gx", None),
            P("gy", "gx"),
            P("gy", "gx", None),
            P("gy", "gx", None, None, None, None),
            P("gy", "gx", None, None, None, None),
            P("gy", "gx", None, None, None),
        ),
        out_specs=(P(None, None, "gy", "gx"), P()),
        check_vma=False,
    )
```

```python
import functools
import math

import jax
import jax.numpy as jnp
from jax import lax
from jax.experimental import pallas as pl
from jax.experimental.pallas import tpu as pltpu
from jax.sharding import PartitionSpec as P

F32 = jnp.float32
BF16 = jnp.bfloat16
AXES = ("gx", "gy")
MIB = 1024 * 1024
CHUNK = 512


def params(mib):
    return pltpu.CompilerParams(vmem_limit_bytes=mib * MIB)


def cost(flops, moved):
    return pl.CostEstimate(flops=int(flops), bytes_accessed=int(moved), transcendentals=0)


def round_up(number, step):
    return -(-number // step) * step


def write_edges(field, comps, clear, perm_ref, side_y, sends):
    send_y_0, send_y_1, send_x = sends
    layers, rows, cols = perm_ref.shape
    lane = lax.broadcasted_iota(jnp.int32, (rows, cols), 1)
    pair = lane // 2
    along_x = jnp.zeros((rows, cols), F32)
    side_y[...] = jnp.zeros_like(side_y)
    for k in range(layers):
        for c in range(comps + 1):
            if c < comps:
                value, at = field(k, c) * clear, k * comps + c
            else:
                value, at = perm_ref[k], layers * comps + k
            side_y[0, at : at + 1, :] = value[0:1]
            side_y[1, at : at + 1, :] = value[rows - 1 : rows]
            along_x = jnp.where(pair == at, pltpu.roll(value, (2 * at + 1) % cols, 1), along_x)
    even = lax.axis_index("gy") % 2 == 0
    send_x[...] = along_x.astype(BF16)
    low, high = side_y[0].astype(BF16), side_y[1].astype(BF16)
    send_y_0[...] = jnp.where(even, high, low)
    send_y_1[...] = jnp.where(even, low, high)


def opening_kernel(
    field_hbm, mask_hbm, perm_hbm,
    send_y_0, send_y_1, send_x, field_ref, mask_ref, perm_ref,
    side_y, sems,
):
    sources, targets = (field_hbm, mask_hbm, perm_hbm), (field_ref, mask_ref, perm_ref)
    copies = [pltpu.make_async_copy(a, b, sems.at[i]) for i, (a, b) in enumerate(zip(sources, targets))]
    for copy in copies:
        copy.start()
    for copy in copies:
        copy.wait()
    clear = 1.0 - mask_ref[...].astype(F32)
    sends = (send_y_0, send_y_1, send_x)
    write_edges(lambda k, c: field_ref[k, c], field_ref.shape[1], clear, perm_ref, side_y, sends)


def edge_rows(layers, comps):
    return round_up(layers * (comps + 1), 16)


def edge_shapes(layers, comps, rows, cols):
    along_y = (edge_rows(layers, comps), cols)
    return [jax.ShapeDtypeStruct(shape, BF16) for shape in (along_y, along_y, (rows, cols))]


def edge_scratch(layers, comps, cols):
    return pltpu.VMEM((2, edge_rows(layers, comps), cols), F32)


def opening(field, mask, perm):
    layers, comps, rows, cols = field.shape
    hbm = pl.BlockSpec(memory_space=pltpu.HBM)
    vmem = pl.BlockSpec(memory_space=pltpu.VMEM)
    arrays = (field, mask, perm)
    return pl.pallas_call(
        opening_kernel,
        in_specs=[hbm] * 3,
        out_specs=[vmem] * 6,
        out_shape=[*edge_shapes(*field.shape), *(pltpu.VMEM(array.shape, array.dtype) for array in arrays)],
        scratch_shapes=[
            edge_scratch(layers, comps, cols),
            pltpu.SemaphoreType.DMA((3,)),
        ],
        compiler_params=params(16),
        cost_estimate=cost(4 * field.size, 8 * field.size),
    )(*(pltpu.with_memory_space_constraint(array, pltpu.HBM) for array in arrays))


def exchange(send_y_0, send_y_1, send_x):
    def swaps(axis, first, second):
        count = lax.axis_size(axis)
        results = []
        for start, array in ((0, first), (1, second)):
            pairs = [(i, i + 1) for i in range(start, count - 1, 2)]
            results.append(lax.ppermute(array, axis, pairs + [(j, i) for i, j in pairs]))
        return results

    return (*swaps("gy", send_y_0, send_y_1), *swaps("gx", send_x, send_x))


TILE = 16


def reciprocal(value):
    guess = pl.reciprocal(value, approx=True)
    return guess * (2.0 - value * guess)


def weight(centre, beside):
    return 2.0 * centre * beside * reciprocal(centre + beside)


def apply_kernel(is_first_apply, field_ref, mask_ref, perm_ref, y_0, y_1, x_0, x_1, diag_in, flux_in, *rest):
    if is_first_apply:
        out_ref, rounded_ref, diag_ref, flux_ref, *rest, sems = rest
    else:
        out_hbm, *rest, out_ref, out_sems = rest
        diag_ref, flux_ref = diag_in, flux_in
    padded, padded_perm, edge_x, place, beside_edge, perm_edge = rest
    layers, comps, rows, cols = field_ref.shape
    top = 8

    def out_copy(k):
        return pltpu.make_async_copy(out_ref.at[k], out_hbm.at[k], out_sems.at[k])

    def blocks(k):
        return (
            pltpu.make_async_copy(diag_in.at[k], diag_ref.at[k], sems.at[0, k]),
            pltpu.make_async_copy(flux_in.at[k], flux_ref.at[k], sems.at[1, k]),
        )

    if is_first_apply:
        for k in range(layers):
            for copy in blocks(k):
                copy.start()

    lane = lax.broadcasted_iota(jnp.int32, (rows, cols), 1)
    number = lax.broadcasted_iota(jnp.int32, (cols, cols), 0)
    spot = lax.broadcasted_iota(jnp.int32, (cols, cols), 1)
    for r in range(comps):
        taken = ((number == 2 * r) & (spot == 0)) | ((number == 2 * r + 1) & (spot == cols - 1))
        place[:, r * cols : (r + 1) * cols] = jnp.where(taken, 1.0, 0.0).astype(BF16)
    even_x = lax.axis_index("gx") % 2 == 0
    even_y = lax.axis_index("gy") % 2 == 0
    side_0, side_1 = x_0[...].astype(F32), x_1[...].astype(F32)
    edge_x[...] = jnp.where((lane % 2 == 0) == even_x, side_1, side_0)
    clear = 1.0 - mask_ref[...].astype(F32)

    def layer(k, carry):
        above = jnp.minimum(k + 1, layers - 1)
        below = jnp.maximum(k - 1, 0)

        turned = pltpu.roll(edge_x[...], lax.rem(cols - 2 * comps * k, cols), 1).astype(BF16)
        beside_edge[...] = jnp.dot(turned, place[...], preferred_element_type=F32)
        at_low = 2 * (layers * comps + k)
        perm_low = pltpu.roll(edge_x[...], lax.rem(cols - at_low, cols), 1)
        perm_high = pltpu.roll(edge_x[...], lax.rem(2 * cols - at_low - 2, cols), 1)
        perm_edge[...] = jnp.where(lane == 0, perm_low, perm_high)

        odd = k % 2 == 1
        here = pl.ds(pl.multiple_of(16 * (k // 2), 16), 16)
        side_0, side_1 = y_0[here].astype(F32), y_1[here].astype(F32)
        side_0 = jnp.where(odd, side_0[comps:], side_0[:comps])
        side_1 = jnp.where(odd, side_1[comps:], side_1[:comps])
        low_y, high_y = jnp.where(even_y, side_1, side_0), jnp.where(even_y, side_0, side_1)
        here = slice(layers * comps, layers * comps + 16)
        mine = lax.broadcasted_iota(jnp.int32, (16, cols), 0) == k
        perm_0 = jnp.sum(jnp.where(mine, y_0[here].astype(F32), 0.0), axis=0, keepdims=True)
        perm_1 = jnp.sum(jnp.where(mine, y_1[here].astype(F32), 0.0), axis=0, keepdims=True)
        for c in range(comps):
            padded[c, top : top + rows] = field_ref[k, c] * clear
            padded[c, top - 1 : top] = low_y[c : c + 1]
            padded[c, top + rows : top + rows + 1] = high_y[c : c + 1]
        padded_perm[top : top + rows] = perm_ref[k]
        padded_perm[top - 1 : top] = jnp.where(even_y, perm_1, perm_0)
        padded_perm[top + rows : top + rows + 1] = jnp.where(even_y, perm_0, perm_1)
        if is_first_apply:
            for copy in blocks(k):
                copy.wait()
        narrow = lax.broadcasted_iota(jnp.int32, (TILE, cols), 1)
        is_first, is_last = narrow == 0, narrow == cols - 1
        for y in range(0, rows, TILE):
            here = slice(y, y + TILE)
            at = top + y
            well = mask_ref[here].astype(F32)
            free = 1.0 - well
            centre = perm_ref[k, here]
            perm_beside = perm_edge[here]
            perm_left = jnp.where(is_first, perm_beside, pltpu.roll(centre, 1, 1))
            perm_right = jnp.where(is_last, perm_beside, pltpu.roll(centre, cols - 1, 1))
            to_left, to_right = weight(centre, perm_left), weight(centre, perm_right)
            weights = [
                jnp.where(k < layers - 1, weight(centre, perm_ref[above, here]), 0.0) * free,
                jnp.where(k > 0, weight(centre, perm_ref[below, here]), 0.0) * free,
                weight(centre, padded_perm[at + 1 : at + 1 + TILE]),
                weight(centre, padded_perm[at - 1 : at - 1 + TILE]),
                jnp.where(is_last, 0.0, to_right),
                jnp.where(is_first, 0.0, to_left),
                jnp.where(is_first, to_left, jnp.where(is_last, to_right, 0.0)),
            ]
            total = [None] * comps
            for r in range(comps):
                own = padded[r, at : at + TILE]
                summed = (
                    weights[0] * field_ref[above, r, here]
                    + weights[1] * field_ref[below, r, here]
                    + weights[2] * padded[r, at + 1 : at + 1 + TILE]
                    + weights[3] * padded[r, at - 1 : at - 1 + TILE]
                    + weights[4] * pltpu.roll(own, cols - 1, 1)
                    + weights[5] * pltpu.roll(own, 1, 1)
                    + weights[6] * beside_edge[here, r * cols : (r + 1) * cols]
                )
                for c in range(comps):
                    term = diag_ref[k, r, c, here].astype(F32) * own - flux_ref[k, r, c, here].astype(F32) * summed
                    total[c] = term if r == 0 else total[c] + term
            for c in range(comps):
                value = total[c] + well * field_ref[k, c, here]
                out_ref[k, c, here] = value
                if is_first_apply:
                    columns = pl.ds(pl.multiple_of(k * cols, cols), cols)
                    rounded_ref[c * rows + y : c * rows + y + TILE, columns] = value.astype(BF16)
        if not is_first_apply:
            out_copy(k).start()
        return carry

    lax.fori_loop(0, layers, layer, 0)
    if not is_first_apply:
        for k in range(layers):
            out_copy(k).wait()


def apply_transposed(field, mask, perm, halos, diag, flux, is_first_apply):
    layers, comps, rows, cols = field.shape
    vmem = pl.BlockSpec(memory_space=pltpu.VMEM)
    hbm = pl.BlockSpec(memory_space=pltpu.HBM)
    out_shape = [jax.ShapeDtypeStruct(field.shape, F32)]
    if is_first_apply:
        block_spec, out_specs = hbm, [vmem] * 4
        out_shape.append(jax.ShapeDtypeStruct((comps * rows, layers * cols), BF16))
        out_shape += [pltpu.VMEM(diag.shape, BF16), pltpu.VMEM(flux.shape, BF16)]
        tail = [pltpu.SemaphoreType.DMA((2, layers))]
        diag, flux = (pltpu.with_memory_space_constraint(block, pltpu.HBM) for block in (diag, flux))
    else:
        block_spec, out_specs = vmem, [hbm]
        tail = [pltpu.VMEM(field.shape, F32), pltpu.SemaphoreType.DMA((layers,))]
    return pl.pallas_call(
        functools.partial(apply_kernel, is_first_apply),
        in_specs=[vmem] * 7 + [block_spec] * 2,
        out_specs=out_specs,
        out_shape=out_shape,
        scratch_shapes=[
            pltpu.VMEM((comps, rows + 16, cols), F32),
            pltpu.VMEM((rows + 16, cols), F32),
            pltpu.VMEM((rows, cols), F32),
            pltpu.VMEM((cols, comps * cols), BF16),
            pltpu.VMEM((rows, comps * cols), F32),
            pltpu.VMEM((rows, cols), F32),
            *tail,
        ],
        compiler_params=params(24),
        cost_estimate=cost(8 * diag.size, 4 * diag.size + 8 * field.size),
    )(field, mask, perm, *halos, diag, flux)


def split_cells(cells, rows, cols):
    layer = cells // (rows * cols)
    y = (cells // cols) % rows
    return layer * cols + cells % cols, y


def one_hot(column, count, slots):
    number = lax.broadcasted_iota(jnp.int32, (count, slots), 0)
    return jnp.where(number == column, 1.0, 0.0).astype(BF16)


def gather_kernel(rows, cols, helper_ref, count_ref, cells_ref, rounded_ref, sent_ref):
    chunks, _, slots = cells_ref.shape
    comps, width = sent_ref.shape[1:]
    per_chunk = slots // width
    row_number = lax.broadcasted_iota(jnp.int32, (rows, slots), 0)

    def one(i, carry):
        column, y = split_cells(cells_ref[i], rows, cols)
        chosen = one_hot(column, rounded_ref.shape[1], slots)
        found = jnp.dot(rounded_ref[...], chosen, preferred_element_type=F32)
        at_row = row_number == y
        values = [
            jnp.sum(jnp.where(at_row, found[c * rows : (c + 1) * rows], 0.0), axis=0, keepdims=True)
            for c in range(comps)
        ]
        values = jnp.concatenate(values, axis=0)
        for j in range(per_chunk):
            b = i * per_chunk + j
            live = jnp.where(b < count_ref[0, 0], 1.0, 0.0)
            sent_ref[helper_ref[0, 0, b]] = (values[:, j * width : (j + 1) * width] * live).astype(BF16)
        return carry

    lax.fori_loop(0, chunks, one, 0)


def gather(rounded, cells, helper, count, comps, rows, cols, width):
    blocks = helper.shape[-1]
    shape = jax.ShapeDtypeStruct((blocks, comps, width), BF16)
    smem = pl.BlockSpec(memory_space=pltpu.SMEM)
    vmem = pl.BlockSpec(memory_space=pltpu.VMEM)
    return pl.pallas_call(
        functools.partial(gather_kernel, rows, cols),
        in_specs=[smem, smem, vmem, vmem],
        out_specs=vmem,
        out_shape=shape,
        compiler_params=params(16),
        cost_estimate=cost(2 * rounded.size * cells.size, 2 * rounded.size),
    )(helper, count, cells, rounded)


PARTS = 3


def helper_kernel(inverse_ref, coupling_ref, state_ref, picked_ref, reply_ref):
    blocks, comps = inverse_ref.shape[:2]
    width = inverse_ref.shape[-1]

    def transposed(block_ref, b, value):
        block = block_ref[b].astype(F32)
        total = block[0] * value[0:1]
        for r in range(1, comps):
            total += block[r] * value[r : r + 1]
        return total

    def one(b, totals):
        multiplier = transposed(inverse_ref, b, picked_ref[b].astype(F32))
        state = state_ref[b].astype(F32)
        part = multiplier * state
        correction = -transposed(coupling_ref, b, multiplier)
        reply_ref[b, 0:comps] = correction.astype(BF16)
        return tuple(totals[j] + part * state[j : j + 1] for j in range(comps))

    totals = lax.fori_loop(0, blocks, one, (jnp.zeros((comps, width), F32),) * comps)
    lane = lax.broadcasted_iota(jnp.int32, (comps, width), 1)
    rest = jnp.zeros((comps, width), F32)
    for j in range(comps):
        column = jnp.sum(totals[j], axis=1, keepdims=True)
        rest = jnp.where(lane % comps == j, column, rest)
    packed = jnp.zeros((comps, width), F32)
    for part in range(PARTS):
        rounded = rest.astype(BF16).astype(F32)
        packed = jnp.where(lane // comps == part, rounded, packed)
        rest = rest - rounded
    packed = packed.astype(BF16)
    for b in range(blocks):
        reply_ref[b, comps : 2 * comps] = packed


def at_helper(inverse, coupling, state, picked):
    blocks, comps, _, width = inverse.shape
    return pl.pallas_call(
        helper_kernel,
        out_shape=jax.ShapeDtypeStruct((blocks, 2 * comps, width), BF16),
        compiler_params=params(16),
        cost_estimate=cost(4 * inverse.size, 4 * inverse.size),
    )(inverse, coupling, state, picked)


def scatter_kernel(
    scale, helper_ref, cells_ref, back_ref, first_ref, mask_ref, perm_ref,
    second_ref, send_y_0, send_y_1, send_x, grad_ref,
    added, side_y,
):
    layers, comps, rows, cols = first_ref.shape
    chunks, _, slots = cells_ref.shape
    width = back_ref.shape[-1]
    per_chunk = slots // width
    row_number = lax.broadcasted_iota(jnp.int32, (rows, slots), 0)
    added[...] = jnp.zeros_like(added)

    def one(i, carry):
        column, y = split_cells(cells_ref[i], rows, cols)
        chosen = one_hot(column, added.shape[1], slots)
        parts = [back_ref[helper_ref[0, 0, i * per_chunk + j]].astype(F32)[:comps] for j in range(per_chunk)]
        correction = jnp.concatenate(parts, axis=1)
        at_row = row_number == y
        spread = jnp.concatenate(
            [jnp.where(at_row, correction[c : c + 1], 0.0).astype(BF16) for c in range(comps)], axis=0
        )
        added[...] += lax.dot_general(spread, chosen, (((1,), (1,)), ((), ())), preferred_element_type=F32)
        return carry

    lax.fori_loop(0, chunks, one, 0)
    for k in range(layers):
        for c in range(comps):
            second_ref[k, c] = first_ref[k, c] + added[c * rows : (c + 1) * rows, k * cols : (k + 1) * cols]
    clear = 1.0 - mask_ref[...].astype(F32)
    sends = (send_y_0, send_y_1, send_x)
    write_edges(lambda k, c: second_ref[k, c], comps, clear, perm_ref, side_y, sends)

    def add_part(b, total):
        return total + back_ref[b].astype(F32)[comps:]

    total = lax.fori_loop(0, back_ref.shape[0], add_part, jnp.zeros((comps, width), F32))
    whole = total
    for part in range(1, PARTS):
        whole += pltpu.roll(total, width - part * comps, 1)
    grad_ref[...] = (whole * scale)[:, :comps]


def scatter(first, back, helper, cells, mask, perm, scale):
    layers, comps, rows, cols = first.shape
    smem = pl.BlockSpec(memory_space=pltpu.SMEM)
    vmem = pl.BlockSpec(memory_space=pltpu.VMEM)
    return pl.pallas_call(
        functools.partial(scatter_kernel, scale),
        in_specs=[smem] + [vmem] * 5,
        out_specs=[vmem] * 5,
        out_shape=[
            jax.ShapeDtypeStruct(first.shape, F32),
            *edge_shapes(*first.shape),
            jax.ShapeDtypeStruct((comps, comps), F32),
        ],
        scratch_shapes=[pltpu.VMEM((comps * rows, layers * cols), F32), edge_scratch(layers, comps, cols)],
        compiler_params=params(24),
        cost_estimate=cost(2 * first.size * cells.size, 8 * first.size),
    )(helper, cells, back, first, mask, perm)


def shards(
    cotangent,
    permeability,
    well_mask,
    diag_block,
    flux_block,
    cell_list,
    block_count,
    helper_of,
    flash_inverse,
    flash_coupling,
    phase_state,
):
    layers, comps, rows, cols = cotangent.shape
    blocks, width = helper_of.shape[-1], flash_inverse.shape[-1]
    inverse = flash_inverse.reshape(blocks, comps, comps, width)
    coupling = flash_coupling.reshape(blocks, comps, comps, width)
    state = phase_state.reshape(blocks, comps, width)
    cells = cell_list.reshape(-1, 1, min(CHUNK, cell_list.shape[-1]))

    def to_partners(array):
        return lax.all_to_all(array, AXES, split_axis=0, concat_axis=0, tiled=True)

    *sides, field, mask, perm = opening(cotangent, well_mask, permeability)
    halos = exchange(*sides)
    first, rounded, *kept = apply_transposed(field, mask, perm, halos, diag_block, flux_block, True)
    sent = gather(rounded, cells, helper_of, block_count, comps, rows, cols, width)
    reply = at_helper(inverse, coupling, state, to_partners(sent))
    devices = lax.axis_size("gx") * lax.axis_size("gy")
    scale = -1.0 / math.sqrt(width * devices * devices)
    second, *sides, interaction_grad = scatter(
        first, to_partners(reply), helper_of, cells, mask, perm, scale
    )
    halos = exchange(*sides)
    (adjoint,) = apply_transposed(second, mask, perm, halos, *kept, False)
    return (adjoint, interaction_grad)


def solution(mesh):
    return jax.shard_map(
        shards,
        mesh=mesh,
        in_specs=(
            P(None, None, "gy", "gx"),
            P(None, "gy", "gx"),
            P("gy", "gx"),
            P(None, None, None, "gy", "gx"),
            P(None, None, None, "gy", "gx"),
            P("gy", "gx", None),
            P("gy", "gx"),
            P("gy", "gx", None),
            P("gy", "gx", None, None, None, None),
            P("gy", "gx", None, None, None, None),
            P("gy", "gx", None, None, None),
        ),
        out_specs=(P(None, None, "gy", "gx"), P()),
        check_vma=False,
    )
```

```python
import functools
import math

import jax
import jax.numpy as jnp
from jax import lax
from jax.experimental import pallas as pl
from jax.experimental.pallas import tpu as pltpu
from jax.sharding import PartitionSpec as P

F32 = jnp.float32
BF16 = jnp.bfloat16
AXES = ("gx", "gy")
MIB = 1024 * 1024
GATHER_CHUNK, SCATTER_CHUNK = 512, 1024


def params(mib):
    return pltpu.CompilerParams(vmem_limit_bytes=mib * MIB)


def cost(flops, moved):
    return pl.CostEstimate(flops=int(flops), bytes_accessed=int(moved), transcendentals=0)


def round_up(number, step):
    return -(-number // step) * step


def write_edges(field, shape, clear, perm_ref, side_y, sends):
    send_y_0, send_y_1, send_x = sends
    layers, comps, rows, cols = shape
    with_perm = perm_ref is not None
    lane = lax.broadcasted_iota(jnp.int32, (rows, cols), 1)
    pair = lane // 2
    along_x = jnp.zeros((rows, cols), F32)
    side_y[...] = jnp.zeros_like(side_y)
    for k in range(layers):
        for c in range(comps + with_perm):
            if c < comps:
                value, at = field(k, c) * clear, k * comps + c
            else:
                value, at = perm_ref[k], layers * comps + k
            side_y[0, at : at + 1, :] = value[0:1]
            side_y[1, at : at + 1, :] = value[rows - 1 : rows]
            along_x = jnp.where(pair == at, pltpu.roll(value, (2 * at + 1) % cols, 1), along_x)
    even = lax.axis_index("gy") % 2 == 0
    send_x[...] = along_x.astype(BF16)
    low, high = side_y[0].astype(BF16), side_y[1].astype(BF16)
    send_y_0[...] = jnp.where(even, high, low)
    send_y_1[...] = jnp.where(even, low, high)


def opening_kernel(
    field_hbm, mask_hbm, perm_hbm, diag_hbm, flux_hbm,
    send_y_0, send_y_1, send_x, field_ref, mask_ref, perm_ref, diag_ref, flux_ref,
    side_y, sems,
):
    early = pl.ds(0, diag_ref.shape[0])
    sources = (field_hbm, mask_hbm, perm_hbm, diag_hbm.at[early], flux_hbm.at[early])
    targets = (field_ref, mask_ref, perm_ref, diag_ref, flux_ref)
    copies = [pltpu.make_async_copy(a, b, sems.at[i]) for i, (a, b) in enumerate(zip(sources, targets))]
    for copy in copies:
        copy.start()
    for copy in copies[:3]:
        copy.wait()
    clear = 1.0 - mask_ref[...].astype(F32)
    sends = (send_y_0, send_y_1, send_x)
    write_edges(lambda k, c: field_ref[k, c], field_ref.shape, clear, perm_ref, side_y, sends)
    for copy in copies[3:]:
        copy.wait()


def edge_rows(layers, comps):
    return round_up(layers * (comps + 1), 16)


def edge_shapes(layers, comps, rows, cols):
    along_y = (edge_rows(layers, comps), cols)
    return [jax.ShapeDtypeStruct(shape, BF16) for shape in (along_y, along_y, (rows, cols))]


def edge_scratch(layers, comps, cols):
    return pltpu.VMEM((2, edge_rows(layers, comps), cols), F32)


def in_hbm(*arrays):
    return [pltpu.with_memory_space_constraint(array, pltpu.HBM) for array in arrays]


def opening(field, mask, perm, diag, flux, early):
    layers, comps, rows, cols = field.shape
    hbm = pl.BlockSpec(memory_space=pltpu.HBM)
    vmem = pl.BlockSpec(memory_space=pltpu.VMEM)
    kept = [(array.shape, array.dtype) for array in (field, mask, perm)]
    kept += [((early, *block.shape[1:]), BF16) for block in (diag, flux)]
    return pl.pallas_call(
        opening_kernel,
        in_specs=[hbm] * 5,
        out_specs=[vmem] * 8,
        out_shape=[*edge_shapes(*field.shape), *(pltpu.VMEM(*item) for item in kept)],
        scratch_shapes=[edge_scratch(layers, comps, cols), pltpu.SemaphoreType.DMA((5,))],
        compiler_params=params(16),
        cost_estimate=cost(4 * field.size, 8 * field.size),
    )(*in_hbm(field, mask, perm, diag, flux))


def exchange(send_y_0, send_y_1, send_x):
    def swaps(axis, first, second):
        count = lax.axis_size(axis)
        results = []
        for start, array in ((0, first), (1, second)):
            pairs = [(i, i + 1) for i in range(start, count - 1, 2)]
            results.append(lax.ppermute(array, axis, pairs + [(j, i) for i, j in pairs]))
        return results

    return (*swaps("gy", send_y_0, send_y_1), *swaps("gx", send_x, send_x))


TILE = 16
EARLY = 2
WEIGHTS = 7


def reciprocal(value):
    guess = pl.reciprocal(value, approx=True)
    return guess * (2.0 - value * guess)


def weight(centre, beside):
    return 2.0 * centre * beside * reciprocal(centre + beside)


def write_weights(k, weights_ref, mask_ref, perm_ref, padded, edge_x, y_0, y_1, comps):
    layers, rows, cols = perm_ref.shape
    top = 8
    lane = lax.broadcasted_iota(jnp.int32, (rows, cols), 1)
    is_first, is_last = lane == 0, lane == cols - 1
    even_y = lax.axis_index("gy") % 2 == 0
    at_low = 2 * (layers * comps + k)
    perm_low = pltpu.roll(edge_x[...], lax.rem(cols - at_low, cols), 1)
    perm_high = pltpu.roll(edge_x[...], lax.rem(2 * cols - at_low - 2, cols), 1)
    here = slice(layers * comps, layers * comps + 16)
    mine = lax.broadcasted_iota(jnp.int32, (16, cols), 0) == k
    perm_0 = jnp.sum(jnp.where(mine, y_0[here].astype(F32), 0.0), axis=0, keepdims=True)
    perm_1 = jnp.sum(jnp.where(mine, y_1[here].astype(F32), 0.0), axis=0, keepdims=True)
    centre = perm_ref[k]
    padded[top : top + rows] = centre
    padded[top - 1 : top] = jnp.where(even_y, perm_1, perm_0)
    padded[top + rows : top + rows + 1] = jnp.where(even_y, perm_0, perm_1)
    free = 1.0 - mask_ref[...].astype(F32)
    above = perm_ref[jnp.minimum(k + 1, layers - 1)]
    below = perm_ref[jnp.maximum(k - 1, 0)]
    weights_ref[k, 0] = jnp.where(k < layers - 1, weight(centre, above), 0.0) * free
    weights_ref[k, 1] = jnp.where(k > 0, weight(centre, below), 0.0) * free
    weights_ref[k, 2] = weight(centre, padded[top + 1 : top + 1 + rows])
    weights_ref[k, 3] = weight(centre, padded[top - 1 : top - 1 + rows])
    to_left = weight(centre, jnp.where(is_first, perm_low, pltpu.roll(centre, 1, 1)))
    to_right = weight(centre, jnp.where(is_last, perm_high, pltpu.roll(centre, cols - 1, 1)))
    weights_ref[k, 4] = jnp.where(is_last, 0.0, to_right)
    weights_ref[k, 5] = jnp.where(is_first, 0.0, to_left)
    weights_ref[k, 6] = jnp.where(is_first, to_left, jnp.where(is_last, to_right, 0.0))


def apply_kernel(is_first_apply, field_ref, mask_ref, y_0, y_1, x_0, x_1, early_diag, early_flux, *rest):
    if is_first_apply:
        perm_ref, diag_hbm, flux_hbm, out_ref, rounded_ref, late_diag, late_flux, weights_ref, *rest, padded_perm, sems = rest
    else:
        late_diag, late_flux, weights_ref, out_hbm, *rest, out_ref, out_sems = rest
    padded, edge_x, place, beside_edge = rest
    layers, comps, rows, cols = field_ref.shape
    early = early_diag.shape[0]
    top = 8

    def out_copy(k):
        return pltpu.make_async_copy(out_ref.at[k], out_hbm.at[k], out_sems.at[k])

    def blocks(i):
        return (
            pltpu.make_async_copy(diag_hbm.at[early + i], late_diag.at[i], sems.at[0, i]),
            pltpu.make_async_copy(flux_hbm.at[early + i], late_flux.at[i], sems.at[1, i]),
        )

    if is_first_apply:
        for i in range(layers - early):
            for copy in blocks(i):
                copy.start()

    lane = lax.broadcasted_iota(jnp.int32, (rows, cols), 1)
    number = lax.broadcasted_iota(jnp.int32, (cols, cols), 0)
    spot = lax.broadcasted_iota(jnp.int32, (cols, cols), 1)
    for r in range(comps):
        taken = ((number == 2 * r) & (spot == 0)) | ((number == 2 * r + 1) & (spot == cols - 1))
        place[:, r * cols : (r + 1) * cols] = jnp.where(taken, 1.0, 0.0).astype(BF16)
    even_x = lax.axis_index("gx") % 2 == 0
    even_y = lax.axis_index("gy") % 2 == 0
    edge_x[...] = jnp.where((lane % 2 == 0) == even_x, x_1[...].astype(F32), x_0[...].astype(F32))
    clear = 1.0 - mask_ref[...].astype(F32)

    def layer(diag_ref, flux_ref, start, i, carry):
        k = i + start
        above = jnp.minimum(k + 1, layers - 1)
        below = jnp.maximum(k - 1, 0)
        turned = pltpu.roll(edge_x[...], lax.rem(cols - 2 * comps * k, cols), 1).astype(BF16)
        beside_edge[...] = jnp.dot(turned, place[...], preferred_element_type=F32)
        odd = k % 2 == 1
        here = pl.ds(pl.multiple_of(16 * (k // 2), 16), 16)
        side_0, side_1 = y_0[here].astype(F32), y_1[here].astype(F32)
        side_0 = jnp.where(odd, side_0[comps:], side_0[:comps])
        side_1 = jnp.where(odd, side_1[comps:], side_1[:comps])
        low_y, high_y = jnp.where(even_y, side_1, side_0), jnp.where(even_y, side_0, side_1)
        for c in range(comps):
            padded[c, top : top + rows] = field_ref[k, c] * clear
            padded[c, top - 1 : top] = low_y[c : c + 1]
            padded[c, top + rows : top + rows + 1] = high_y[c : c + 1]
        if is_first_apply:
            write_weights(k, weights_ref, mask_ref, perm_ref, padded_perm, edge_x, y_0, y_1, comps)
            if start > 0:
                for copy in blocks(i):
                    copy.wait()

        for y in range(0, rows, TILE):
            here = slice(y, y + TILE)
            at = top + y
            well = mask_ref[here].astype(F32)
            weights = [weights_ref[k, j, here] for j in range(WEIGHTS)]
            total = [None] * comps
            for r in range(comps):
                own = padded[r, at : at + TILE]
                summed = (
                    weights[0] * field_ref[above, r, here]
                    + weights[1] * field_ref[below, r, here]
                    + weights[2] * padded[r, at + 1 : at + 1 + TILE]
                    + weights[3] * padded[r, at - 1 : at - 1 + TILE]
                    + weights[4] * pltpu.roll(own, cols - 1, 1)
                    + weights[5] * pltpu.roll(own, 1, 1)
                    + weights[6] * beside_edge[here, r * cols : (r + 1) * cols]
                )
                for c in range(comps):
                    term = diag_ref[i, r, c, here].astype(F32) * own - flux_ref[i, r, c, here].astype(F32) * summed
                    total[c] = term if r == 0 else total[c] + term
            for c in range(comps):
                value = total[c] + well * field_ref[k, c, here]
                out_ref[k, c, here] = value
                if is_first_apply:
                    columns = pl.ds(pl.multiple_of(k * cols, cols), cols)
                    rounded_ref[c * rows + y : c * rows + y + TILE, columns] = value.astype(BF16)
        if not is_first_apply:
            out_copy(k).start()
        return carry

    lax.fori_loop(0, early, functools.partial(layer, early_diag, early_flux, 0), 0)
    lax.fori_loop(0, layers - early, functools.partial(layer, late_diag, late_flux, early), 0)
    if not is_first_apply:
        for k in range(layers):
            out_copy(k).wait()


def apply_transposed(field, mask, halos, early_blocks, rest):
    layers, comps, rows, cols = field.shape
    vmem = pl.BlockSpec(memory_space=pltpu.VMEM)
    hbm = pl.BlockSpec(memory_space=pltpu.HBM)
    is_first_apply = rest[0].ndim == 3
    out_shape = [jax.ShapeDtypeStruct(field.shape, F32)]
    if is_first_apply:
        perm, *blocks = rest
        late = layers - early_blocks[0].shape[0]
        rest, rest_specs, out_specs = [perm, *in_hbm(*blocks)], [vmem, hbm, hbm], [vmem] * 5
        out_shape.append(jax.ShapeDtypeStruct((comps * rows, layers * cols), BF16))
        out_shape += [pltpu.VMEM((late, *block.shape[1:]), BF16) for block in blocks]
        out_shape.append(pltpu.VMEM((layers, WEIGHTS, rows, cols), F32))
        tail = [pltpu.VMEM((rows + 16, cols), F32), pltpu.SemaphoreType.DMA((2, late))]
    else:
        rest_specs, out_specs = [vmem] * 3, [hbm]
        tail = [pltpu.VMEM(field.shape, F32), pltpu.SemaphoreType.DMA((layers,))]
    size = layers * comps * comps * rows * cols
    return pl.pallas_call(
        functools.partial(apply_kernel, is_first_apply),
        in_specs=[vmem] * 8 + rest_specs,
        out_specs=out_specs,
        out_shape=out_shape,
        scratch_shapes=[
            pltpu.VMEM((comps, rows + 16, cols), F32),
            pltpu.VMEM((rows, cols), F32),
            pltpu.VMEM((cols, comps * cols), BF16),
            pltpu.VMEM((rows, comps * cols), F32),
            *tail,
        ],
        compiler_params=params(24),
        cost_estimate=cost(8 * size, 4 * size + 8 * field.size),
    )(field, mask, *halos, *early_blocks, *rest)


def split_cells(cells, rows, cols):
    layer = cells // (rows * cols)
    y = (cells // cols) % rows
    return layer * cols + cells % cols, y


def unrolled(count, together, body):
    def group(i, carry):
        for j in range(together):
            body(i * together + j, None)
        return carry

    together = math.gcd(count, together)
    lax.fori_loop(0, count // together, group, 0)


def one_hot(column, count, slots):
    number = lax.broadcasted_iota(jnp.int32, (count, slots), 0)
    return jnp.where(number == column, 1.0, 0.0).astype(BF16)


def gather_kernel(rows, cols, helper_ref, count_ref, cells_ref, rounded_ref, sent_ref):
    chunks, _, slots = cells_ref.shape
    comps, width = sent_ref.shape[1:]
    per_chunk = slots // width
    row_number = lax.broadcasted_iota(jnp.int32, (rows, slots), 0)

    def one(i, carry):
        column, y = split_cells(cells_ref[i], rows, cols)
        chosen = one_hot(column, rounded_ref.shape[1], slots)
        found = jnp.dot(rounded_ref[...], chosen, preferred_element_type=F32)
        at_row = row_number == y
        values = [
            jnp.sum(jnp.where(at_row, found[c * rows : (c + 1) * rows], 0.0), axis=0, keepdims=True)
            for c in range(comps)
        ]
        values = jnp.concatenate(values, axis=0)
        for j in range(per_chunk):
            b = i * per_chunk + j
            live = jnp.where(b < count_ref[0, 0], 1.0, 0.0)
            sent_ref[helper_ref[0, 0, b]] = (values[:, j * width : (j + 1) * width] * live).astype(BF16)
        return carry

    unrolled(chunks, 4, one)


def gather(rounded, cells, helper, count, comps, rows, cols, width):
    blocks = helper.shape[-1]
    shape = jax.ShapeDtypeStruct((blocks, comps, width), BF16)
    smem = pl.BlockSpec(memory_space=pltpu.SMEM)
    vmem = pl.BlockSpec(memory_space=pltpu.VMEM)
    return pl.pallas_call(
        functools.partial(gather_kernel, rows, cols),
        in_specs=[smem, smem, vmem, vmem],
        out_specs=vmem,
        out_shape=shape,
        compiler_params=params(16),
        cost_estimate=cost(2 * rounded.size * cells.size, 2 * rounded.size),
    )(helper, count, cells, rounded)


PARTS = 3


def helper_kernel(inverse_ref, coupling_ref, state_ref, picked_ref, reply_ref):
    blocks, comps = inverse_ref.shape[:2]
    width = inverse_ref.shape[-1]

    def transposed(block_ref, b, value):
        block = block_ref[b].astype(F32)
        total = block[0] * value[0:1]
        for r in range(1, comps):
            total += block[r] * value[r : r + 1]
        return total

    def one(b, totals):
        multiplier = transposed(inverse_ref, b, picked_ref[b].astype(F32))
        state = state_ref[b].astype(F32)
        part = multiplier * state
        correction = -transposed(coupling_ref, b, multiplier)
        reply_ref[b, 0:comps] = correction.astype(BF16)
        return tuple(totals[j] + part * state[j : j + 1] for j in range(comps))

    totals = lax.fori_loop(0, blocks, one, (jnp.zeros((comps, width), F32),) * comps)
    lane = lax.broadcasted_iota(jnp.int32, (comps, width), 1)
    rest = jnp.zeros((comps, width), F32)
    for j in range(comps):
        column = jnp.sum(totals[j], axis=1, keepdims=True)
        rest = jnp.where(lane % comps == j, column, rest)
    packed = jnp.zeros((comps, width), F32)
    for part in range(PARTS):
        rounded = rest.astype(BF16).astype(F32)
        packed = jnp.where(lane // comps == part, rounded, packed)
        rest = rest - rounded
    packed = packed.astype(BF16)
    for b in range(blocks):
        reply_ref[b, comps : 2 * comps] = packed


def at_helper(inverse, coupling, state, picked):
    blocks, comps, _, width = inverse.shape
    return pl.pallas_call(
        helper_kernel,
        out_shape=jax.ShapeDtypeStruct((blocks, 2 * comps, width), BF16),
        compiler_params=params(16),
        cost_estimate=cost(4 * inverse.size, 4 * inverse.size),
    )(inverse, coupling, state, picked)


def scatter_kernel(
    scale, helper_ref, cells_ref, back_ref, first_ref, mask_ref,
    second_ref, send_y_0, send_y_1, send_x, grad_ref,
    added, side_y,
):
    layers, comps, rows, cols = first_ref.shape
    chunks, _, slots = cells_ref.shape
    width = back_ref.shape[-1]
    per_chunk = slots // width
    row_number = lax.broadcasted_iota(jnp.int32, (rows, slots), 0)
    added[...] = jnp.zeros_like(added)

    def one(i, carry):
        column, y = split_cells(cells_ref[i], rows, cols)
        chosen = one_hot(column, added.shape[1], slots)
        parts = [back_ref[helper_ref[0, 0, i * per_chunk + j]].astype(F32)[:comps] for j in range(per_chunk)]
        correction = jnp.concatenate(parts, axis=1)
        at_row = row_number == y
        spread = jnp.concatenate(
            [jnp.where(at_row, correction[c : c + 1], 0.0).astype(BF16) for c in range(comps)], axis=0
        )
        added[...] += lax.dot_general(spread, chosen, (((1,), (1,)), ((), ())), preferred_element_type=F32)
        return carry

    unrolled(chunks, 2, one)
    for k in range(layers):
        for c in range(comps):
            second_ref[k, c] = first_ref[k, c] + added[c * rows : (c + 1) * rows, k * cols : (k + 1) * cols]
    clear = 1.0 - mask_ref[...].astype(F32)
    sends = (send_y_0, send_y_1, send_x)
    write_edges(lambda k, c: second_ref[k, c], second_ref.shape, clear, None, side_y, sends)

    def add_part(b, total):
        return total + back_ref[b].astype(F32)[comps:]

    total = lax.fori_loop(0, back_ref.shape[0], add_part, jnp.zeros((comps, width), F32))
    whole = total
    for part in range(1, PARTS):
        whole += pltpu.roll(total, width - part * comps, 1)
    grad_ref[...] = (whole * scale)[:, :comps]


def scatter(first, back, helper, cells, mask, scale):
    layers, comps, rows, cols = first.shape
    smem = pl.BlockSpec(memory_space=pltpu.SMEM)
    vmem = pl.BlockSpec(memory_space=pltpu.VMEM)
    return pl.pallas_call(
        functools.partial(scatter_kernel, scale),
        in_specs=[smem] + [vmem] * 4,
        out_specs=[vmem] * 5,
        out_shape=[
            jax.ShapeDtypeStruct(first.shape, F32),
            *edge_shapes(*first.shape),
            jax.ShapeDtypeStruct((comps, comps), F32),
        ],
        scratch_shapes=[pltpu.VMEM((comps * rows, layers * cols), F32), edge_scratch(layers, comps, cols)],
        compiler_params=params(24),
        cost_estimate=cost(2 * first.size * cells.size, 8 * first.size),
    )(helper, cells, back, first, mask)


def shards(
    cotangent,
    permeability,
    well_mask,
    diag_block,
    flux_block,
    cell_list,
    block_count,
    helper_of,
    flash_inverse,
    flash_coupling,
    phase_state,
):
    layers, comps, rows, cols = cotangent.shape
    blocks, width = helper_of.shape[-1], flash_inverse.shape[-1]
    inverse = flash_inverse.reshape(blocks, comps, comps, width)
    coupling = flash_coupling.reshape(blocks, comps, comps, width)
    state = phase_state.reshape(blocks, comps, width)

    def cells(chunk):
        return cell_list.reshape(-1, 1, min(chunk, cell_list.shape[-1]))

    def to_partners(array):
        return lax.all_to_all(array, AXES, split_axis=0, concat_axis=0, tiled=True)

    *sides, field, mask, perm, early_diag, early_flux = opening(
        cotangent, well_mask, permeability, diag_block, flux_block, min(EARLY, layers - 1)
    )
    early = (early_diag, early_flux)
    halos = exchange(*sides)
    first, rounded, *kept = apply_transposed(field, mask, halos, early, (perm, diag_block, flux_block))
    sent = gather(rounded, cells(GATHER_CHUNK), helper_of, block_count, comps, rows, cols, width)
    reply = at_helper(inverse, coupling, state, to_partners(sent))
    devices = lax.axis_size("gx") * lax.axis_size("gy")
    scale = -1.0 / math.sqrt(width * devices * devices)
    second, *sides, interaction_grad = scatter(
        first, to_partners(reply), helper_of, cells(SCATTER_CHUNK), mask, scale
    )
    halos = exchange(*sides)
    (adjoint,) = apply_transposed(second, mask, halos, early, kept)
    return (adjoint, interaction_grad)


def solution(mesh):
    return jax.shard_map(
        shards,
        mesh=mesh,
        in_specs=(
            P(None, None, "gy", "gx"),
            P(None, "gy", "gx"),
            P("gy", "gx"),
            P(None, None, None, "gy", "gx"),
            P(None, None, None, "gy", "gx"),
            P("gy", "gx", None),
            P("gy", "gx"),
            P("gy", "gx", None),
            P("gy", "gx", None, None, None, None),
            P("gy", "gx", None, None, None, None),
            P("gy", "gx", None, None, None),
        ),
        out_specs=(P(None, None, "gy", "gx"), P()),
        check_vma=False,
    )
```

```python
import functools
import math

import jax
import jax.numpy as jnp
from jax import lax
from jax.experimental import pallas as pl
from jax.experimental.pallas import tpu as pltpu
from jax.sharding import PartitionSpec as P

F32 = jnp.float32
BF16 = jnp.bfloat16
AXES = ("gx", "gy")
MIB = 1024 * 1024
GATHER_CHUNK, SCATTER_CHUNK = 512, 1024


def params(mib):
    return pltpu.CompilerParams(vmem_limit_bytes=mib * MIB)


def cost(flops, moved):
    return pl.CostEstimate(flops=int(flops), bytes_accessed=int(moved), transcendentals=0)


def round_up(number, step):
    return -(-number // step) * step


def write_edges(field_ref, mask_ref, perm_ref, masked_ref, side_y, sends):
    send_y_0, send_y_1, send_x = sends
    layers, comps, rows, cols = field_ref.shape
    with_perm = perm_ref is not None
    clear = 1.0 - mask_ref[...].astype(F32)
    lane = lax.broadcasted_iota(jnp.int32, (rows, cols), 1)
    pair = lane // 2
    along_x = jnp.zeros((rows, cols), F32)
    side_y[...] = jnp.zeros_like(side_y)
    for k in range(layers):
        for c in range(comps + with_perm):
            if c < comps:
                value, at = field_ref[k, c] * clear, k * comps + c
                masked_ref[k, c] = value
            else:
                value, at = perm_ref[k], layers * comps + k
            side_y[0, at : at + 1, :] = value[0:1]
            side_y[1, at : at + 1, :] = value[rows - 1 : rows]
            along_x = jnp.where(pair == at, pltpu.roll(value, (2 * at + 1) % cols, 1), along_x)
    even = lax.axis_index("gy") % 2 == 0
    send_x[...] = along_x.astype(BF16)
    low, high = side_y[0].astype(BF16), side_y[1].astype(BF16)
    send_y_0[...] = jnp.where(even, high, low)
    send_y_1[...] = jnp.where(even, low, high)


def opening_kernel(
    field_hbm, mask_hbm, perm_hbm, diag_hbm, flux_hbm,
    send_y_0, send_y_1, send_x, masked_ref, field_ref, mask_ref, perm_ref, diag_ref, flux_ref,
    side_y, sems,
):
    early = pl.ds(0, diag_ref.shape[0])
    sources = (field_hbm, mask_hbm, perm_hbm, diag_hbm.at[early], flux_hbm.at[early])
    targets = (field_ref, mask_ref, perm_ref, diag_ref, flux_ref)
    copies = [pltpu.make_async_copy(a, b, sems.at[i]) for i, (a, b) in enumerate(zip(sources, targets))]
    for copy in copies:
        copy.start()
    for copy in copies[:3]:
        copy.wait()
    write_edges(field_ref, mask_ref, perm_ref, masked_ref, side_y, (send_y_0, send_y_1, send_x))
    for copy in copies[3:]:
        copy.wait()


def edge_rows(layers, comps):
    return round_up(layers * (comps + 1), 16)


def edge_shapes(layers, comps, rows, cols):
    along_y = (edge_rows(layers, comps), cols)
    return [jax.ShapeDtypeStruct(shape, BF16) for shape in (along_y, along_y, (rows, cols))]


def edge_scratch(layers, comps, cols):
    return pltpu.VMEM((2, edge_rows(layers, comps), cols), F32)


def in_hbm(*arrays):
    return [pltpu.with_memory_space_constraint(array, pltpu.HBM) for array in arrays]


def opening(field, mask, perm, diag, flux, early):
    layers, comps, rows, cols = field.shape
    hbm = pl.BlockSpec(memory_space=pltpu.HBM)
    vmem = pl.BlockSpec(memory_space=pltpu.VMEM)
    kept = [(array.shape, array.dtype) for array in (field, field, mask, perm)]
    kept += [((early, *block.shape[1:]), BF16) for block in (diag, flux)]
    return pl.pallas_call(
        opening_kernel,
        in_specs=[hbm] * 5,
        out_specs=[vmem] * 9,
        out_shape=[*edge_shapes(*field.shape), *(pltpu.VMEM(*item) for item in kept)],
        scratch_shapes=[edge_scratch(layers, comps, cols), pltpu.SemaphoreType.DMA((5,))],
        compiler_params=params(16),
        cost_estimate=cost(4 * field.size, 8 * field.size),
    )(*in_hbm(field, mask, perm, diag, flux))


def exchange(send_y_0, send_y_1, send_x):
    def swaps(axis, first, second):
        count = lax.axis_size(axis)
        results = []
        for start, array in ((0, first), (1, second)):
            pairs = [(i, i + 1) for i in range(start, count - 1, 2)]
            results.append(lax.ppermute(array, axis, pairs + [(j, i) for i, j in pairs]))
        return results

    return (*swaps("gx", send_x, send_x), *swaps("gy", send_y_0, send_y_1))


TILE = 16
EARLY = 2
WEIGHTS = 7


def reciprocal(value):
    guess = pl.reciprocal(value, approx=True)
    return guess * (2.0 - value * guess)


def weight(centre, beside):
    return 2.0 * centre * beside * reciprocal(centre + beside)


def tile_weights(k, y, perm_ref, edge_x, y_rows, comps):
    layers, rows, cols = perm_ref.shape
    here = slice(y, y + TILE)
    lane = lax.broadcasted_iota(jnp.int32, (TILE, cols), 1)
    is_first, is_last = lane == 0, lane == cols - 1
    at_low = 2 * (layers * comps + k)
    perm_low = pltpu.roll(edge_x[here], lax.rem(cols - at_low, cols), 1)
    perm_high = pltpu.roll(edge_x[here], lax.rem(2 * cols - at_low - 2, cols), 1)
    centre = perm_ref[k, here]
    low_y, high_y = beside_y(perm_ref, (k,), y, y_rows)
    to_left = weight(centre, jnp.where(is_first, perm_low, pltpu.roll(centre, 1, 1)))
    to_right = weight(centre, jnp.where(is_last, perm_high, pltpu.roll(centre, cols - 1, 1)))
    return [
        jnp.where(k < layers - 1, weight(centre, perm_ref[jnp.minimum(k + 1, layers - 1), here]), 0.0),
        jnp.where(k > 0, weight(centre, perm_ref[jnp.maximum(k - 1, 0), here]), 0.0),
        weight(centre, high_y),
        weight(centre, low_y),
        jnp.where(is_last, 0.0, to_right),
        jnp.where(is_first, 0.0, to_left),
        jnp.where(is_first, to_left, jnp.where(is_last, to_right, 0.0)),
    ]


def beside_y(ref, index, y, y_rows):
    rows, cols = ref.shape[-2:]
    row = lax.broadcasted_iota(jnp.int32, (TILE, cols), 0)
    if y > 0:
        low = ref[(*index, slice(y - 1, y - 1 + TILE))]
    else:
        low = jnp.where(row == 0, y_rows[0], pltpu.roll(ref[(*index, slice(0, TILE))], 1, 0))
    if y + TILE < rows:
        high = ref[(*index, slice(y + 1, y + 1 + TILE))]
    else:
        high = jnp.where(row == TILE - 1, y_rows[1], pltpu.roll(ref[(*index, slice(y, y + TILE))], TILE - 1, 0))
    return low, high


def apply_kernel(is_first_apply, is_inner, *refs):
    names = ["field", "masked", "mask", "x_0", "x_1", "early_diag", "early_flux"]
    names += ["diag_hbm", "flux_hbm"] if is_first_apply and is_inner else ["late_diag", "late_flux"]
    names += ["perm"] if is_first_apply else ["weights"]
    names += [] if is_inner else ["y_0", "y_1", "inner"]
    names += ["out"] if is_inner or is_first_apply else ["out_hbm"]
    if is_first_apply:
        names += ["late_diag", "late_flux"] if is_inner else ["rounded"]
        names += ["weights"]
    names += ["edge_x", "place", "turned", "beside_x"]
    names += ["sems"] if is_first_apply and is_inner else []
    names += [] if is_inner or is_first_apply else ["out", "sems"]
    ref = dict(zip(names, refs, strict=True))
    field_ref, masked_ref, edge_x, place = ref["field"], ref["masked"], ref["edge_x"], ref["place"]
    layers, comps, rows, cols = field_ref.shape
    early = ref["early_diag"].shape[0]
    inner_rows = rows - 2 * TILE
    tiles = list(range(TILE, rows - TILE, TILE)) if is_inner else [0, rows - TILE]
    here_rows = len(tiles) * TILE

    def blocks(i):
        return [
            pltpu.make_async_copy(ref[f"{name}_hbm"].at[early + i], ref[f"late_{name}"].at[i], ref["sems"].at[j, i])
            for j, name in enumerate(("diag", "flux"))
        ]

    def out_copies(k):
        middle = slice(TILE, rows - TILE)
        pairs = [(ref["inner"].at[k], ref["out_hbm"].at[k, :, middle])]
        pairs += [
            (ref["out"].at[k, :, j * TILE : (j + 1) * TILE], ref["out_hbm"].at[k, :, y : y + TILE]) for j, y in enumerate(tiles)
        ]
        return [pltpu.make_async_copy(a, b, ref["sems"].at[j, k]) for j, (a, b) in enumerate(pairs)]

    if is_first_apply and is_inner:
        for i in range(layers - early):
            for copy in blocks(i):
                copy.start()

    lane = lax.broadcasted_iota(jnp.int32, (rows, cols), 1)
    number = lax.broadcasted_iota(jnp.int32, (cols, cols), 0)
    spot = lax.broadcasted_iota(jnp.int32, (cols, cols), 1)
    for r in range(comps):
        taken = ((number == 2 * r) & (spot == 0)) | ((number == 2 * r + 1) & (spot == cols - 1))
        place[:, r * cols : (r + 1) * cols] = jnp.where(taken, 1.0, 0.0).astype(BF16)
    even_x = lax.axis_index("gx") % 2 == 0
    even_y = lax.axis_index("gy") % 2 == 0
    edge_x[...] = jnp.where((lane % 2 == 0) == even_x, ref["x_1"][...].astype(F32), ref["x_0"][...].astype(F32))
    for k in range(layers):
        for j, y in enumerate(tiles):
            start = k * here_rows + j * TILE
            piece = pltpu.roll(edge_x[y : y + TILE], (cols - 2 * comps * k) % cols, 1)
            ref["turned"][start : start + TILE] = piece.astype(BF16)
    ref["beside_x"][...] = jnp.dot(ref["turned"][...], place[...], preferred_element_type=F32)

    def layer(diag_ref, flux_ref, start, i, carry):
        k = i + start
        above = jnp.minimum(k + 1, layers - 1)
        below = jnp.maximum(k - 1, 0)
        rows_y, perm_y = None, None
        if not is_inner:
            odd = k % 2 == 1
            here = pl.ds(pl.multiple_of(16 * (k // 2), 16), 16)
            sides = [ref[name][here].astype(F32) for name in ("y_0", "y_1")]
            sides = [jnp.where(odd, side[comps:], side[:comps]) for side in sides]
            rows_y = (jnp.where(even_y, sides[1], sides[0]), jnp.where(even_y, sides[0], sides[1]))
        if is_first_apply and not is_inner:
            here = slice(layers * comps, layers * comps + 16)
            mine = lax.broadcasted_iota(jnp.int32, (16, cols), 0) == k
            sides = [
                jnp.sum(jnp.where(mine, ref[name][here].astype(F32), 0.0), axis=0, keepdims=True) for name in ("y_0", "y_1")
            ]
            perm_y = (jnp.where(even_y, sides[1], sides[0]), jnp.where(even_y, sides[0], sides[1]))
        if is_first_apply and is_inner and start > 0:
            for copy in blocks(i):
                copy.wait()

        for j, y in enumerate(tiles):
            here, local = slice(y, y + TILE), slice(j * TILE, (j + 1) * TILE)
            side_rows = pl.ds(pl.multiple_of(k * here_rows + j * TILE, TILE), TILE)
            if is_first_apply:
                weights = tile_weights(k, y, ref["perm"], edge_x, perm_y, comps)
                for number, value in enumerate(weights):
                    ref["weights"][k, number, local] = value
            else:
                weights = [ref["weights"][k, number, local] for number in range(WEIGHTS)]
            total = [None] * comps
            for r in range(comps):
                own = masked_ref[k, r, here]
                low, high = beside_y(masked_ref, (k, r), y, None if is_inner else [side[r : r + 1] for side in rows_y])
                summed = (
                    weights[0] * masked_ref[above, r, here]
                    + weights[1] * masked_ref[below, r, here]
                    + weights[2] * high
                    + weights[3] * low
                    + weights[4] * pltpu.roll(own, cols - 1, 1)
                    + weights[5] * pltpu.roll(own, 1, 1)
                    + weights[6] * ref["beside_x"][side_rows, r * cols : (r + 1) * cols]
                )
                for c in range(comps):
                    term = diag_ref[i, r, c, here].astype(F32) * own - flux_ref[i, r, c, here].astype(F32) * summed
                    total[c] = term if r == 0 else total[c] + term
            well = ref["mask"][here].astype(F32)
            for c in range(comps):
                value = total[c] + well * field_ref[k, c, here]
                if is_first_apply and not is_inner:
                    ref["out"][k, c, here] = value
                    columns = pl.ds(pl.multiple_of(k * cols, cols), cols)
                    ref["rounded"][c * rows + y : c * rows + y + TILE, columns] = value.astype(BF16)
                else:
                    ref["out"][k, c, local] = value
        if is_first_apply and not is_inner:
            columns = pl.ds(pl.multiple_of(k * cols, cols), cols)
            for c in range(comps):
                value = ref["inner"][k, c]
                ref["out"][k, c, TILE : rows - TILE] = value
                ref["rounded"][c * rows + TILE : (c + 1) * rows - TILE, columns] = value.astype(BF16)
        if not is_first_apply and not is_inner:
            for copy in out_copies(k):
                copy.start()
        return carry

    lax.fori_loop(0, early, functools.partial(layer, ref["early_diag"], ref["early_flux"], 0), 0)
    lax.fori_loop(0, layers - early, functools.partial(layer, ref["late_diag"], ref["late_flux"], early), 0)
    if not is_first_apply and not is_inner:
        for k in range(layers):
            for copy in out_copies(k):
                copy.wait()


def apply_rows(is_first_apply, is_inner, field, masked, mask, halos, early, late, third, inner=None):
    layers, comps, rows, cols = field.shape
    vmem = pl.BlockSpec(memory_space=pltpu.VMEM)
    hbm = pl.BlockSpec(memory_space=pltpu.HBM)
    here_rows = rows - 2 * TILE if is_inner else 2 * TILE
    late_count = layers - early[0].shape[0]
    here = (layers, comps, here_rows, cols)
    loads = is_first_apply and is_inner
    late_spec = hbm if loads else vmem
    arrays = [field, masked, mask, *halos[:2], *early, *(in_hbm(*late) if loads else late), third]
    specs = [vmem] * 7 + [late_spec] * 2 + [vmem]
    if not is_inner:
        arrays += [*halos[2:], inner]
        specs += [vmem] * 3
    if is_inner:
        out_shape, out_specs = [pltpu.VMEM(here, F32)], [vmem]
    else:
        out_shape = [jax.ShapeDtypeStruct(field.shape, F32)]
        out_specs = [vmem if is_first_apply else hbm]
    if is_first_apply:
        if is_inner:
            out_shape += [pltpu.VMEM((late_count, *block.shape[1:]), BF16) for block in late]
        else:
            out_shape.append(jax.ShapeDtypeStruct((comps * rows, layers * cols), BF16))
        out_shape.append(pltpu.VMEM((layers, WEIGHTS, here_rows, cols), F32))
        out_specs = [vmem] * len(out_shape)
    scratch = [
        pltpu.VMEM((rows, cols), F32),
        pltpu.VMEM((cols, comps * cols), BF16),
        pltpu.VMEM((layers * here_rows, cols), BF16),
        pltpu.VMEM((layers * here_rows, comps * cols), F32),
    ]
    if loads:
        scratch.append(pltpu.SemaphoreType.DMA((2, late_count)))
    if not is_first_apply and not is_inner:
        scratch += [pltpu.VMEM(here, F32), pltpu.SemaphoreType.DMA((3, layers))]
    size = layers * comps * comps * here_rows * cols
    return pl.pallas_call(
        functools.partial(apply_kernel, is_first_apply, is_inner),
        in_specs=specs,
        out_specs=out_specs,
        out_shape=out_shape,
        scratch_shapes=scratch,
        compiler_params=params(16),
        cost_estimate=cost(8 * size, 4 * size + 8 * field.size),
    )(*arrays)


def split_cells(cells, rows, cols):
    layer = cells // (rows * cols)
    y = (cells // cols) % rows
    return layer * cols + cells % cols, y


def unrolled(count, together, body):
    def group(i, carry):
        for j in range(together):
            body(i * together + j, None)
        return carry

    together = math.gcd(count, together)
    lax.fori_loop(0, count // together, group, 0)


def one_hot(column, count, slots):
    number = lax.broadcasted_iota(jnp.int32, (count, slots), 0)
    return jnp.where(number == column, 1.0, 0.0).astype(BF16)


def gather_kernel(rows, cols, helper_ref, count_ref, cells_ref, rounded_ref, sent_ref):
    chunks, _, slots = cells_ref.shape
    comps, width = sent_ref.shape[1:]
    per_chunk = slots // width
    row_number = lax.broadcasted_iota(jnp.int32, (rows, slots), 0)

    def one(i, carry):
        column, y = split_cells(cells_ref[i], rows, cols)
        chosen = one_hot(column, rounded_ref.shape[1], slots)
        found = jnp.dot(rounded_ref[...], chosen, preferred_element_type=F32)
        at_row = row_number == y
        values = [
            jnp.sum(jnp.where(at_row, found[c * rows : (c + 1) * rows], 0.0), axis=0, keepdims=True)
            for c in range(comps)
        ]
        values = jnp.concatenate(values, axis=0)
        for j in range(per_chunk):
            b = i * per_chunk + j
            live = jnp.where(b < count_ref[0, 0], 1.0, 0.0)
            sent_ref[helper_ref[0, 0, b]] = (values[:, j * width : (j + 1) * width] * live).astype(BF16)
        return carry

    unrolled(chunks, 4, one)


def gather(rounded, cells, helper, count, comps, rows, cols, width):
    blocks = helper.shape[-1]
    shape = jax.ShapeDtypeStruct((blocks, comps, width), BF16)
    smem = pl.BlockSpec(memory_space=pltpu.SMEM)
    vmem = pl.BlockSpec(memory_space=pltpu.VMEM)
    return pl.pallas_call(
        functools.partial(gather_kernel, rows, cols),
        in_specs=[smem, smem, vmem, vmem],
        out_specs=vmem,
        out_shape=shape,
        compiler_params=params(16),
        cost_estimate=cost(2 * rounded.size * cells.size, 2 * rounded.size),
    )(helper, count, cells, rounded)


PARTS = 3


def helper_kernel(inverse_ref, coupling_ref, state_ref, picked_ref, reply_ref):
    blocks, comps = inverse_ref.shape[:2]
    width = inverse_ref.shape[-1]

    def transposed(block_ref, b, value):
        block = block_ref[b].astype(F32)
        total = block[0] * value[0:1]
        for r in range(1, comps):
            total += block[r] * value[r : r + 1]
        return total

    def one(b, totals):
        multiplier = transposed(inverse_ref, b, picked_ref[b].astype(F32))
        state = state_ref[b].astype(F32)
        part = multiplier * state
        correction = -transposed(coupling_ref, b, multiplier)
        reply_ref[b, 0:comps] = correction.astype(BF16)
        return tuple(totals[j] + part * state[j : j + 1] for j in range(comps))

    totals = lax.fori_loop(0, blocks, one, (jnp.zeros((comps, width), F32),) * comps)
    lane = lax.broadcasted_iota(jnp.int32, (comps, width), 1)
    rest = jnp.zeros((comps, width), F32)
    for j in range(comps):
        column = jnp.sum(totals[j], axis=1, keepdims=True)
        rest = jnp.where(lane % comps == j, column, rest)
    packed = jnp.zeros((comps, width), F32)
    for part in range(PARTS):
        rounded = rest.astype(BF16).astype(F32)
        packed = jnp.where(lane // comps == part, rounded, packed)
        rest = rest - rounded
    packed = packed.astype(BF16)
    for b in range(blocks):
        reply_ref[b, comps : 2 * comps] = packed


def at_helper(inverse, coupling, state, picked):
    blocks, comps, _, width = inverse.shape
    return pl.pallas_call(
        helper_kernel,
        out_shape=jax.ShapeDtypeStruct((blocks, 2 * comps, width), BF16),
        compiler_params=params(16),
        cost_estimate=cost(4 * inverse.size, 4 * inverse.size),
    )(inverse, coupling, state, picked)


def scatter_kernel(
    scale, helper_ref, cells_ref, back_ref, first_ref, mask_ref,
    second_ref, masked_ref, send_y_0, send_y_1, send_x, grad_ref,
    added, side_y,
):
    layers, comps, rows, cols = first_ref.shape
    chunks, _, slots = cells_ref.shape
    width = back_ref.shape[-1]
    per_chunk = slots // width
    row_number = lax.broadcasted_iota(jnp.int32, (rows, slots), 0)
    added[...] = jnp.zeros_like(added)

    def one(i, carry):
        column, y = split_cells(cells_ref[i], rows, cols)
        chosen = one_hot(column, added.shape[1], slots)
        parts = [back_ref[helper_ref[0, 0, i * per_chunk + j]].astype(F32)[:comps] for j in range(per_chunk)]
        correction = jnp.concatenate(parts, axis=1)
        at_row = row_number == y
        spread = jnp.concatenate(
            [jnp.where(at_row, correction[c : c + 1], 0.0).astype(BF16) for c in range(comps)], axis=0
        )
        added[...] += lax.dot_general(spread, chosen, (((1,), (1,)), ((), ())), preferred_element_type=F32)
        return carry

    unrolled(chunks, 2, one)
    for k in range(layers):
        for c in range(comps):
            second_ref[k, c] = first_ref[k, c] + added[c * rows : (c + 1) * rows, k * cols : (k + 1) * cols]
    write_edges(second_ref, mask_ref, None, masked_ref, side_y, (send_y_0, send_y_1, send_x))

    def add_part(b, total):
        return total + back_ref[b].astype(F32)[comps:]

    total = lax.fori_loop(0, back_ref.shape[0], add_part, jnp.zeros((comps, width), F32))
    whole = total
    for part in range(1, PARTS):
        whole += pltpu.roll(total, width - part * comps, 1)
    grad_ref[...] = (whole * scale)[:, :comps]


def scatter(first, back, helper, cells, mask, scale):
    layers, comps, rows, cols = first.shape
    smem = pl.BlockSpec(memory_space=pltpu.SMEM)
    vmem = pl.BlockSpec(memory_space=pltpu.VMEM)
    return pl.pallas_call(
        functools.partial(scatter_kernel, scale),
        in_specs=[smem] + [vmem] * 4,
        out_specs=[vmem] * 6,
        out_shape=[
            pltpu.VMEM(first.shape, F32),
            pltpu.VMEM(first.shape, F32),
            *edge_shapes(*first.shape),
            jax.ShapeDtypeStruct((comps, comps), F32),
        ],
        scratch_shapes=[pltpu.VMEM((comps * rows, layers * cols), F32), edge_scratch(layers, comps, cols)],
        compiler_params=params(24),
        cost_estimate=cost(2 * first.size * cells.size, 8 * first.size),
    )(helper, cells, back, first, mask)


def shards(
    cotangent,
    permeability,
    well_mask,
    diag_block,
    flux_block,
    cell_list,
    block_count,
    helper_of,
    flash_inverse,
    flash_coupling,
    phase_state,
):
    layers, comps, rows, cols = cotangent.shape
    blocks, width = helper_of.shape[-1], flash_inverse.shape[-1]
    inverse = flash_inverse.reshape(blocks, comps, comps, width)
    coupling = flash_coupling.reshape(blocks, comps, comps, width)
    state = phase_state.reshape(blocks, comps, width)

    def cells(chunk):
        return cell_list.reshape(-1, 1, min(chunk, cell_list.shape[-1]))

    def to_partners(array):
        return lax.all_to_all(array, AXES, split_axis=0, concat_axis=0, tiled=True)

    *sides, masked, field, mask, perm, early_diag, early_flux = opening(
        cotangent, well_mask, permeability, diag_block, flux_block, min(EARLY, layers - 1)
    )
    early = (early_diag, early_flux)
    halos = exchange(*sides)
    inner, *late, inner_weights = apply_rows(
        True, True, field, masked, mask, halos, early, (diag_block, flux_block), perm
    )
    first, rounded, outer_weights = apply_rows(True, False, field, masked, mask, halos, early, late, perm, inner)
    sent = gather(rounded, cells(GATHER_CHUNK), helper_of, block_count, comps, rows, cols, width)
    reply = at_helper(inverse, coupling, state, to_partners(sent))
    devices = lax.axis_size("gx") * lax.axis_size("gy")
    scale = -1.0 / math.sqrt(width * devices * devices)
    second, masked, *sides, interaction_grad = scatter(
        first, to_partners(reply), helper_of, cells(SCATTER_CHUNK), mask, scale
    )
    halos = exchange(*sides)
    (inner,) = apply_rows(False, True, second, masked, mask, halos, early, late, inner_weights)
    (adjoint,) = apply_rows(False, False, second, masked, mask, halos, early, late, outer_weights, inner)
    return (adjoint, interaction_grad)


def solution(mesh):
    return jax.shard_map(
        shards,
        mesh=mesh,
        in_specs=(
            P(None, None, "gy", "gx"),
            P(None, "gy", "gx"),
            P("gy", "gx"),
            P(None, None, None, "gy", "gx"),
            P(None, None, None, "gy", "gx"),
            P("gy", "gx", None),
            P("gy", "gx"),
            P("gy", "gx", None),
            P("gy", "gx", None, None, None, None),
            P("gy", "gx", None, None, None, None),
            P("gy", "gx", None, None, None),
        ),
        out_specs=(P(None, None, "gy", "gx"), P()),
        check_vma=False,
    )
```

```python
import functools
import math

import jax
import jax.numpy as jnp
from jax import lax
from jax.experimental import pallas as pl
from jax.experimental.pallas import tpu as pltpu
from jax.sharding import PartitionSpec as P

F32 = jnp.float32
BF16 = jnp.bfloat16
AXES = ("gx", "gy")
MIB = 1024 * 1024
GATHER_CHUNK, SCATTER_CHUNK = 512, 1024


def params(mib):
    return pltpu.CompilerParams(vmem_limit_bytes=mib * MIB)


def cost(flops, moved):
    return pl.CostEstimate(flops=int(flops), bytes_accessed=int(moved), transcendentals=0)


def round_up(number, step):
    return -(-number // step) * step


def write_edges(field_ref, mask_ref, perm_ref, masked_ref, side_y, sends):
    send_y, send_x = sends
    layers, comps, rows, cols = field_ref.shape
    with_perm = perm_ref is not None
    clear = 1.0 - mask_ref[...].astype(F32)
    lane = lax.broadcasted_iota(jnp.int32, (rows, cols), 1)
    pair = lane // 2
    along_x = jnp.zeros((rows, cols), F32)
    side_y[...] = jnp.zeros_like(side_y)
    for k in range(layers):
        for c in range(comps + with_perm):
            if c < comps:
                value, at = field_ref[k, c] * clear, k * comps + c
                masked_ref[k, c] = value
            else:
                value, at = perm_ref[k], layers * comps + k
            side_y[0, at : at + 1, :] = value[0:1]
            side_y[1, at : at + 1, :] = value[rows - 1 : rows]
            along_x = jnp.where(pair == at, pltpu.roll(value, (2 * at + 1) % cols, 1), along_x)
    even = lax.axis_index("gy") % 2 == 0
    send_x[...] = along_x.astype(BF16)
    low, high = side_y[0].astype(BF16), side_y[1].astype(BF16)
    send_y[0] = jnp.where(even, high, low)
    send_y[1] = jnp.where(even, low, high)


def opening_kernel(
    field_hbm, mask_hbm, perm_hbm, diag_hbm, flux_hbm,
    send_y, send_x, masked_ref, field_ref, mask_ref, perm_ref, diag_ref, flux_ref,
    side_y, sems,
):
    early = pl.ds(0, diag_ref.shape[0])
    sources = (field_hbm, mask_hbm, perm_hbm, diag_hbm.at[early], flux_hbm.at[early])
    targets = (field_ref, mask_ref, perm_ref, diag_ref, flux_ref)
    copies = [pltpu.make_async_copy(a, b, sems.at[i]) for i, (a, b) in enumerate(zip(sources, targets))]
    for copy in copies:
        copy.start()
    for copy in copies[:3]:
        copy.wait()
    write_edges(field_ref, mask_ref, perm_ref, masked_ref, side_y, (send_y, send_x))
    for copy in copies[3:]:
        copy.wait()


def edge_rows(layers, comps):
    return round_up(layers * (comps + 1), 16)


def edge_shapes(layers, comps, rows, cols):
    along_y = (2, edge_rows(layers, comps), cols)
    return [jax.ShapeDtypeStruct(shape, BF16) for shape in (along_y, (rows, cols))]


def edge_scratch(layers, comps, cols):
    return pltpu.VMEM((2, edge_rows(layers, comps), cols), F32)


def in_hbm(*arrays):
    return [pltpu.with_memory_space_constraint(array, pltpu.HBM) for array in arrays]


def opening(field, mask, perm, diag, flux, early):
    layers, comps, rows, cols = field.shape
    hbm = pl.BlockSpec(memory_space=pltpu.HBM)
    vmem = pl.BlockSpec(memory_space=pltpu.VMEM)
    kept = [(array.shape, array.dtype) for array in (field, field, mask, perm)]
    kept += [((early, *block.shape[1:]), BF16) for block in (diag, flux)]
    return pl.pallas_call(
        opening_kernel,
        in_specs=[hbm] * 5,
        out_specs=[vmem] * 8,
        out_shape=[*edge_shapes(*field.shape), *(pltpu.VMEM(*item) for item in kept)],
        scratch_shapes=[edge_scratch(layers, comps, cols), pltpu.SemaphoreType.DMA((5,))],
        compiler_params=params(16),
        cost_estimate=cost(4 * field.size, 8 * field.size),
    )(*in_hbm(field, mask, perm, diag, flux))


def exchange(send_y, send_x):
    def swap(array, axis):
        pairs = [(i, i + 1) for i in range(0, lax.axis_size(axis) - 1, 2)]
        return lax.ppermute(array, axis, pairs + [(j, i) for i, j in pairs])

    def pass_on(array, axis):
        count = lax.axis_size(axis)
        pairs = [(i, i + 2 if i % 2 == 0 else i - 2) for i in range(count)]
        return lax.ppermute(array, axis, [(i, j) for i, j in pairs if 0 <= j < count])

    x, y = swap(send_x, "gx"), swap(send_y, "gy")
    return x, pass_on(x, "gx"), y, pass_on(y, "gy")


TILE = 16
EARLY = 2
WEIGHTS = 7


def reciprocal(value):
    guess = pl.reciprocal(value, approx=True)
    return guess * (2.0 - value * guess)


def weight(centre, beside):
    return 2.0 * centre * beside * reciprocal(centre + beside)


def tile_weights(k, y, perm_ref, edge_x, y_rows, comps):
    layers, rows, cols = perm_ref.shape
    here = slice(y, y + TILE)
    lane = lax.broadcasted_iota(jnp.int32, (TILE, cols), 1)
    is_first, is_last = lane == 0, lane == cols - 1
    at_low = 2 * (layers * comps + k)
    perm_low = pltpu.roll(edge_x[here], lax.rem(cols - at_low, cols), 1)
    perm_high = pltpu.roll(edge_x[here], lax.rem(2 * cols - at_low - 2, cols), 1)
    centre = perm_ref[k, here]
    low_y, high_y = beside_y(perm_ref, (k,), y, y_rows)
    to_left = weight(centre, jnp.where(is_first, perm_low, pltpu.roll(centre, 1, 1)))
    to_right = weight(centre, jnp.where(is_last, perm_high, pltpu.roll(centre, cols - 1, 1)))
    return [
        jnp.where(k < layers - 1, weight(centre, perm_ref[jnp.minimum(k + 1, layers - 1), here]), 0.0),
        jnp.where(k > 0, weight(centre, perm_ref[jnp.maximum(k - 1, 0), here]), 0.0),
        weight(centre, high_y),
        weight(centre, low_y),
        jnp.where(is_last, 0.0, to_right),
        jnp.where(is_first, 0.0, to_left),
        jnp.where(is_first, to_left, jnp.where(is_last, to_right, 0.0)),
    ]


def beside_y(ref, index, y, y_rows):
    rows, cols = ref.shape[-2:]
    row = lax.broadcasted_iota(jnp.int32, (TILE, cols), 0)
    if y > 0:
        low = ref[(*index, slice(y - 1, y - 1 + TILE))]
    else:
        low = jnp.where(row == 0, y_rows[0], pltpu.roll(ref[(*index, slice(0, TILE))], 1, 0))
    if y + TILE < rows:
        high = ref[(*index, slice(y + 1, y + 1 + TILE))]
    else:
        high = jnp.where(row == TILE - 1, y_rows[1], pltpu.roll(ref[(*index, slice(y, y + TILE))], TILE - 1, 0))
    return low, high


def apply_kernel(is_first_apply, is_inner, *refs):
    names = ["field", "masked", "mask", "x_0", "x_1", "early_diag", "early_flux"]
    names += ["diag_hbm", "flux_hbm"] if is_first_apply and is_inner else ["late_diag", "late_flux"]
    names += ["perm"] if is_first_apply else ["weights"]
    names += [] if is_inner else ["y_0", "y_1", "inner"]
    names += ["out"] if is_inner or is_first_apply else ["out_hbm"]
    if is_first_apply:
        names += ["late_diag", "late_flux"] if is_inner else ["rounded"]
        names += ["weights"]
    names += ["edge_x", "place", "turned", "beside_x"]
    names += ["sems"] if is_first_apply and is_inner else []
    names += [] if is_inner or is_first_apply else ["out", "sems"]
    ref = dict(zip(names, refs, strict=True))
    field_ref, masked_ref, edge_x, place = ref["field"], ref["masked"], ref["edge_x"], ref["place"]
    layers, comps, rows, cols = field_ref.shape
    early = ref["early_diag"].shape[0]
    inner_rows = rows - 2 * TILE
    tiles = list(range(TILE, rows - TILE, TILE)) if is_inner else [0, rows - TILE]
    here_rows = len(tiles) * TILE

    def blocks(i):
        return [
            pltpu.make_async_copy(ref[f"{name}_hbm"].at[early + i], ref[f"late_{name}"].at[i], ref["sems"].at[j, i])
            for j, name in enumerate(("diag", "flux"))
        ]

    def out_copies(k):
        middle = slice(TILE, rows - TILE)
        pairs = [(ref["inner"].at[k], ref["out_hbm"].at[k, :, middle])]
        pairs += [
            (ref["out"].at[k, :, j * TILE : (j + 1) * TILE], ref["out_hbm"].at[k, :, y : y + TILE]) for j, y in enumerate(tiles)
        ]
        return [pltpu.make_async_copy(a, b, ref["sems"].at[j, k]) for j, (a, b) in enumerate(pairs)]

    if is_first_apply and is_inner:
        for i in range(layers - early):
            for copy in blocks(i):
                copy.start()

    lane = lax.broadcasted_iota(jnp.int32, (rows, cols), 1)
    number = lax.broadcasted_iota(jnp.int32, (cols, cols), 0)
    spot = lax.broadcasted_iota(jnp.int32, (cols, cols), 1)
    for r in range(comps):
        taken = ((number == 2 * r) & (spot == 0)) | ((number == 2 * r + 1) & (spot == cols - 1))
        place[:, r * cols : (r + 1) * cols] = jnp.where(taken, 1.0, 0.0).astype(BF16)
    even_x = lax.axis_index("gx") % 2 == 0
    even_y = lax.axis_index("gy") % 2 == 0
    edge_x[...] = jnp.where((lane % 2 == 0) == even_x, ref["x_1"][...].astype(F32), ref["x_0"][...].astype(F32))
    for k in range(layers):
        for j, y in enumerate(tiles):
            start = k * here_rows + j * TILE
            piece = pltpu.roll(edge_x[y : y + TILE], (cols - 2 * comps * k) % cols, 1)
            ref["turned"][start : start + TILE] = piece.astype(BF16)
    ref["beside_x"][...] = jnp.dot(ref["turned"][...], place[...], preferred_element_type=F32)

    def layer(diag_ref, flux_ref, start, i, carry):
        k = i + start
        above = jnp.minimum(k + 1, layers - 1)
        below = jnp.maximum(k - 1, 0)
        rows_y, perm_y = None, None
        if not is_inner:
            odd = k % 2 == 1
            here = pl.ds(pl.multiple_of(16 * (k // 2), 16), 16)
            sides = [ref[f"y_{n}"][n, here].astype(F32) for n in range(2)]
            sides = [jnp.where(odd, side[comps:], side[:comps]) for side in sides]
            rows_y = (jnp.where(even_y, sides[1], sides[0]), jnp.where(even_y, sides[0], sides[1]))
        if is_first_apply and not is_inner:
            here = slice(layers * comps, layers * comps + 16)
            mine = lax.broadcasted_iota(jnp.int32, (16, cols), 0) == k
            sides = [
                jnp.sum(jnp.where(mine, ref[f"y_{n}"][n, here].astype(F32), 0.0), axis=0, keepdims=True) for n in range(2)
            ]
            perm_y = (jnp.where(even_y, sides[1], sides[0]), jnp.where(even_y, sides[0], sides[1]))
        if is_first_apply and is_inner and start > 0:
            for copy in blocks(i):
                copy.wait()

        for j, y in enumerate(tiles):
            here, local = slice(y, y + TILE), slice(j * TILE, (j + 1) * TILE)
            side_rows = pl.ds(pl.multiple_of(k * here_rows + j * TILE, TILE), TILE)
            if is_first_apply:
                weights = tile_weights(k, y, ref["perm"], edge_x, perm_y, comps)
                for number, value in enumerate(weights):
                    ref["weights"][k, number, local] = value
            else:
                weights = [ref["weights"][k, number, local] for number in range(WEIGHTS)]
            total = [None] * comps
            for r in range(comps):
                own = masked_ref[k, r, here]
                low, high = beside_y(masked_ref, (k, r), y, None if is_inner else [side[r : r + 1] for side in rows_y])
                summed = (
                    weights[0] * masked_ref[above, r, here]
                    + weights[1] * masked_ref[below, r, here]
                    + weights[2] * high
                    + weights[3] * low
                    + weights[4] * pltpu.roll(own, cols - 1, 1)
                    + weights[5] * pltpu.roll(own, 1, 1)
                    + weights[6] * ref["beside_x"][side_rows, r * cols : (r + 1) * cols]
                )
                for c in range(comps):
                    term = diag_ref[i, r, c, here].astype(F32) * own - flux_ref[i, r, c, here].astype(F32) * summed
                    total[c] = term if r == 0 else total[c] + term
            well = ref["mask"][here].astype(F32)
            for c in range(comps):
                value = total[c] + well * field_ref[k, c, here]
                if is_first_apply and not is_inner:
                    ref["out"][k, c, here] = value
                    columns = pl.ds(pl.multiple_of(k * cols, cols), cols)
                    ref["rounded"][c * rows + y : c * rows + y + TILE, columns] = value.astype(BF16)
                else:
                    ref["out"][k, c, local] = value
        if is_first_apply and not is_inner:
            columns = pl.ds(pl.multiple_of(k * cols, cols), cols)
            for c in range(comps):
                value = ref["inner"][k, c]
                ref["out"][k, c, TILE : rows - TILE] = value
                ref["rounded"][c * rows + TILE : (c + 1) * rows - TILE, columns] = value.astype(BF16)
        if not is_first_apply and not is_inner:
            for copy in out_copies(k):
                copy.start()
        return carry

    lax.fori_loop(0, early, functools.partial(layer, ref["early_diag"], ref["early_flux"], 0), 0)
    lax.fori_loop(0, layers - early, functools.partial(layer, ref["late_diag"], ref["late_flux"], early), 0)
    if not is_first_apply and not is_inner:
        for k in range(layers):
            for copy in out_copies(k):
                copy.wait()


def apply_rows(is_first_apply, is_inner, field, masked, mask, halos, early, late, third, inner=None):
    layers, comps, rows, cols = field.shape
    vmem = pl.BlockSpec(memory_space=pltpu.VMEM)
    hbm = pl.BlockSpec(memory_space=pltpu.HBM)
    here_rows = rows - 2 * TILE if is_inner else 2 * TILE
    late_count = layers - early[0].shape[0]
    here = (layers, comps, here_rows, cols)
    loads = is_first_apply and is_inner
    late_spec = hbm if loads else vmem
    arrays = [field, masked, mask, *halos[:2], *early, *(in_hbm(*late) if loads else late), third]
    specs = [vmem] * 7 + [late_spec] * 2 + [vmem]
    if not is_inner:
        arrays += [*halos[2:], inner]
        specs += [vmem] * 3
    if is_inner:
        out_shape, out_specs = [pltpu.VMEM(here, F32)], [vmem]
    else:
        out_shape = [jax.ShapeDtypeStruct(field.shape, F32)]
        out_specs = [vmem if is_first_apply else hbm]
    if is_first_apply:
        if is_inner:
            out_shape += [pltpu.VMEM((late_count, *block.shape[1:]), BF16) for block in late]
        else:
            out_shape.append(jax.ShapeDtypeStruct((comps * rows, layers * cols), BF16))
        out_shape.append(pltpu.VMEM((layers, WEIGHTS, here_rows, cols), F32))
        out_specs = [vmem] * len(out_shape)
    scratch = [
        pltpu.VMEM((rows, cols), F32),
        pltpu.VMEM((cols, comps * cols), BF16),
        pltpu.VMEM((layers * here_rows, cols), BF16),
        pltpu.VMEM((layers * here_rows, comps * cols), F32),
    ]
    if loads:
        scratch.append(pltpu.SemaphoreType.DMA((2, late_count)))
    if not is_first_apply and not is_inner:
        scratch += [pltpu.VMEM(here, F32), pltpu.SemaphoreType.DMA((3, layers))]
    size = layers * comps * comps * here_rows * cols
    return pl.pallas_call(
        functools.partial(apply_kernel, is_first_apply, is_inner),
        in_specs=specs,
        out_specs=out_specs,
        out_shape=out_shape,
        scratch_shapes=scratch,
        compiler_params=params(16),
        cost_estimate=cost(8 * size, 4 * size + 8 * field.size),
    )(*arrays)


def split_cells(cells, rows, cols):
    layer = cells // (rows * cols)
    y = (cells // cols) % rows
    return layer * cols + cells % cols, y


def unrolled(count, together, body):
    def group(i, carry):
        for j in range(together):
            body(i * together + j, None)
        return carry

    together = math.gcd(count, together)
    lax.fori_loop(0, count // together, group, 0)


def one_hot(column, count, slots):
    number = lax.broadcasted_iota(jnp.int32, (count, slots), 0)
    return jnp.where(number == column, 1.0, 0.0).astype(BF16)


def gather_kernel(rows, cols, helper_ref, count_ref, cells_ref, rounded_ref, sent_ref):
    chunks, _, slots = cells_ref.shape
    comps, width = sent_ref.shape[1:]
    per_chunk = slots // width
    row_number = lax.broadcasted_iota(jnp.int32, (rows, slots), 0)

    def one(i, carry):
        column, y = split_cells(cells_ref[i], rows, cols)
        chosen = one_hot(column, rounded_ref.shape[1], slots)
        found = jnp.dot(rounded_ref[...], chosen, preferred_element_type=F32)
        at_row = row_number == y
        values = [
            jnp.sum(jnp.where(at_row, found[c * rows : (c + 1) * rows], 0.0), axis=0, keepdims=True)
            for c in range(comps)
        ]
        values = jnp.concatenate(values, axis=0)
        for j in range(per_chunk):
            b = i * per_chunk + j
            live = jnp.where(b < count_ref[0, 0], 1.0, 0.0)
            sent_ref[helper_ref[0, 0, b]] = (values[:, j * width : (j + 1) * width] * live).astype(BF16)
        return carry

    unrolled(chunks, 4, one)


def gather(rounded, cells, helper, count, comps, rows, cols, width):
    blocks = helper.shape[-1]
    shape = jax.ShapeDtypeStruct((blocks, comps, width), BF16)
    smem = pl.BlockSpec(memory_space=pltpu.SMEM)
    vmem = pl.BlockSpec(memory_space=pltpu.VMEM)
    return pl.pallas_call(
        functools.partial(gather_kernel, rows, cols),
        in_specs=[smem, smem, vmem, vmem],
        out_specs=vmem,
        out_shape=shape,
        compiler_params=params(16),
        cost_estimate=cost(2 * rounded.size * cells.size, 2 * rounded.size),
    )(helper, count, cells, rounded)


PARTS = 3


def helper_kernel(inverse_ref, coupling_ref, state_ref, picked_ref, reply_ref):
    blocks, comps = inverse_ref.shape[:2]
    width = inverse_ref.shape[-1]

    def transposed(block_ref, b, value):
        block = block_ref[b].astype(F32)
        total = block[0] * value[0:1]
        for r in range(1, comps):
            total += block[r] * value[r : r + 1]
        return total

    def one(b, totals):
        multiplier = transposed(inverse_ref, b, picked_ref[b].astype(F32))
        state = state_ref[b].astype(F32)
        part = multiplier * state
        correction = -transposed(coupling_ref, b, multiplier)
        reply_ref[b, 0:comps] = correction.astype(BF16)
        return tuple(totals[j] + part * state[j : j + 1] for j in range(comps))

    totals = lax.fori_loop(0, blocks, one, (jnp.zeros((comps, width), F32),) * comps)
    lane = lax.broadcasted_iota(jnp.int32, (comps, width), 1)
    rest = jnp.zeros((comps, width), F32)
    for j in range(comps):
        column = jnp.sum(totals[j], axis=1, keepdims=True)
        rest = jnp.where(lane % comps == j, column, rest)
    packed = jnp.zeros((comps, width), F32)
    for part in range(PARTS):
        rounded = rest.astype(BF16).astype(F32)
        packed = jnp.where(lane // comps == part, rounded, packed)
        rest = rest - rounded
    packed = packed.astype(BF16)
    for b in range(blocks):
        reply_ref[b, comps : 2 * comps] = packed


def at_helper(inverse, coupling, state, picked):
    blocks, comps, _, width = inverse.shape
    return pl.pallas_call(
        helper_kernel,
        out_shape=jax.ShapeDtypeStruct((blocks, 2 * comps, width), BF16),
        compiler_params=params(16),
        cost_estimate=cost(4 * inverse.size, 4 * inverse.size),
    )(inverse, coupling, state, picked)


def scatter_kernel(
    scale, helper_ref, cells_ref, back_ref, first_ref, mask_ref,
    second_ref, masked_ref, send_y, send_x, grad_ref,
    added, side_y,
):
    layers, comps, rows, cols = first_ref.shape
    chunks, _, slots = cells_ref.shape
    width = back_ref.shape[-1]
    per_chunk = slots // width
    row_number = lax.broadcasted_iota(jnp.int32, (rows, slots), 0)
    added[...] = jnp.zeros_like(added)

    def one(i, carry):
        column, y = split_cells(cells_ref[i], rows, cols)
        chosen = one_hot(column, added.shape[1], slots)
        parts = [back_ref[helper_ref[0, 0, i * per_chunk + j]].astype(F32)[:comps] for j in range(per_chunk)]
        correction = jnp.concatenate(parts, axis=1)
        at_row = row_number == y
        spread = jnp.concatenate(
            [jnp.where(at_row, correction[c : c + 1], 0.0).astype(BF16) for c in range(comps)], axis=0
        )
        added[...] += lax.dot_general(spread, chosen, (((1,), (1,)), ((), ())), preferred_element_type=F32)
        return carry

    unrolled(chunks, 2, one)
    for k in range(layers):
        for c in range(comps):
            second_ref[k, c] = first_ref[k, c] + added[c * rows : (c + 1) * rows, k * cols : (k + 1) * cols]
    write_edges(second_ref, mask_ref, None, masked_ref, side_y, (send_y, send_x))

    def add_part(b, total):
        return total + back_ref[b].astype(F32)[comps:]

    total = lax.fori_loop(0, back_ref.shape[0], add_part, jnp.zeros((comps, width), F32))
    whole = total
    for part in range(1, PARTS):
        whole += pltpu.roll(total, width - part * comps, 1)
    grad_ref[...] = (whole * scale)[:, :comps]


def scatter(first, back, helper, cells, mask, scale):
    layers, comps, rows, cols = first.shape
    smem = pl.BlockSpec(memory_space=pltpu.SMEM)
    vmem = pl.BlockSpec(memory_space=pltpu.VMEM)
    return pl.pallas_call(
        functools.partial(scatter_kernel, scale),
        in_specs=[smem] + [vmem] * 4,
        out_specs=[vmem] * 5,
        out_shape=[
            pltpu.VMEM(first.shape, F32),
            pltpu.VMEM(first.shape, F32),
            *edge_shapes(*first.shape),
            jax.ShapeDtypeStruct((comps, comps), F32),
        ],
        scratch_shapes=[pltpu.VMEM((comps * rows, layers * cols), F32), edge_scratch(layers, comps, cols)],
        compiler_params=params(24),
        cost_estimate=cost(2 * first.size * cells.size, 8 * first.size),
    )(helper, cells, back, first, mask)


def shards(
    cotangent,
    permeability,
    well_mask,
    diag_block,
    flux_block,
    cell_list,
    block_count,
    helper_of,
    flash_inverse,
    flash_coupling,
    phase_state,
):
    layers, comps, rows, cols = cotangent.shape
    blocks, width = helper_of.shape[-1], flash_inverse.shape[-1]
    inverse = flash_inverse.reshape(blocks, comps, comps, width)
    coupling = flash_coupling.reshape(blocks, comps, comps, width)
    state = phase_state.reshape(blocks, comps, width)

    def cells(chunk):
        return cell_list.reshape(-1, 1, min(chunk, cell_list.shape[-1]))

    def to_partners(array):
        return lax.all_to_all(array, AXES, split_axis=0, concat_axis=0, tiled=True)

    *sides, masked, field, mask, perm, early_diag, early_flux = opening(
        cotangent, well_mask, permeability, diag_block, flux_block, min(EARLY, layers - 1)
    )
    early = (early_diag, early_flux)
    halos = exchange(*sides)
    inner, *late, inner_weights = apply_rows(
        True, True, field, masked, mask, halos, early, (diag_block, flux_block), perm
    )
    first, rounded, outer_weights = apply_rows(True, False, field, masked, mask, halos, early, late, perm, inner)
    sent = gather(rounded, cells(GATHER_CHUNK), helper_of, block_count, comps, rows, cols, width)
    reply = at_helper(inverse, coupling, state, to_partners(sent))
    devices = lax.axis_size("gx") * lax.axis_size("gy")
    scale = -1.0 / math.sqrt(width * devices * devices)
    second, masked, *sides, interaction_grad = scatter(
        first, to_partners(reply), helper_of, cells(SCATTER_CHUNK), mask, scale
    )
    halos = exchange(*sides)
    (inner,) = apply_rows(False, True, second, masked, mask, halos, early, late, inner_weights)
    (adjoint,) = apply_rows(False, False, second, masked, mask, halos, early, late, outer_weights, inner)
    return (adjoint, interaction_grad)


def solution(mesh):
    return jax.shard_map(
        shards,
        mesh=mesh,
        in_specs=(
            P(None, None, "gy", "gx"),
            P(None, "gy", "gx"),
            P("gy", "gx"),
            P(None, None, None, "gy", "gx"),
            P(None, None, None, "gy", "gx"),
            P("gy", "gx", None),
            P("gy", "gx"),
            P("gy", "gx", None),
            P("gy", "gx", None, None, None, None),
            P("gy", "gx", None, None, None, None),
            P("gy", "gx", None, None, None),
        ),
        out_specs=(P(None, None, "gy", "gx"), P()),
        check_vma=False,
    )
```

```python
import functools
import math

import jax
import jax.numpy as jnp
from jax import lax
from jax.experimental import pallas as pl
from jax.experimental.pallas import tpu as pltpu
from jax.sharding import PartitionSpec as P

F32 = jnp.float32
BF16 = jnp.bfloat16
AXES = ("gx", "gy")
MIB = 1024 * 1024
GATHER_CHUNK, SCATTER_CHUNK = 512, 2048
KEPT_BYTES = 8 * MIB


def params(mib):
    return pltpu.CompilerParams(vmem_limit_bytes=mib * MIB)


def cost(flops, moved):
    return pl.CostEstimate(flops=int(flops), bytes_accessed=int(moved), transcendentals=0)


def round_up(number, step):
    return -(-number // step) * step


def write_edges(field_ref, mask_ref, perm_ref, masked_ref, side_y, sends):
    send_y_0, send_y_1, send_x = sends
    layers, comps, rows, cols = field_ref.shape
    with_perm = perm_ref is not None
    clear = 1.0 - mask_ref[...].astype(F32)
    lane = lax.broadcasted_iota(jnp.int32, (rows, cols), 1)
    pair = lane // 2
    along_x = jnp.zeros((rows, cols), F32)
    side_y[...] = jnp.zeros_like(side_y)
    for k in range(layers):
        for c in range(comps + with_perm):
            if c < comps:
                value, at = field_ref[k, c] * clear, k * comps + c
                masked_ref[k, c] = value
            else:
                value, at = perm_ref[k], layers * comps + k
            side_y[0, at : at + 1, :] = value[0:1]
            side_y[1, at : at + 1, :] = value[rows - 1 : rows]
            along_x = jnp.where(pair == at, pltpu.roll(value, (2 * at + 1) % cols, 1), along_x)
    even = lax.axis_index("gy") % 2 == 0
    send_x[...] = along_x.astype(BF16)
    low, high = side_y[0].astype(BF16), side_y[1].astype(BF16)
    send_y_0[...] = jnp.where(even, high, low)
    send_y_1[...] = jnp.where(even, low, high)


def write_place(place_ref):
    cols, width = place_ref.shape
    number = lax.broadcasted_iota(jnp.int32, (cols, cols), 0)
    spot = lax.broadcasted_iota(jnp.int32, (cols, cols), 1)
    for r in range(width // cols):
        taken = ((number == 2 * r) & (spot == 0)) | ((number == 2 * r + 1) & (spot == cols - 1))
        place_ref[:, r * cols : (r + 1) * cols] = jnp.where(taken, 1.0, 0.0).astype(BF16)


def opening_kernel(
    field_hbm, mask_hbm, perm_hbm, diag_hbm, flux_hbm,
    send_y_0, send_y_1, send_x, masked_ref, field_ref, mask_ref, perm_ref, diag_ref, flux_ref, place_ref,
    side_y, sems,
):
    early = pl.ds(0, diag_ref.shape[0])
    sources = (field_hbm, mask_hbm, perm_hbm, diag_hbm.at[early], flux_hbm.at[early])
    targets = (field_ref, mask_ref, perm_ref, diag_ref, flux_ref)
    copies = [pltpu.make_async_copy(a, b, sems.at[i]) for i, (a, b) in enumerate(zip(sources, targets))]
    for copy in copies:
        copy.start()
    write_place(place_ref)
    for copy in copies[:3]:
        copy.wait()
    write_edges(field_ref, mask_ref, perm_ref, masked_ref, side_y, (send_y_0, send_y_1, send_x))
    for copy in copies[3:]:
        copy.wait()


def edge_rows(layers, comps):
    return round_up(layers * (comps + 1), 16)


def edge_shapes(layers, comps, rows, cols):
    along_y = (edge_rows(layers, comps), cols)
    return [jax.ShapeDtypeStruct(shape, BF16) for shape in (along_y, along_y, (rows, cols))]


def edge_scratch(layers, comps, cols):
    return pltpu.VMEM((2, edge_rows(layers, comps), cols), F32)


def in_hbm(*arrays):
    return [pltpu.with_memory_space_constraint(array, pltpu.HBM) for array in arrays]


def opening(field, mask, perm, diag, flux, early):
    layers, comps, rows, cols = field.shape
    hbm = pl.BlockSpec(memory_space=pltpu.HBM)
    vmem = pl.BlockSpec(memory_space=pltpu.VMEM)
    kept = [(array.shape, array.dtype) for array in (field, field, mask, perm)]
    kept += [((early, *block.shape[1:]), BF16) for block in (diag, flux)]
    kept.append(((cols, comps * cols), BF16))
    return pl.pallas_call(
        opening_kernel,
        in_specs=[hbm] * 5,
        out_specs=[vmem] * 10,
        out_shape=[*edge_shapes(*field.shape), *(pltpu.VMEM(*item) for item in kept)],
        scratch_shapes=[edge_scratch(layers, comps, cols), pltpu.SemaphoreType.DMA((5,))],
        compiler_params=params(16),
        cost_estimate=cost(4 * field.size, 8 * field.size),
    )(*in_hbm(field, mask, perm, diag, flux))


def exchange(send_y_0, send_y_1, send_x):
    def swaps(axis, first, second):
        count = lax.axis_size(axis)
        results = []
        for start, array in ((0, first), (1, second)):
            pairs = [(i, i + 1) for i in range(start, count - 1, 2)]
            results.append(lax.ppermute(array, axis, pairs + [(j, i) for i, j in pairs]))
        return results

    return (*swaps("gx", send_x, send_x), *swaps("gy", send_y_0, send_y_1))


TILE = 16
EARLY = 2
WEIGHTS = 7


def reciprocal(value):
    guess = pl.reciprocal(value, approx=True)
    return guess * (2.0 - value * guess)


def weight(centre, beside):
    return 2.0 * centre * beside * reciprocal(centre + beside)


def tile_weights(k, y, perm_ref, edge_x, y_rows, comps):
    layers, rows, cols = perm_ref.shape
    here = slice(y, y + TILE)
    lane = lax.broadcasted_iota(jnp.int32, (TILE, cols), 1)
    is_first, is_last = lane == 0, lane == cols - 1
    at_low = 2 * (layers * comps + k)
    perm_low = pltpu.roll(edge_x[here], lax.rem(cols - at_low, cols), 1)
    perm_high = pltpu.roll(edge_x[here], lax.rem(2 * cols - at_low - 2, cols), 1)
    centre = perm_ref[k, here]
    low_y, high_y = beside_y(perm_ref, (k,), y, y_rows)
    to_left = weight(centre, jnp.where(is_first, perm_low, pltpu.roll(centre, 1, 1)))
    to_right = weight(centre, jnp.where(is_last, perm_high, pltpu.roll(centre, cols - 1, 1)))
    return [
        jnp.where(k < layers - 1, weight(centre, perm_ref[jnp.minimum(k + 1, layers - 1), here]), 0.0),
        jnp.where(k > 0, weight(centre, perm_ref[jnp.maximum(k - 1, 0), here]), 0.0),
        weight(centre, high_y),
        weight(centre, low_y),
        jnp.where(is_last, 0.0, to_right),
        jnp.where(is_first, 0.0, to_left),
        jnp.where(is_first, to_left, jnp.where(is_last, to_right, 0.0)),
    ]


def beside_y(ref, index, y, y_rows):
    rows, cols = ref.shape[-2:]
    row = lax.broadcasted_iota(jnp.int32, (TILE, cols), 0)
    if y > 0:
        low = ref[(*index, slice(y - 1, y - 1 + TILE))]
    else:
        low = jnp.where(row == 0, y_rows[0], pltpu.roll(ref[(*index, slice(0, TILE))], 1, 0))
    if y + TILE < rows:
        high = ref[(*index, slice(y + 1, y + 1 + TILE))]
    else:
        high = jnp.where(row == TILE - 1, y_rows[1], pltpu.roll(ref[(*index, slice(y, y + TILE))], TILE - 1, 0))
    return low, high


def apply_kernel(is_first_apply, is_inner, *refs):
    names = ["field", "masked", "mask", "place", "x_0", "x_1", "early_diag", "early_flux"]
    names += ["diag_hbm", "flux_hbm"] if is_first_apply and is_inner else ["late_diag", "late_flux"]
    names += ["perm"] if is_first_apply else ["weights"]
    names += [] if is_inner else ["y_0", "y_1", "inner"]
    names += ["out"] if is_inner or is_first_apply else ["out_hbm"]
    if is_first_apply:
        names += ["late_diag", "late_flux"] if is_inner else ["rounded"]
        names += ["weights"]
    names += ["edge_x", "turned", "beside_x"]
    names += ["sems"] if is_first_apply and is_inner else []
    names += [] if is_inner or is_first_apply else ["out", "sems"]
    ref = dict(zip(names, refs, strict=True))
    field_ref, masked_ref, edge_x, place = ref["field"], ref["masked"], ref["edge_x"], ref["place"]
    layers, comps, rows, cols = field_ref.shape
    early = ref["early_diag"].shape[0]
    inner_rows = rows - 2 * TILE
    tiles = list(range(TILE, rows - TILE, TILE)) if is_inner else [0, rows - TILE]
    here_rows = len(tiles) * TILE

    def blocks(i):
        return [
            pltpu.make_async_copy(ref[f"{name}_hbm"].at[early + i], ref[f"late_{name}"].at[i], ref["sems"].at[j, i])
            for j, name in enumerate(("diag", "flux"))
        ]

    def out_copies(k):
        middle = slice(TILE, rows - TILE)
        pairs = [(ref["inner"].at[k], ref["out_hbm"].at[k, :, middle])]
        pairs += [
            (ref["out"].at[k, :, j * TILE : (j + 1) * TILE], ref["out_hbm"].at[k, :, y : y + TILE]) for j, y in enumerate(tiles)
        ]
        return [pltpu.make_async_copy(a, b, ref["sems"].at[j, k]) for j, (a, b) in enumerate(pairs)]

    if is_first_apply and is_inner:
        for i in range(layers - early):
            for copy in blocks(i):
                copy.start()

    lane = lax.broadcasted_iota(jnp.int32, (rows, cols), 1)
    even_x = lax.axis_index("gx") % 2 == 0
    even_y = lax.axis_index("gy") % 2 == 0
    edge_x[...] = jnp.where((lane % 2 == 0) == even_x, ref["x_1"][...].astype(F32), ref["x_0"][...].astype(F32))
    for k in range(layers):
        for j, y in enumerate(tiles):
            start = k * here_rows + j * TILE
            piece = pltpu.roll(edge_x[y : y + TILE], (cols - 2 * comps * k) % cols, 1)
            ref["turned"][start : start + TILE] = piece.astype(BF16)
    ref["beside_x"][...] = jnp.dot(ref["turned"][...], place[...], preferred_element_type=F32)

    def layer(diag_ref, flux_ref, start, i, carry):
        k = i + start
        above = jnp.minimum(k + 1, layers - 1)
        below = jnp.maximum(k - 1, 0)
        rows_y, perm_y = None, None
        if not is_inner:
            odd = k % 2 == 1
            here = pl.ds(pl.multiple_of(16 * (k // 2), 16), 16)
            sides = [ref[name][here].astype(F32) for name in ("y_0", "y_1")]
            sides = [jnp.where(odd, side[comps:], side[:comps]) for side in sides]
            rows_y = (jnp.where(even_y, sides[1], sides[0]), jnp.where(even_y, sides[0], sides[1]))
        if is_first_apply and not is_inner:
            here = slice(layers * comps, layers * comps + 16)
            mine = lax.broadcasted_iota(jnp.int32, (16, cols), 0) == k
            sides = [
                jnp.sum(jnp.where(mine, ref[name][here].astype(F32), 0.0), axis=0, keepdims=True) for name in ("y_0", "y_1")
            ]
            perm_y = (jnp.where(even_y, sides[1], sides[0]), jnp.where(even_y, sides[0], sides[1]))
        if is_first_apply and is_inner and start > 0:
            for copy in blocks(i):
                copy.wait()

        for j, y in enumerate(tiles):
            here, local = slice(y, y + TILE), slice(j * TILE, (j + 1) * TILE)
            side_rows = pl.ds(pl.multiple_of(k * here_rows + j * TILE, TILE), TILE)
            if is_first_apply:
                weights = tile_weights(k, y, ref["perm"], edge_x, perm_y, comps)
                for number, value in enumerate(weights):
                    ref["weights"][k, number, local] = value
            else:
                weights = [ref["weights"][k, number, local] for number in range(WEIGHTS)]
            total = [None] * comps
            for r in range(comps):
                own = masked_ref[k, r, here]
                low, high = beside_y(masked_ref, (k, r), y, None if is_inner else [side[r : r + 1] for side in rows_y])
                summed = (
                    weights[0] * masked_ref[above, r, here]
                    + weights[1] * masked_ref[below, r, here]
                    + weights[2] * high
                    + weights[3] * low
                    + weights[4] * pltpu.roll(own, cols - 1, 1)
                    + weights[5] * pltpu.roll(own, 1, 1)
                    + weights[6] * ref["beside_x"][side_rows, r * cols : (r + 1) * cols]
                )
                for c in range(comps):
                    term = diag_ref[i, r, c, here].astype(F32) * own - flux_ref[i, r, c, here].astype(F32) * summed
                    total[c] = term if r == 0 else total[c] + term
            well = ref["mask"][here].astype(F32)
            for c in range(comps):
                value = total[c] + well * field_ref[k, c, here]
                if is_first_apply and not is_inner:
                    ref["out"][k, c, here] = value
                    columns = pl.ds(pl.multiple_of(k * cols, cols), cols)
                    ref["rounded"][c * rows + y : c * rows + y + TILE, columns] = value.astype(BF16)
                else:
                    ref["out"][k, c, local] = value
        if is_first_apply and not is_inner:
            columns = pl.ds(pl.multiple_of(k * cols, cols), cols)
            for c in range(comps):
                value = ref["inner"][k, c]
                ref["out"][k, c, TILE : rows - TILE] = value
                ref["rounded"][c * rows + TILE : (c + 1) * rows - TILE, columns] = value.astype(BF16)
        if not is_first_apply and not is_inner:
            for copy in out_copies(k):
                copy.start()
        return carry

    unrolled(early, early, functools.partial(layer, ref["early_diag"], ref["early_flux"], 0))
    unrolled(layers - early, 2, functools.partial(layer, ref["late_diag"], ref["late_flux"], early))
    if not is_first_apply and not is_inner:
        for k in range(layers):
            for copy in out_copies(k):
                copy.wait()


def apply_rows(is_first_apply, is_inner, field, masked, mask, place, halos, early, late, third, inner=None):
    layers, comps, rows, cols = field.shape
    vmem = pl.BlockSpec(memory_space=pltpu.VMEM)
    hbm = pl.BlockSpec(memory_space=pltpu.HBM)
    here_rows = rows - 2 * TILE if is_inner else 2 * TILE
    late_count = layers - early[0].shape[0]
    here = (layers, comps, here_rows, cols)
    loads = is_first_apply and is_inner
    late_spec = hbm if loads else vmem
    arrays = [field, masked, mask, place, *halos[:2], *early, *(in_hbm(*late) if loads else late), third]
    specs = [vmem] * 8 + [late_spec] * 2 + [vmem]
    if not is_inner:
        arrays += [*halos[2:], inner]
        specs += [vmem] * 3
    if is_inner:
        out_shape, out_specs = [pltpu.VMEM(here, F32)], [vmem]
    else:
        out_shape = [jax.ShapeDtypeStruct(field.shape, F32)]
        out_specs = [vmem if is_first_apply else hbm]
    if is_first_apply:
        if is_inner:
            out_shape += [pltpu.VMEM((late_count, *block.shape[1:]), BF16) for block in late]
        else:
            out_shape.append(jax.ShapeDtypeStruct((comps * rows, layers * cols), BF16))
        out_shape.append(pltpu.VMEM((layers, WEIGHTS, here_rows, cols), F32))
        out_specs = [vmem] * len(out_shape)
    scratch = [
        pltpu.VMEM((rows, cols), F32),
        pltpu.VMEM((layers * here_rows, cols), BF16),
        pltpu.VMEM((layers * here_rows, comps * cols), F32),
    ]
    if loads:
        scratch.append(pltpu.SemaphoreType.DMA((2, late_count)))
    if not is_first_apply and not is_inner:
        scratch += [pltpu.VMEM(here, F32), pltpu.SemaphoreType.DMA((3, layers))]
    size = layers * comps * comps * here_rows * cols
    return pl.pallas_call(
        functools.partial(apply_kernel, is_first_apply, is_inner),
        in_specs=specs,
        out_specs=out_specs,
        out_shape=out_shape,
        scratch_shapes=scratch,
        compiler_params=params(16),
        cost_estimate=cost(8 * size, 4 * size + 8 * field.size),
    )(*arrays)


def split_cells(cells, rows, cols):
    layer = cells // (rows * cols)
    y = (cells // cols) % rows
    return layer * cols + cells % cols, y


def unrolled(count, together, body):
    def group(i, carry):
        for j in range(together):
            body(i * together + j, None)
        return carry

    together = math.gcd(count, together)
    lax.fori_loop(0, count // together, group, 0)


def one_hot(column, count, slots):
    number = lax.broadcasted_iota(jnp.int32, (count, slots), 0)
    return jnp.where(number == column, 1.0, 0.0).astype(BF16)


def gather_kernel(rows, cols, helper_ref, count_ref, cells_ref, rounded_ref, sent_ref, kept_ref=None):
    chunks, _, slots = cells_ref.shape
    comps, width = sent_ref.shape[1:]
    per_chunk = slots // width
    row_number = lax.broadcasted_iota(jnp.int32, (rows, slots), 0)

    def one(i, carry):
        column, y = split_cells(cells_ref[i], rows, cols)
        chosen = one_hot(column, rounded_ref.shape[1], slots)
        if kept_ref is not None:
            kept_ref[:, pl.ds(pl.multiple_of(i * slots, slots), slots)] = chosen
        found = jnp.dot(rounded_ref[...], chosen, preferred_element_type=F32)
        at_row = row_number == y
        values = [
            jnp.sum(jnp.where(at_row, found[c * rows : (c + 1) * rows], 0.0), axis=0, keepdims=True)
            for c in range(comps)
        ]
        values = jnp.concatenate(values, axis=0)
        for j in range(per_chunk):
            b = i * per_chunk + j
            live = jnp.where(b < count_ref[0, 0], 1.0, 0.0)
            sent_ref[helper_ref[0, 0, b]] = (values[:, j * width : (j + 1) * width] * live).astype(BF16)
        return carry

    unrolled(chunks, 4, one)


def gather(rounded, cells, helper, count, comps, rows, cols, width):
    blocks = helper.shape[-1]
    smem = pl.BlockSpec(memory_space=pltpu.SMEM)
    vmem = pl.BlockSpec(memory_space=pltpu.VMEM)
    out_shape = [jax.ShapeDtypeStruct((blocks, comps, width), BF16)]
    if rounded.shape[1] * cells.size * 2 <= KEPT_BYTES:
        out_shape.append(pltpu.VMEM((rounded.shape[1], cells.size), BF16))
    return pl.pallas_call(
        functools.partial(gather_kernel, rows, cols),
        in_specs=[smem, smem, vmem, vmem],
        out_specs=[vmem] * len(out_shape),
        out_shape=out_shape,
        compiler_params=params(16),
        cost_estimate=cost(2 * rounded.size * cells.size, 2 * rounded.size),
    )(helper, count, cells, rounded)


PARTS = 3


def helper_kernel(inverse_ref, coupling_ref, state_ref, picked_ref, reply_ref):
    blocks, comps = inverse_ref.shape[:2]
    width = inverse_ref.shape[-1]

    def transposed(block_ref, b, value):
        block = block_ref[b].astype(F32)
        total = block[0] * value[0:1]
        for r in range(1, comps):
            total += block[r] * value[r : r + 1]
        return total

    def one(b, totals):
        multiplier = transposed(inverse_ref, b, picked_ref[b].astype(F32))
        state = state_ref[b].astype(F32)
        part = multiplier * state
        correction = -transposed(coupling_ref, b, multiplier)
        reply_ref[b, 0:comps] = correction.astype(BF16)
        return tuple(totals[j] + part * state[j : j + 1] for j in range(comps))

    totals = lax.fori_loop(0, blocks, one, (jnp.zeros((comps, width), F32),) * comps)
    lane = lax.broadcasted_iota(jnp.int32, (comps, width), 1)
    rest = jnp.zeros((comps, width), F32)
    for j in range(comps):
        column = jnp.sum(totals[j], axis=1, keepdims=True)
        rest = jnp.where(lane % comps == j, column, rest)
    packed = jnp.zeros((comps, width), F32)
    for part in range(PARTS):
        rounded = rest.astype(BF16).astype(F32)
        packed = jnp.where(lane // comps == part, rounded, packed)
        rest = rest - rounded
    packed = packed.astype(BF16)
    for b in range(blocks):
        reply_ref[b, comps : 2 * comps] = packed


def at_helper(inverse, coupling, state, picked):
    blocks, comps, _, width = inverse.shape
    return pl.pallas_call(
        helper_kernel,
        out_shape=jax.ShapeDtypeStruct((blocks, 2 * comps, width), BF16),
        compiler_params=params(16),
        cost_estimate=cost(4 * inverse.size, 4 * inverse.size),
    )(inverse, coupling, state, picked)


def scatter_kernel(scale, has_kept, helper_ref, cells_ref, back_ref, first_ref, mask_ref, *refs):
    kept_ref = refs[0] if has_kept else None
    second_ref, masked_ref, *sends, grad_ref, added, side_y = refs[has_kept:]
    layers, comps, rows, cols = first_ref.shape
    chunks, _, slots = cells_ref.shape
    width = back_ref.shape[-1]
    per_chunk = slots // width
    row_number = lax.broadcasted_iota(jnp.int32, (rows, slots), 0)
    for k in range(layers):
        for c in range(comps):
            added[c * rows : (c + 1) * rows, k * cols : (k + 1) * cols] = first_ref[k, c]

    def one(i, carry):
        column, y = split_cells(cells_ref[i], rows, cols)
        if has_kept:
            chosen = kept_ref[:, pl.ds(pl.multiple_of(i * slots, slots), slots)]
        else:
            chosen = one_hot(column, added.shape[1], slots)
        parts = [back_ref[helper_ref[0, 0, i * per_chunk + j]].astype(F32)[:comps] for j in range(per_chunk)]
        correction = jnp.concatenate(parts, axis=1)
        at_row = row_number == y
        spread = jnp.concatenate(
            [jnp.where(at_row, correction[c : c + 1], 0.0).astype(BF16) for c in range(comps)], axis=0
        )
        added[...] += lax.dot_general(spread, chosen, (((1,), (1,)), ((), ())), preferred_element_type=F32)
        return carry

    unrolled(chunks, 2, one)
    for k in range(layers):
        for c in range(comps):
            second_ref[k, c] = added[c * rows : (c + 1) * rows, k * cols : (k + 1) * cols]
    write_edges(second_ref, mask_ref, None, masked_ref, side_y, sends)
    total = back_ref[0].astype(F32)[comps:]
    for b in range(1, back_ref.shape[0]):
        total += back_ref[b].astype(F32)[comps:]
    whole = total
    for part in range(1, PARTS):
        whole += pltpu.roll(total, width - part * comps, 1)
    grad_ref[...] = (whole * scale)[:, :comps]


def scatter(first, back, helper, cells, mask, kept, scale):
    layers, comps, rows, cols = first.shape
    smem = pl.BlockSpec(memory_space=pltpu.SMEM)
    vmem = pl.BlockSpec(memory_space=pltpu.VMEM)
    edges = edge_shapes(*first.shape)
    return pl.pallas_call(
        functools.partial(scatter_kernel, scale, len(kept)),
        in_specs=[smem] + [vmem] * (4 + len(kept)),
        out_specs=[vmem] * (3 + len(edges)),
        out_shape=[
            pltpu.VMEM(first.shape, F32),
            pltpu.VMEM(first.shape, F32),
            *edges,
            jax.ShapeDtypeStruct((comps, comps), F32),
        ],
        scratch_shapes=[pltpu.VMEM((comps * rows, layers * cols), F32), edge_scratch(layers, comps, cols)],
        compiler_params=params(24),
        cost_estimate=cost(2 * first.size * cells.size, 8 * first.size),
    )(helper, cells, back, first, mask, *kept)


def shards(
    cotangent,
    permeability,
    well_mask,
    diag_block,
    flux_block,
    cell_list,
    block_count,
    helper_of,
    flash_inverse,
    flash_coupling,
    phase_state,
):
    layers, comps, rows, cols = cotangent.shape
    blocks, width = helper_of.shape[-1], flash_inverse.shape[-1]
    inverse = flash_inverse.reshape(blocks, comps, comps, width)
    coupling = flash_coupling.reshape(blocks, comps, comps, width)
    state = phase_state.reshape(blocks, comps, width)

    def cells(chunk):
        return cell_list.reshape(-1, 1, min(chunk, cell_list.shape[-1]))

    def to_partners(array):
        return lax.all_to_all(array, AXES, split_axis=0, concat_axis=0, tiled=True)

    *sides, masked, field, mask, perm, early_diag, early_flux, place = opening(
        cotangent, well_mask, permeability, diag_block, flux_block, min(EARLY, layers - 1)
    )
    early = (early_diag, early_flux)
    halos = exchange(*sides)
    inner, *late, inner_weights = apply_rows(
        True, True, field, masked, mask, place, halos, early, (diag_block, flux_block), perm
    )
    first, rounded, outer_weights = apply_rows(True, False, field, masked, mask, place, halos, early, late, perm, inner)
    sent, *chosen = gather(rounded, cells(GATHER_CHUNK), helper_of, block_count, comps, rows, cols, width)
    reply = at_helper(inverse, coupling, state, to_partners(sent))
    devices = lax.axis_size("gx") * lax.axis_size("gy")
    scale = -1.0 / math.sqrt(width * devices * devices)
    second, masked, *sides, interaction_grad = scatter(
        first, to_partners(reply), helper_of, cells(SCATTER_CHUNK), mask, chosen, scale
    )
    halos = exchange(*sides)
    (inner,) = apply_rows(False, True, second, masked, mask, place, halos, early, late, inner_weights)
    (adjoint,) = apply_rows(False, False, second, masked, mask, place, halos, early, late, outer_weights, inner)
    return (adjoint, interaction_grad)


def solution(mesh):
    return jax.shard_map(
        shards,
        mesh=mesh,
        in_specs=(
            P(None, None, "gy", "gx"),
            P(None, "gy", "gx"),
            P("gy", "gx"),
            P(None, None, None, "gy", "gx"),
            P(None, None, None, "gy", "gx"),
            P("gy", "gx", None),
            P("gy", "gx"),
            P("gy", "gx", None),
            P("gy", "gx", None, None, None, None),
            P("gy", "gx", None, None, None, None),
            P("gy", "gx", None, None, None),
        ),
        out_specs=(P(None, None, "gy", "gx"), P()),
        check_vma=False,
    )
```

```python
import functools
import math

import jax
import jax.numpy as jnp
from jax import lax
from jax.experimental import pallas as pl
from jax.experimental.pallas import tpu as pltpu
from jax.sharding import PartitionSpec as P

F32 = jnp.float32
BF16 = jnp.bfloat16
AXES = ("gx", "gy")
MIB = 1024 * 1024
GATHER_CHUNK, SCATTER_CHUNK = 512, 2048
KEPT_BYTES = 8 * MIB


def params(mib):
    return pltpu.CompilerParams(vmem_limit_bytes=mib * MIB)


def cost(flops, moved):
    return pl.CostEstimate(flops=int(flops), bytes_accessed=int(moved), transcendentals=0)


def round_up(number, step):
    return -(-number // step) * step


def write_edges(field_ref, mask_ref, perm_ref, masked_ref, side_y, sends):
    send_y_0, send_y_1, send_x = sends
    layers, comps, rows, cols = field_ref.shape
    with_perm = perm_ref is not None
    clear = 1.0 - mask_ref[...].astype(F32)
    lane = lax.broadcasted_iota(jnp.int32, (rows, cols), 1)
    pair = lane // 2
    along_x = jnp.zeros((rows, cols), F32)
    side_y[...] = jnp.zeros_like(side_y)
    for k in range(layers):
        for c in range(comps + with_perm):
            if c < comps:
                value, at = field_ref[k, c] * clear, k * comps + c
                masked_ref[k, c] = value
            else:
                value, at = perm_ref[k], layers * comps + k
            side_y[0, at : at + 1, :] = value[0:1]
            side_y[1, at : at + 1, :] = value[rows - 1 : rows]
            along_x = jnp.where(pair == at, pltpu.roll(value, (2 * at + 1) % cols, 1), along_x)
    even = lax.axis_index("gy") % 2 == 0
    send_x[...] = along_x.astype(BF16)
    low, high = side_y[0].astype(BF16), side_y[1].astype(BF16)
    send_y_0[...] = jnp.where(even, high, low)
    send_y_1[...] = jnp.where(even, low, high)


def write_place(place_ref):
    cols, width = place_ref.shape
    number = lax.broadcasted_iota(jnp.int32, (cols, cols), 0)
    spot = lax.broadcasted_iota(jnp.int32, (cols, cols), 1)
    for r in range(width // cols):
        taken = ((number == 2 * r) & (spot == 0)) | ((number == 2 * r + 1) & (spot == cols - 1))
        place_ref[:, r * cols : (r + 1) * cols] = jnp.where(taken, 1.0, 0.0).astype(BF16)


def opening_kernel(
    field_hbm, mask_hbm, perm_hbm, diag_hbm, flux_hbm,
    send_y_0, send_y_1, send_x, masked_ref, field_ref, mask_ref, perm_ref, place_ref,
    side_y, sems,
):
    sources, targets = (field_hbm, mask_hbm, perm_hbm), (field_ref, mask_ref, perm_ref)
    copies = [pltpu.make_async_copy(a, b, sems.at[i]) for i, (a, b) in enumerate(zip(sources, targets))]
    for copy in copies:
        copy.start()
    write_place(place_ref)
    for copy in copies:
        copy.wait()
    write_edges(field_ref, mask_ref, perm_ref, masked_ref, side_y, (send_y_0, send_y_1, send_x))


def edge_rows(layers, comps):
    return round_up(layers * (comps + 1), 16)


def edge_shapes(layers, comps, rows, cols):
    along_y = (edge_rows(layers, comps), cols)
    return [jax.ShapeDtypeStruct(shape, BF16) for shape in (along_y, along_y, (rows, cols))]


def edge_scratch(layers, comps, cols):
    return pltpu.VMEM((2, edge_rows(layers, comps), cols), F32)


def opening(field, mask, perm, diag, flux):
    layers, comps, rows, cols = field.shape
    hbm = pl.BlockSpec(memory_space=pltpu.HBM)
    vmem = pl.BlockSpec(memory_space=pltpu.VMEM)
    kept = [(array.shape, array.dtype) for array in (field, field, mask, perm)]
    kept.append(((cols, comps * cols), BF16))
    return pl.pallas_call(
        opening_kernel,
        in_specs=[hbm] * 5,
        out_specs=[vmem] * 8,
        out_shape=[*edge_shapes(*field.shape), *(pltpu.VMEM(*item) for item in kept)],
        scratch_shapes=[edge_scratch(layers, comps, cols), pltpu.SemaphoreType.DMA((3,))],
        compiler_params=params(16),
        cost_estimate=cost(4 * field.size, 8 * field.size),
    )(*(pltpu.with_memory_space_constraint(array, pltpu.HBM) for array in (field, mask, perm, diag, flux)))


def exchange(send_y_0, send_y_1, send_x):
    def swaps(axis, first, second):
        count = lax.axis_size(axis)
        results = []
        for start, array in ((0, first), (1, second)):
            pairs = [(i, i + 1) for i in range(start, count - 1, 2)]
            results.append(lax.ppermute(array, axis, pairs + [(j, i) for i, j in pairs]))
        return results

    return (*swaps("gx", send_x, send_x), *swaps("gy", send_y_0, send_y_1))


TILE = 16
WEIGHTS = 7


def reciprocal(value):
    guess = pl.reciprocal(value, approx=True)
    return guess * (2.0 - value * guess)


def weight(centre, beside):
    return 2.0 * centre * beside * reciprocal(centre + beside)


def tile_weights(k, y, perm_ref, edge_x, y_rows, comps):
    layers, rows, cols = perm_ref.shape
    here = slice(y, y + TILE)
    lane = lax.broadcasted_iota(jnp.int32, (TILE, cols), 1)
    is_first, is_last = lane == 0, lane == cols - 1
    at_low = 2 * (layers * comps + k)
    perm_low = pltpu.roll(edge_x[here], lax.rem(cols - at_low, cols), 1)
    perm_high = pltpu.roll(edge_x[here], lax.rem(2 * cols - at_low - 2, cols), 1)
    centre = perm_ref[k, here]
    low_y, high_y = beside_y(perm_ref, (k,), y, y_rows)
    to_left = weight(centre, jnp.where(is_first, perm_low, pltpu.roll(centre, 1, 1)))
    to_right = weight(centre, jnp.where(is_last, perm_high, pltpu.roll(centre, cols - 1, 1)))
    return [
        jnp.where(k < layers - 1, weight(centre, perm_ref[jnp.minimum(k + 1, layers - 1), here]), 0.0),
        jnp.where(k > 0, weight(centre, perm_ref[jnp.maximum(k - 1, 0), here]), 0.0),
        weight(centre, high_y),
        weight(centre, low_y),
        jnp.where(is_last, 0.0, to_right),
        jnp.where(is_first, 0.0, to_left),
        jnp.where(is_first, to_left, jnp.where(is_last, to_right, 0.0)),
    ]


def beside_y(ref, index, y, y_rows):
    rows, cols = ref.shape[-2:]
    row = lax.broadcasted_iota(jnp.int32, (TILE, cols), 0)
    if y > 0:
        low = ref[(*index, slice(y - 1, y - 1 + TILE))]
    else:
        low = jnp.where(row == 0, y_rows[0], pltpu.roll(ref[(*index, slice(0, TILE))], 1, 0))
    if y + TILE < rows:
        high = ref[(*index, slice(y + 1, y + 1 + TILE))]
    else:
        high = jnp.where(row == TILE - 1, y_rows[1], pltpu.roll(ref[(*index, slice(y, y + TILE))], TILE - 1, 0))
    return low, high


def apply_kernel(is_first_apply, is_inner, *refs):
    names = ["field", "masked", "mask", "place", "x_0", "x_1", "diag", "flux"]
    names += ["perm"] if is_first_apply else ["weights"]
    names += [] if is_inner else ["y_0", "y_1", "inner", "begun"]
    names += ["out"] if is_inner or is_first_apply else ["out_hbm"]
    names += ["begun"] if is_inner else []
    if is_first_apply:
        names += [] if is_inner else ["rounded"]
        names += ["weights"]
    names += ["edge_x", "turned", "beside_x"]
    names += [] if is_inner or is_first_apply else ["out", "sems"]
    ref = dict(zip(names, refs, strict=True))
    field_ref, masked_ref, edge_x, place = ref["field"], ref["masked"], ref["edge_x"], ref["place"]
    layers, comps, rows, cols = field_ref.shape
    diag_ref, flux_ref = ref["diag"], ref["flux"]
    tiles = list(range(TILE, rows - TILE, TILE)) if is_inner else [0, rows - TILE]
    here_rows = len(tiles) * TILE

    def out_copies(k):
        middle = slice(TILE, rows - TILE)
        pairs = [(ref["inner"].at[k], ref["out_hbm"].at[k, :, middle])]
        pairs += [
            (ref["out"].at[k, :, j * TILE : (j + 1) * TILE], ref["out_hbm"].at[k, :, y : y + TILE]) for j, y in enumerate(tiles)
        ]
        return [pltpu.make_async_copy(a, b, ref["sems"].at[j, k]) for j, (a, b) in enumerate(pairs)]

    lane = lax.broadcasted_iota(jnp.int32, (rows, cols), 1)
    even_x = lax.axis_index("gx") % 2 == 0
    even_y = lax.axis_index("gy") % 2 == 0
    edge_x[...] = jnp.where((lane % 2 == 0) == even_x, ref["x_1"][...].astype(F32), ref["x_0"][...].astype(F32))
    for k in range(layers):
        for j, y in enumerate(tiles):
            start = k * here_rows + j * TILE
            piece = pltpu.roll(edge_x[y : y + TILE], (cols - 2 * comps * k) % cols, 1)
            ref["turned"][start : start + TILE] = piece.astype(BF16)
    ref["beside_x"][...] = jnp.dot(ref["turned"][...], place[...], preferred_element_type=F32)

    def layer(k, carry):
        above = jnp.minimum(k + 1, layers - 1)
        below = jnp.maximum(k - 1, 0)
        rows_y, perm_y = None, None
        if not is_inner:
            odd = k % 2 == 1
            here = pl.ds(pl.multiple_of(16 * (k // 2), 16), 16)
            sides = [ref[name][here].astype(F32) for name in ("y_0", "y_1")]
            sides = [jnp.where(odd, side[comps:], side[:comps]) for side in sides]
            rows_y = (jnp.where(even_y, sides[1], sides[0]), jnp.where(even_y, sides[0], sides[1]))
        if is_first_apply and not is_inner:
            here = slice(layers * comps, layers * comps + 16)
            mine = lax.broadcasted_iota(jnp.int32, (16, cols), 0) == k
            sides = [
                jnp.sum(jnp.where(mine, ref[name][here].astype(F32), 0.0), axis=0, keepdims=True) for name in ("y_0", "y_1")
            ]
            perm_y = (jnp.where(even_y, sides[1], sides[0]), jnp.where(even_y, sides[0], sides[1]))
        for j, y in enumerate(tiles):
            here, local = slice(y, y + TILE), slice(j * TILE, (j + 1) * TILE)
            side_rows = pl.ds(pl.multiple_of(k * here_rows + j * TILE, TILE), TILE)
            if is_first_apply:
                weights = tile_weights(k, y, ref["perm"], edge_x, perm_y, comps)
                for number, value in enumerate(weights):
                    ref["weights"][k, number, local] = value
            else:
                weights = [ref["weights"][k, number, local] for number in range(WEIGHTS)]
            total = [None] * comps
            for r in range(comps):
                own = masked_ref[k, r, here]
                low, high = beside_y(masked_ref, (k, r), y, None if is_inner else [side[r : r + 1] for side in rows_y])
                summed = (
                    weights[0] * masked_ref[above, r, here]
                    + weights[1] * masked_ref[below, r, here]
                    + weights[2] * high
                    + weights[3] * low
                    + weights[4] * pltpu.roll(own, cols - 1, 1)
                    + weights[5] * pltpu.roll(own, 1, 1)
                    + weights[6] * ref["beside_x"][side_rows, r * cols : (r + 1) * cols]
                )
                for c in range(comps):
                    term = -flux_ref[k, r, c, here].astype(F32) * summed
                    if is_inner:
                        term = diag_ref[k, r, c, here].astype(F32) * own + term
                    total[c] = term if r == 0 else total[c] + term
            well = ref["mask"][here].astype(F32) if is_inner else None
            for c in range(comps):
                value = total[c] + (well * field_ref[k, c, here] if is_inner else ref["begun"][k, c, local])
                if is_first_apply and not is_inner:
                    ref["out"][k, c, here] = value
                    columns = pl.ds(pl.multiple_of(k * cols, cols), cols)
                    ref["rounded"][c * rows + y : c * rows + y + TILE, columns] = value.astype(BF16)
                else:
                    ref["out"][k, c, local] = value
        for j, y in enumerate([0, rows - TILE] if is_inner else []):
            here, local = slice(y, y + TILE), slice(j * TILE, (j + 1) * TILE)
            well = ref["mask"][here].astype(F32)
            total = [well * field_ref[k, c, here] for c in range(comps)]
            for r in range(comps):
                own = masked_ref[k, r, here]
                for c in range(comps):
                    total[c] += diag_ref[k, r, c, here].astype(F32) * own
            for c in range(comps):
                ref["begun"][k, c, local] = total[c]
        if is_first_apply and not is_inner:
            columns = pl.ds(pl.multiple_of(k * cols, cols), cols)
            for c in range(comps):
                value = ref["inner"][k, c]
                ref["out"][k, c, TILE : rows - TILE] = value
                ref["rounded"][c * rows + TILE : (c + 1) * rows - TILE, columns] = value.astype(BF16)
        if not is_first_apply and not is_inner:
            for copy in out_copies(k):
                copy.start()
        return carry

    unrolled(layers, 2, layer)
    if not is_first_apply and not is_inner:
        for k in range(layers):
            for copy in out_copies(k):
                copy.wait()


def apply_rows(is_first_apply, is_inner, field, masked, mask, place, halos, blocks, third, *inner):
    layers, comps, rows, cols = field.shape
    vmem = pl.BlockSpec(memory_space=pltpu.VMEM)
    hbm = pl.BlockSpec(memory_space=pltpu.HBM)
    here_rows = rows - 2 * TILE if is_inner else 2 * TILE
    here = (layers, comps, here_rows, cols)
    arrays = [field, masked, mask, place, *halos[:2], *blocks, third]
    specs = [vmem] * 9
    if not is_inner:
        arrays += [*halos[2:], *inner]
        specs += [vmem] * 4
    if is_inner:
        begun = (layers, comps, 2 * TILE, cols)
        out_shape, out_specs = [pltpu.VMEM(here, F32), pltpu.VMEM(begun, F32)], [vmem] * 2
    else:
        out_shape = [jax.ShapeDtypeStruct(field.shape, F32)]
        out_specs = [vmem if is_first_apply else hbm]
    if is_first_apply:
        if not is_inner:
            out_shape.append(jax.ShapeDtypeStruct((comps * rows, layers * cols), BF16))
        out_shape.append(pltpu.VMEM((layers, WEIGHTS, here_rows, cols), F32))
        out_specs = [vmem] * len(out_shape)
    scratch = [
        pltpu.VMEM((rows, cols), F32),
        pltpu.VMEM((layers * here_rows, cols), BF16),
        pltpu.VMEM((layers * here_rows, comps * cols), F32),
    ]
    if not is_first_apply and not is_inner:
        scratch += [pltpu.VMEM(here, F32), pltpu.SemaphoreType.DMA((3, layers))]
    size = layers * comps * comps * here_rows * cols
    return pl.pallas_call(
        functools.partial(apply_kernel, is_first_apply, is_inner),
        in_specs=specs,
        out_specs=out_specs,
        out_shape=out_shape,
        scratch_shapes=scratch,
        compiler_params=params(16),
        cost_estimate=cost(8 * size, 4 * size + 8 * field.size),
    )(*arrays)


def split_cells(cells, rows, cols):
    layer = cells // (rows * cols)
    y = (cells // cols) % rows
    return layer * cols + cells % cols, y


def unrolled(count, together, body):
    def group(i, carry):
        for j in range(together):
            body(i * together + j, None)
        return carry

    together = math.gcd(count, together)
    lax.fori_loop(0, count // together, group, 0)


def one_hot(column, count, slots):
    number = lax.broadcasted_iota(jnp.int32, (count, slots), 0)
    return jnp.where(number == column, 1.0, 0.0).astype(BF16)


def gather_kernel(rows, cols, helper_ref, count_ref, cells_ref, rounded_ref, sent_ref, kept_ref=None):
    chunks, _, slots = cells_ref.shape
    comps, width = sent_ref.shape[1:]
    per_chunk = slots // width
    row_number = lax.broadcasted_iota(jnp.int32, (rows, slots), 0)

    def one(i, carry):
        column, y = split_cells(cells_ref[i], rows, cols)
        chosen = one_hot(column, rounded_ref.shape[1], slots)
        if kept_ref is not None:
            kept_ref[:, pl.ds(pl.multiple_of(i * slots, slots), slots)] = chosen
        found = jnp.dot(rounded_ref[...], chosen, preferred_element_type=F32)
        at_row = row_number == y
        values = [
            jnp.sum(jnp.where(at_row, found[c * rows : (c + 1) * rows], 0.0), axis=0, keepdims=True)
            for c in range(comps)
        ]
        values = jnp.concatenate(values, axis=0)
        for j in range(per_chunk):
            b = i * per_chunk + j
            live = jnp.where(b < count_ref[0, 0], 1.0, 0.0)
            sent_ref[helper_ref[0, 0, b]] = (values[:, j * width : (j + 1) * width] * live).astype(BF16)
        return carry

    unrolled(chunks, 4, one)


def gather(rounded, cells, helper, count, comps, rows, cols, width):
    blocks = helper.shape[-1]
    smem = pl.BlockSpec(memory_space=pltpu.SMEM)
    vmem = pl.BlockSpec(memory_space=pltpu.VMEM)
    out_shape = [jax.ShapeDtypeStruct((blocks, comps, width), BF16)]
    if rounded.shape[1] * cells.size * 2 <= KEPT_BYTES:
        out_shape.append(pltpu.VMEM((rounded.shape[1], cells.size), BF16))
    return pl.pallas_call(
        functools.partial(gather_kernel, rows, cols),
        in_specs=[smem, smem, vmem, vmem],
        out_specs=[vmem] * len(out_shape),
        out_shape=out_shape,
        compiler_params=params(16),
        cost_estimate=cost(2 * rounded.size * cells.size, 2 * rounded.size),
    )(helper, count, cells, rounded)


PARTS = 3


def helper_kernel(inverse_ref, coupling_ref, state_ref, picked_ref, reply_ref):
    blocks, comps = inverse_ref.shape[:2]
    width = inverse_ref.shape[-1]

    def transposed(block_ref, b, value):
        block = block_ref[b].astype(F32)
        total = block[0] * value[0:1]
        for r in range(1, comps):
            total += block[r] * value[r : r + 1]
        return total

    def one(b, totals):
        multiplier = transposed(inverse_ref, b, picked_ref[b].astype(F32))
        state = state_ref[b].astype(F32)
        part = multiplier * state
        correction = -transposed(coupling_ref, b, multiplier)
        reply_ref[b, 0:comps] = correction.astype(BF16)
        return tuple(totals[j] + part * state[j : j + 1] for j in range(comps))

    totals = lax.fori_loop(0, blocks, one, (jnp.zeros((comps, width), F32),) * comps)
    lane = lax.broadcasted_iota(jnp.int32, (comps, width), 1)
    rest = jnp.zeros((comps, width), F32)
    for j in range(comps):
        column = jnp.sum(totals[j], axis=1, keepdims=True)
        rest = jnp.where(lane % comps == j, column, rest)
    packed = jnp.zeros((comps, width), F32)
    for part in range(PARTS):
        rounded = rest.astype(BF16).astype(F32)
        packed = jnp.where(lane // comps == part, rounded, packed)
        rest = rest - rounded
    packed = packed.astype(BF16)
    for b in range(blocks):
        reply_ref[b, comps : 2 * comps] = packed


def at_helper(inverse, coupling, state, picked):
    blocks, comps, _, width = inverse.shape
    return pl.pallas_call(
        helper_kernel,
        out_shape=jax.ShapeDtypeStruct((blocks, 2 * comps, width), BF16),
        compiler_params=params(16),
        cost_estimate=cost(4 * inverse.size, 4 * inverse.size),
    )(inverse, coupling, state, picked)


def scatter_kernel(scale, has_kept, helper_ref, cells_ref, back_ref, first_ref, mask_ref, *refs):
    kept_ref = refs[0] if has_kept else None
    second_ref, masked_ref, *sends, grad_ref, added, side_y = refs[has_kept:]
    layers, comps, rows, cols = first_ref.shape
    chunks, _, slots = cells_ref.shape
    width = back_ref.shape[-1]
    per_chunk = slots // width
    row_number = lax.broadcasted_iota(jnp.int32, (rows, slots), 0)
    for k in range(layers):
        for c in range(comps):
            added[c * rows : (c + 1) * rows, k * cols : (k + 1) * cols] = first_ref[k, c]

    def one(i, carry):
        column, y = split_cells(cells_ref[i], rows, cols)
        if has_kept:
            chosen = kept_ref[:, pl.ds(pl.multiple_of(i * slots, slots), slots)]
        else:
            chosen = one_hot(column, added.shape[1], slots)
        parts = [back_ref[helper_ref[0, 0, i * per_chunk + j]].astype(F32)[:comps] for j in range(per_chunk)]
        correction = jnp.concatenate(parts, axis=1)
        at_row = row_number == y
        spread = jnp.concatenate(
            [jnp.where(at_row, correction[c : c + 1], 0.0).astype(BF16) for c in range(comps)], axis=0
        )
        added[...] += lax.dot_general(spread, chosen, (((1,), (1,)), ((), ())), preferred_element_type=F32)
        return carry

    unrolled(chunks, 2, one)
    for k in range(layers):
        for c in range(comps):
            second_ref[k, c] = added[c * rows : (c + 1) * rows, k * cols : (k + 1) * cols]
    write_edges(second_ref, mask_ref, None, masked_ref, side_y, sends)
    total = back_ref[0].astype(F32)[comps:]
    for b in range(1, back_ref.shape[0]):
        total += back_ref[b].astype(F32)[comps:]
    whole = total
    for part in range(1, PARTS):
        whole += pltpu.roll(total, width - part * comps, 1)
    grad_ref[...] = (whole * scale)[:, :comps]


def scatter(first, back, helper, cells, mask, kept, scale):
    layers, comps, rows, cols = first.shape
    smem = pl.BlockSpec(memory_space=pltpu.SMEM)
    vmem = pl.BlockSpec(memory_space=pltpu.VMEM)
    edges = edge_shapes(*first.shape)
    return pl.pallas_call(
        functools.partial(scatter_kernel, scale, len(kept)),
        in_specs=[smem] + [vmem] * (4 + len(kept)),
        out_specs=[vmem] * (3 + len(edges)),
        out_shape=[
            pltpu.VMEM(first.shape, F32),
            pltpu.VMEM(first.shape, F32),
            *edges,
            jax.ShapeDtypeStruct((comps, comps), F32),
        ],
        scratch_shapes=[pltpu.VMEM((comps * rows, layers * cols), F32), edge_scratch(layers, comps, cols)],
        compiler_params=params(24),
        cost_estimate=cost(2 * first.size * cells.size, 8 * first.size),
    )(helper, cells, back, first, mask, *kept)


def shards(
    cotangent,
    permeability,
    well_mask,
    diag_block,
    flux_block,
    cell_list,
    block_count,
    helper_of,
    flash_inverse,
    flash_coupling,
    phase_state,
):
    layers, comps, rows, cols = cotangent.shape
    slots, width = helper_of.shape[-1], flash_inverse.shape[-1]
    inverse = flash_inverse.reshape(slots, comps, comps, width)
    coupling = flash_coupling.reshape(slots, comps, comps, width)
    state = phase_state.reshape(slots, comps, width)

    def cells(chunk):
        return cell_list.reshape(-1, 1, min(chunk, cell_list.shape[-1]))

    def to_partners(array):
        return lax.all_to_all(array, AXES, split_axis=0, concat_axis=0, tiled=True)

    *sides, masked, field, mask, perm, place = opening(cotangent, well_mask, permeability, diag_block, flux_block)
    halos = exchange(*sides)
    blocks = [pltpu.with_memory_space_constraint(block, pltpu.VMEM) for block in (diag_block, flux_block)]
    inner, begun, inner_weights = apply_rows(True, True, field, masked, mask, place, halos, blocks, perm)
    first, rounded, outer_weights = apply_rows(
        True, False, field, masked, mask, place, halos, blocks, perm, inner, begun
    )
    sent, *chosen = gather(rounded, cells(GATHER_CHUNK), helper_of, block_count, comps, rows, cols, width)
    reply = at_helper(inverse, coupling, state, to_partners(sent))
    devices = lax.axis_size("gx") * lax.axis_size("gy")
    scale = -1.0 / math.sqrt(width * devices * devices)
    second, masked, *sides, interaction_grad = scatter(
        first, to_partners(reply), helper_of, cells(SCATTER_CHUNK), mask, chosen, scale
    )
    halos = exchange(*sides)
    inner, begun = apply_rows(False, True, second, masked, mask, place, halos, blocks, inner_weights)
    (adjoint,) = apply_rows(False, False, second, masked, mask, place, halos, blocks, outer_weights, inner, begun)
    return (adjoint, interaction_grad)


def solution(mesh):
    return jax.shard_map(
        shards,
        mesh=mesh,
        in_specs=(
            P(None, None, "gy", "gx"),
            P(None, "gy", "gx"),
            P("gy", "gx"),
            P(None, None, None, "gy", "gx"),
            P(None, None, None, "gy", "gx"),
            P("gy", "gx", None),
            P("gy", "gx"),
            P("gy", "gx", None),
            P("gy", "gx", None, None, None, None),
            P("gy", "gx", None, None, None, None),
            P("gy", "gx", None, None, None),
        ),
        out_specs=(P(None, None, "gy", "gx"), P()),
        check_vma=False,
    )
```

```python
import functools
import math

import jax
import jax.numpy as jnp
from jax import lax
from jax.experimental import pallas as pl
from jax.experimental.pallas import tpu as pltpu
from jax.sharding import PartitionSpec as P

F32 = jnp.float32
BF16 = jnp.bfloat16
AXES = ("gx", "gy")
MIB = 1024 * 1024
GATHER_CHUNK, SCATTER_CHUNK = 512, 2048
KEPT_BYTES = 8 * MIB


def params(mib):
    return pltpu.CompilerParams(vmem_limit_bytes=mib * MIB)


def cost(flops, moved):
    return pl.CostEstimate(flops=int(flops), bytes_accessed=int(moved), transcendentals=0)


def round_up(number, step):
    return -(-number // step) * step


def write_edges(field_ref, mask_ref, perm_ref, masked_ref, side_y, sends, ready=lambda k: None):
    send_y_0, send_y_1, send_x = sends
    layers, comps, rows, cols = field_ref.shape
    with_perm = perm_ref is not None
    clear = 1.0 - mask_ref[...].astype(F32)
    lane = lax.broadcasted_iota(jnp.int32, (rows, cols), 1)
    pair = lane // 2
    along_x = jnp.zeros((rows, cols), F32)
    side_y[...] = jnp.zeros_like(side_y)
    for k in range(layers):
        ready(k)
        for c in range(comps + with_perm):
            if c < comps:
                value, at = field_ref[k, c] * clear, k * comps + c
                masked_ref[k, c] = value
            else:
                value, at = perm_ref[k], layers * comps + k
            side_y[0, at : at + 1, :] = value[0:1]
            side_y[1, at : at + 1, :] = value[rows - 1 : rows]
            along_x = jnp.where(pair == at, pltpu.roll(value, (2 * at + 1) % cols, 1), along_x)
    even = lax.axis_index("gy") % 2 == 0
    send_x[...] = along_x.astype(BF16)
    low, high = side_y[0].astype(BF16), side_y[1].astype(BF16)
    send_y_0[...] = jnp.where(even, high, low)
    send_y_1[...] = jnp.where(even, low, high)


def write_place(place_ref):
    cols, width = place_ref.shape
    number = lax.broadcasted_iota(jnp.int32, (cols, cols), 0)
    spot = lax.broadcasted_iota(jnp.int32, (cols, cols), 1)
    for r in range(width // cols):
        taken = ((number == 2 * r) & (spot == 0)) | ((number == 2 * r + 1) & (spot == cols - 1))
        place_ref[:, r * cols : (r + 1) * cols] = jnp.where(taken, 1.0, 0.0).astype(BF16)


def opening_kernel(
    field_hbm, mask_hbm, perm_hbm, diag_hbm, flux_hbm,
    send_y_0, send_y_1, send_x, masked_ref, field_ref, mask_ref, perm_ref, place_ref,
    side_y, sems,
):
    layers = field_ref.shape[0]
    pairs = [(mask_hbm, mask_ref), (perm_hbm, perm_ref)]
    pairs += [(field_hbm.at[k], field_ref.at[k]) for k in range(layers)]
    copies = [pltpu.make_async_copy(a, b, sems.at[i]) for i, (a, b) in enumerate(pairs)]
    for copy in copies:
        copy.start()
    write_place(place_ref)
    for copy in copies[:2]:
        copy.wait()
    sends = (send_y_0, send_y_1, send_x)
    write_edges(field_ref, mask_ref, perm_ref, masked_ref, side_y, sends, lambda k: copies[2 + k].wait())


def edge_rows(layers, comps):
    return round_up(layers * (comps + 1), 16)


def edge_shapes(layers, comps, rows, cols):
    along_y = (edge_rows(layers, comps), cols)
    return [jax.ShapeDtypeStruct(shape, BF16) for shape in (along_y, along_y, (rows, cols))]


def edge_scratch(layers, comps, cols):
    return pltpu.VMEM((2, edge_rows(layers, comps), cols), F32)


def opening(field, mask, perm, diag, flux):
    layers, comps, rows, cols = field.shape
    hbm = pl.BlockSpec(memory_space=pltpu.HBM)
    vmem = pl.BlockSpec(memory_space=pltpu.VMEM)
    kept = [(array.shape, array.dtype) for array in (field, field, mask, perm)]
    kept.append(((cols, comps * cols), BF16))
    return pl.pallas_call(
        opening_kernel,
        in_specs=[hbm] * 5,
        out_specs=[vmem] * 8,
        out_shape=[*edge_shapes(*field.shape), *(pltpu.VMEM(*item) for item in kept)],
        scratch_shapes=[edge_scratch(layers, comps, cols), pltpu.SemaphoreType.DMA((2 + layers,))],
        compiler_params=params(16),
        cost_estimate=cost(4 * field.size, 8 * field.size),
    )(*(pltpu.with_memory_space_constraint(array, pltpu.HBM) for array in (field, mask, perm, diag, flux)))


def exchange(send_y_0, send_y_1, send_x):
    def swaps(axis, first, second):
        count = lax.axis_size(axis)
        results = []
        for start, array in ((0, first), (1, second)):
            pairs = [(i, i + 1) for i in range(start, count - 1, 2)]
            results.append(lax.ppermute(array, axis, pairs + [(j, i) for i, j in pairs]))
        return results

    return (*swaps("gx", send_x, send_x), *swaps("gy", send_y_0, send_y_1))


TILE = 16
WEIGHTS = 7


def reciprocal(value):
    guess = pl.reciprocal(value, approx=True)
    return guess * (2.0 - value * guess)


def weight(centre, beside):
    return 2.0 * centre * beside * reciprocal(centre + beside)


def tile_weights(k, y, perm_ref, edge_x, y_rows, comps):
    layers, rows, cols = perm_ref.shape
    here = slice(y, y + TILE)
    lane = lax.broadcasted_iota(jnp.int32, (TILE, cols), 1)
    is_first, is_last = lane == 0, lane == cols - 1
    at_low = 2 * (layers * comps + k)
    perm_low = pltpu.roll(edge_x[here], lax.rem(cols - at_low, cols), 1)
    perm_high = pltpu.roll(edge_x[here], lax.rem(2 * cols - at_low - 2, cols), 1)
    centre = perm_ref[k, here]
    low_y, high_y = beside_y(perm_ref, (k,), y, y_rows)
    to_left = weight(centre, jnp.where(is_first, perm_low, pltpu.roll(centre, 1, 1)))
    to_right = weight(centre, jnp.where(is_last, perm_high, pltpu.roll(centre, cols - 1, 1)))
    return [
        jnp.where(k < layers - 1, weight(centre, perm_ref[jnp.minimum(k + 1, layers - 1), here]), 0.0),
        jnp.where(k > 0, weight(centre, perm_ref[jnp.maximum(k - 1, 0), here]), 0.0),
        weight(centre, high_y),
        weight(centre, low_y),
        jnp.where(is_last, 0.0, to_right),
        jnp.where(is_first, 0.0, to_left),
        jnp.where(is_first, to_left, jnp.where(is_last, to_right, 0.0)),
    ]


def beside_y(ref, index, y, y_rows):
    rows, cols = ref.shape[-2:]
    row = lax.broadcasted_iota(jnp.int32, (TILE, cols), 0)
    if y > 0:
        low = ref[(*index, slice(y - 1, y - 1 + TILE))]
    else:
        low = jnp.where(row == 0, y_rows[0], pltpu.roll(ref[(*index, slice(0, TILE))], 1, 0))
    if y + TILE < rows:
        high = ref[(*index, slice(y + 1, y + 1 + TILE))]
    else:
        high = jnp.where(row == TILE - 1, y_rows[1], pltpu.roll(ref[(*index, slice(y, y + TILE))], TILE - 1, 0))
    return low, high


def apply_kernel(is_first_apply, is_inner, *refs):
    names = ["field", "masked", "mask", "place", "x_1", "x_0", "diag", "flux"]
    names += ["perm"] if is_first_apply else ["weights"]
    names += [] if is_inner else ["y_0", "y_1", "inner", "begun"]
    names += ["out"] if is_inner or is_first_apply else ["out_hbm"]
    names += ["begun"] if is_inner else []
    if is_first_apply:
        names += [] if is_inner else ["rounded"]
        names += ["weights"]
    names += ["edge_x", "turned", "beside_x"]
    names += [] if is_inner or is_first_apply else ["out", "sems"]
    ref = dict(zip(names, refs, strict=True))
    field_ref, masked_ref, edge_x, place = ref["field"], ref["masked"], ref["edge_x"], ref["place"]
    layers, comps, rows, cols = field_ref.shape
    diag_ref, flux_ref = ref["diag"], ref["flux"]
    tiles = list(range(TILE, rows - TILE, TILE)) if is_inner else [0, rows - TILE]
    here_rows = len(tiles) * TILE

    def out_copies(k):
        middle = slice(TILE, rows - TILE)
        pairs = [(ref["inner"].at[k], ref["out_hbm"].at[k, :, middle])]
        pairs += [
            (ref["out"].at[k, :, j * TILE : (j + 1) * TILE], ref["out_hbm"].at[k, :, y : y + TILE]) for j, y in enumerate(tiles)
        ]
        return [pltpu.make_async_copy(a, b, ref["sems"].at[j, k]) for j, (a, b) in enumerate(pairs)]

    lane = lax.broadcasted_iota(jnp.int32, (rows, cols), 1)
    even_x = lax.axis_index("gx") % 2 == 0
    even_y = lax.axis_index("gy") % 2 == 0
    edge_x[...] = jnp.where((lane % 2 == 0) == even_x, ref["x_1"][...].astype(F32), ref["x_0"][...].astype(F32))
    for k in range(layers):
        for j, y in enumerate(tiles):
            start = k * here_rows + j * TILE
            piece = pltpu.roll(edge_x[y : y + TILE], (cols - 2 * comps * k) % cols, 1)
            ref["turned"][start : start + TILE] = piece.astype(BF16)
    ref["beside_x"][...] = jnp.dot(ref["turned"][...], place[...], preferred_element_type=F32)

    def layer(k, carry):
        above = jnp.minimum(k + 1, layers - 1)
        below = jnp.maximum(k - 1, 0)
        rows_y, perm_y = None, None
        if not is_inner:
            odd = k % 2 == 1
            here = pl.ds(pl.multiple_of(16 * (k // 2), 16), 16)
            sides = [ref[name][here].astype(F32) for name in ("y_0", "y_1")]
            sides = [jnp.where(odd, side[comps:], side[:comps]) for side in sides]
            rows_y = (jnp.where(even_y, sides[1], sides[0]), jnp.where(even_y, sides[0], sides[1]))
        if is_first_apply and not is_inner:
            here = slice(layers * comps, layers * comps + 16)
            mine = lax.broadcasted_iota(jnp.int32, (16, cols), 0) == k
            sides = [
                jnp.sum(jnp.where(mine, ref[name][here].astype(F32), 0.0), axis=0, keepdims=True) for name in ("y_0", "y_1")
            ]
            perm_y = (jnp.where(even_y, sides[1], sides[0]), jnp.where(even_y, sides[0], sides[1]))
        for j, y in enumerate(tiles):
            here, local = slice(y, y + TILE), slice(j * TILE, (j + 1) * TILE)
            side_rows = pl.ds(pl.multiple_of(k * here_rows + j * TILE, TILE), TILE)
            if is_first_apply:
                weights = tile_weights(k, y, ref["perm"], edge_x, perm_y, comps)
                for number, value in enumerate(weights):
                    ref["weights"][k, number, local] = value
            else:
                weights = [ref["weights"][k, number, local] for number in range(WEIGHTS)]
            total = [None] * comps
            for r in range(comps):
                own = masked_ref[k, r, here]
                low, high = beside_y(masked_ref, (k, r), y, None if is_inner else [side[r : r + 1] for side in rows_y])
                summed = (
                    weights[0] * masked_ref[above, r, here]
                    + weights[1] * masked_ref[below, r, here]
                    + weights[2] * high
                    + weights[3] * low
                    + weights[4] * pltpu.roll(own, cols - 1, 1)
                    + weights[5] * pltpu.roll(own, 1, 1)
                    + weights[6] * ref["beside_x"][side_rows, r * cols : (r + 1) * cols]
                )
                for c in range(comps):
                    term = -flux_ref[k, r, c, here].astype(F32) * summed
                    if is_inner:
                        term = diag_ref[k, r, c, here].astype(F32) * own + term
                    total[c] = term if r == 0 else total[c] + term
            well = ref["mask"][here].astype(F32) if is_inner else None
            for c in range(comps):
                value = total[c] + (well * field_ref[k, c, here] if is_inner else ref["begun"][k, c, local])
                if is_first_apply and not is_inner:
                    ref["out"][k, c, here] = value
                    columns = pl.ds(pl.multiple_of(k * cols, cols), cols)
                    ref["rounded"][c * rows + y : c * rows + y + TILE, columns] = value.astype(BF16)
                else:
                    ref["out"][k, c, local] = value
        for j, y in enumerate([0, rows - TILE] if is_inner else []):
            here, local = slice(y, y + TILE), slice(j * TILE, (j + 1) * TILE)
            well = ref["mask"][here].astype(F32)
            total = [well * field_ref[k, c, here] for c in range(comps)]
            for r in range(comps):
                own = masked_ref[k, r, here]
                for c in range(comps):
                    total[c] += diag_ref[k, r, c, here].astype(F32) * own
            for c in range(comps):
                ref["begun"][k, c, local] = total[c]
        if is_first_apply and not is_inner:
            columns = pl.ds(pl.multiple_of(k * cols, cols), cols)
            for c in range(comps):
                value = ref["inner"][k, c]
                ref["out"][k, c, TILE : rows - TILE] = value
                ref["rounded"][c * rows + TILE : (c + 1) * rows - TILE, columns] = value.astype(BF16)
        if not is_first_apply and not is_inner:
            for copy in out_copies(k):
                copy.start()
        return carry

    unrolled(layers, 2, layer)
    if not is_first_apply and not is_inner:
        for k in range(layers):
            for copy in out_copies(k):
                copy.wait()


def apply_rows(is_first_apply, is_inner, field, masked, mask, place, halos, blocks, third, *inner):
    layers, comps, rows, cols = field.shape
    vmem = pl.BlockSpec(memory_space=pltpu.VMEM)
    hbm = pl.BlockSpec(memory_space=pltpu.HBM)
    here_rows = rows - 2 * TILE if is_inner else 2 * TILE
    here = (layers, comps, here_rows, cols)
    arrays = [field, masked, mask, place, halos[1], halos[0], *blocks, third]
    specs = [vmem] * 9
    if not is_inner:
        arrays += [*halos[2:], *inner]
        specs += [vmem] * 4
    if is_inner:
        begun = (layers, comps, 2 * TILE, cols)
        out_shape, out_specs = [pltpu.VMEM(here, F32), pltpu.VMEM(begun, F32)], [vmem] * 2
    else:
        out_shape = [jax.ShapeDtypeStruct(field.shape, F32)]
        out_specs = [vmem if is_first_apply else hbm]
    if is_first_apply:
        if not is_inner:
            out_shape.append(jax.ShapeDtypeStruct((comps * rows, layers * cols), BF16))
        out_shape.append(pltpu.VMEM((layers, WEIGHTS, here_rows, cols), F32))
        out_specs = [vmem] * len(out_shape)
    scratch = [
        pltpu.VMEM((rows, cols), F32),
        pltpu.VMEM((layers * here_rows, cols), BF16),
        pltpu.VMEM((layers * here_rows, comps * cols), F32),
    ]
    if not is_first_apply and not is_inner:
        scratch += [pltpu.VMEM(here, F32), pltpu.SemaphoreType.DMA((3, layers))]
    size = layers * comps * comps * here_rows * cols
    return pl.pallas_call(
        functools.partial(apply_kernel, is_first_apply, is_inner),
        in_specs=specs,
        out_specs=out_specs,
        out_shape=out_shape,
        scratch_shapes=scratch,
        compiler_params=params(16),
        cost_estimate=cost(8 * size, 4 * size + 8 * field.size),
    )(*arrays)


def split_cells(cells, rows, cols):
    layer = cells // (rows * cols)
    y = (cells // cols) % rows
    return layer * cols + cells % cols, y


def unrolled(count, together, body):
    def group(i, carry):
        for j in range(together):
            body(i * together + j, None)
        return carry

    together = math.gcd(count, together)
    lax.fori_loop(0, count // together, group, 0)


def one_hot(column, count, slots):
    number = lax.broadcasted_iota(jnp.int32, (count, slots), 0)
    return jnp.where(number == column, 1.0, 0.0).astype(BF16)


def gather_kernel(rows, cols, helper_ref, count_ref, cells_ref, rounded_ref, sent_ref, kept_ref=None):
    chunks, _, slots = cells_ref.shape
    comps, width = sent_ref.shape[1:]
    per_chunk = slots // width
    row_number = lax.broadcasted_iota(jnp.int32, (rows, slots), 0)

    def one(i, carry):
        column, y = split_cells(cells_ref[i], rows, cols)
        chosen = one_hot(column, rounded_ref.shape[1], slots)
        if kept_ref is not None:
            kept_ref[:, pl.ds(pl.multiple_of(i * slots, slots), slots)] = chosen
        found = jnp.dot(rounded_ref[...], chosen, preferred_element_type=F32)
        at_row = row_number == y
        values = [
            jnp.sum(jnp.where(at_row, found[c * rows : (c + 1) * rows], 0.0), axis=0, keepdims=True)
            for c in range(comps)
        ]
        values = jnp.concatenate(values, axis=0)
        for j in range(per_chunk):
            b = i * per_chunk + j
            live = jnp.where(b < count_ref[0, 0], 1.0, 0.0)
            sent_ref[helper_ref[0, 0, b]] = (values[:, j * width : (j + 1) * width] * live).astype(BF16)
        return carry

    unrolled(chunks, 4, one)


def gather(rounded, cells, helper, count, comps, rows, cols, width):
    blocks = helper.shape[-1]
    smem = pl.BlockSpec(memory_space=pltpu.SMEM)
    vmem = pl.BlockSpec(memory_space=pltpu.VMEM)
    out_shape = [jax.ShapeDtypeStruct((blocks, comps, width), BF16)]
    if rounded.shape[1] * cells.size * 2 <= KEPT_BYTES:
        out_shape.append(pltpu.VMEM((rounded.shape[1], cells.size), BF16))
    return pl.pallas_call(
        functools.partial(gather_kernel, rows, cols),
        in_specs=[smem, smem, vmem, vmem],
        out_specs=[vmem] * len(out_shape),
        out_shape=out_shape,
        compiler_params=params(16),
        cost_estimate=cost(2 * rounded.size * cells.size, 2 * rounded.size),
    )(helper, count, cells, rounded)


PARTS = 3


def helper_kernel(inverse_ref, coupling_ref, state_ref, picked_ref, reply_ref):
    blocks, comps = inverse_ref.shape[:2]
    width = inverse_ref.shape[-1]

    def transposed(block_ref, b, value):
        block = block_ref[b].astype(F32)
        total = block[0] * value[0:1]
        for r in range(1, comps):
            total += block[r] * value[r : r + 1]
        return total

    def one(b, totals):
        multiplier = transposed(inverse_ref, b, picked_ref[b].astype(F32))
        state = state_ref[b].astype(F32)
        part = multiplier * state
        correction = -transposed(coupling_ref, b, multiplier)
        reply_ref[b, 0:comps] = correction.astype(BF16)
        return tuple(totals[j] + part * state[j : j + 1] for j in range(comps))

    totals = lax.fori_loop(0, blocks, one, (jnp.zeros((comps, width), F32),) * comps)
    lane = lax.broadcasted_iota(jnp.int32, (comps, width), 1)
    rest = jnp.zeros((comps, width), F32)
    for j in range(comps):
        column = jnp.sum(totals[j], axis=1, keepdims=True)
        rest = jnp.where(lane % comps == j, column, rest)
    packed = jnp.zeros((comps, width), F32)
    for part in range(PARTS):
        rounded = rest.astype(BF16).astype(F32)
        packed = jnp.where(lane // comps == part, rounded, packed)
        rest = rest - rounded
    packed = packed.astype(BF16)
    for b in range(blocks):
        reply_ref[b, comps : 2 * comps] = packed


def at_helper(inverse, coupling, state, picked):
    blocks, comps, _, width = inverse.shape
    return pl.pallas_call(
        helper_kernel,
        out_shape=jax.ShapeDtypeStruct((blocks, 2 * comps, width), BF16),
        compiler_params=params(16),
        cost_estimate=cost(4 * inverse.size, 4 * inverse.size),
    )(inverse, coupling, state, picked)


def scatter_kernel(scale, has_kept, helper_ref, cells_ref, back_ref, first_ref, mask_ref, *refs):
    kept_ref = refs[0] if has_kept else None
    second_ref, masked_ref, *sends, grad_ref, added, side_y = refs[has_kept:]
    layers, comps, rows, cols = first_ref.shape
    chunks, _, slots = cells_ref.shape
    width = back_ref.shape[-1]
    per_chunk = slots // width
    row_number = lax.broadcasted_iota(jnp.int32, (rows, slots), 0)
    for k in range(layers):
        for c in range(comps):
            added[c * rows : (c + 1) * rows, k * cols : (k + 1) * cols] = first_ref[k, c]

    def one(i, carry):
        column, y = split_cells(cells_ref[i], rows, cols)
        if has_kept:
            chosen = kept_ref[:, pl.ds(pl.multiple_of(i * slots, slots), slots)]
        else:
            chosen = one_hot(column, added.shape[1], slots)
        parts = [back_ref[helper_ref[0, 0, i * per_chunk + j]].astype(F32)[:comps] for j in range(per_chunk)]
        correction = jnp.concatenate(parts, axis=1)
        at_row = row_number == y
        spread = jnp.concatenate(
            [jnp.where(at_row, correction[c : c + 1], 0.0).astype(BF16) for c in range(comps)], axis=0
        )
        added[...] += lax.dot_general(spread, chosen, (((1,), (1,)), ((), ())), preferred_element_type=F32)
        return carry

    unrolled(chunks, 2, one)
    for k in range(layers):
        for c in range(comps):
            second_ref[k, c] = added[c * rows : (c + 1) * rows, k * cols : (k + 1) * cols]
    write_edges(second_ref, mask_ref, None, masked_ref, side_y, sends)
    total = back_ref[0].astype(F32)[comps:]
    for b in range(1, back_ref.shape[0]):
        total += back_ref[b].astype(F32)[comps:]
    whole = total
    for part in range(1, PARTS):
        whole += pltpu.roll(total, width - part * comps, 1)
    grad_ref[...] = (whole * scale)[:, :comps]


def scatter(first, back, helper, cells, mask, kept, scale):
    layers, comps, rows, cols = first.shape
    smem = pl.BlockSpec(memory_space=pltpu.SMEM)
    vmem = pl.BlockSpec(memory_space=pltpu.VMEM)
    edges = edge_shapes(*first.shape)
    return pl.pallas_call(
        functools.partial(scatter_kernel, scale, len(kept)),
        in_specs=[smem] + [vmem] * (4 + len(kept)),
        out_specs=[vmem] * (3 + len(edges)),
        out_shape=[
            pltpu.VMEM(first.shape, F32),
            pltpu.VMEM(first.shape, F32),
            *edges,
            jax.ShapeDtypeStruct((comps, comps), F32),
        ],
        scratch_shapes=[pltpu.VMEM((comps * rows, layers * cols), F32), edge_scratch(layers, comps, cols)],
        compiler_params=params(24),
        cost_estimate=cost(2 * first.size * cells.size, 8 * first.size),
    )(helper, cells, back, first, mask, *kept)


def shards(
    cotangent,
    permeability,
    well_mask,
    diag_block,
    flux_block,
    cell_list,
    block_count,
    helper_of,
    flash_inverse,
    flash_coupling,
    phase_state,
):
    layers, comps, rows, cols = cotangent.shape
    slots, width = helper_of.shape[-1], flash_inverse.shape[-1]
    inverse = flash_inverse.reshape(slots, comps, comps, width)
    coupling = flash_coupling.reshape(slots, comps, comps, width)
    state = phase_state.reshape(slots, comps, width)

    def cells(chunk):
        return cell_list.reshape(-1, 1, min(chunk, cell_list.shape[-1]))

    def to_partners(array):
        return lax.all_to_all(array, AXES, split_axis=0, concat_axis=0, tiled=True)

    *sides, masked, field, mask, perm, place = opening(cotangent, well_mask, permeability, diag_block, flux_block)
    halos = exchange(*sides)
    blocks = [pltpu.with_memory_space_constraint(block, pltpu.VMEM) for block in (diag_block, flux_block)]
    inner, begun, inner_weights = apply_rows(True, True, field, masked, mask, place, halos, blocks, perm)
    first, rounded, outer_weights = apply_rows(
        True, False, field, masked, mask, place, halos, blocks, perm, inner, begun
    )
    sent, *chosen = gather(rounded, cells(GATHER_CHUNK), helper_of, block_count, comps, rows, cols, width)
    reply = at_helper(inverse, coupling, state, to_partners(sent))
    devices = lax.axis_size("gx") * lax.axis_size("gy")
    scale = -1.0 / math.sqrt(width * devices * devices)
    second, masked, *sides, interaction_grad = scatter(
        first, to_partners(reply), helper_of, cells(SCATTER_CHUNK), mask, chosen, scale
    )
    halos = exchange(*sides)
    inner, begun = apply_rows(False, True, second, masked, mask, place, halos, blocks, inner_weights)
    (adjoint,) = apply_rows(False, False, second, masked, mask, place, halos, blocks, outer_weights, inner, begun)
    return (adjoint, interaction_grad)


def solution(mesh):
    return jax.shard_map(
        shards,
        mesh=mesh,
        in_specs=(
            P(None, None, "gy", "gx"),
            P(None, "gy", "gx"),
            P("gy", "gx"),
            P(None, None, None, "gy", "gx"),
            P(None, None, None, "gy", "gx"),
            P("gy", "gx", None),
            P("gy", "gx"),
            P("gy", "gx", None),
            P("gy", "gx", None, None, None, None),
            P("gy", "gx", None, None, None, None),
            P("gy", "gx", None, None, None),
        ),
        out_specs=(P(None, None, "gy", "gx"), P()),
        check_vma=False,
    )
```

```python
import functools
import math

import jax
import jax.numpy as jnp
from jax import lax
from jax.experimental import pallas as pl
from jax.experimental.pallas import tpu as pltpu
from jax.sharding import PartitionSpec as P

F32 = jnp.float32
BF16 = jnp.bfloat16
AXES = ("gx", "gy")
MIB = 1024 * 1024
GATHER_CHUNK, SCATTER_CHUNK = 512, 2048
KEPT_BYTES = 8 * MIB


def params(mib):
    return pltpu.CompilerParams(vmem_limit_bytes=mib * MIB)


def cost(flops, moved):
    return pl.CostEstimate(flops=int(flops), bytes_accessed=int(moved), transcendentals=0)


def round_up(number, step):
    return -(-number // step) * step


def write_edges(field_ref, mask_ref, perm_ref, masked_ref, side_y, sends):
    send_y_0, send_y_1, send_x = sends
    layers, comps, rows, cols = field_ref.shape
    with_perm = perm_ref is not None
    clear = 1.0 - mask_ref[...].astype(F32)
    lane = lax.broadcasted_iota(jnp.int32, (rows, cols), 1)
    pair = lane // 2
    along_x = jnp.zeros((rows, cols), F32)
    side_y[...] = jnp.zeros_like(side_y)
    for k in range(layers):
        for c in range(comps + with_perm):
            if c < comps:
                value, at = field_ref[k, c] * clear, k * comps + c
                masked_ref[k, c] = value
            else:
                value, at = perm_ref[k], layers * comps + k
            side_y[0, at : at + 1, :] = value[0:1]
            side_y[1, at : at + 1, :] = value[rows - 1 : rows]
            along_x = jnp.where(pair == at, pltpu.roll(value, (2 * at + 1) % cols, 1), along_x)
    even = lax.axis_index("gy") % 2 == 0
    send_x[...] = along_x.astype(BF16)
    low, high = side_y[0].astype(BF16), side_y[1].astype(BF16)
    send_y_0[...] = jnp.where(even, high, low)
    send_y_1[...] = jnp.where(even, low, high)


def write_place(place_ref):
    cols, width = place_ref.shape
    number = lax.broadcasted_iota(jnp.int32, (cols, cols), 0)
    spot = lax.broadcasted_iota(jnp.int32, (cols, cols), 1)
    for r in range(width // cols):
        taken = ((number == 2 * r) & (spot == 0)) | ((number == 2 * r + 1) & (spot == cols - 1))
        place_ref[:, r * cols : (r + 1) * cols] = jnp.where(taken, 1.0, 0.0).astype(BF16)


def opening_kernel(
    field_hbm, mask_hbm, perm_hbm, diag_hbm, flux_hbm,
    send_y_0, send_y_1, send_x, masked_ref, field_ref, mask_ref, perm_ref, place_ref,
    side_y, sems,
):
    pairs = [(mask_hbm, mask_ref), (perm_hbm, perm_ref)]
    pairs.append((field_hbm, field_ref))
    copies = [pltpu.make_async_copy(a, b, sems.at[i]) for i, (a, b) in enumerate(pairs)]
    for copy in copies:
        copy.start()
    write_place(place_ref)
    for copy in copies:
        copy.wait()
    write_edges(field_ref, mask_ref, perm_ref, masked_ref, side_y, (send_y_0, send_y_1, send_x))


def edge_rows(layers, comps):
    return round_up(layers * (comps + 1), 16)


def edge_shapes(layers, comps, rows, cols):
    along_y = (edge_rows(layers, comps), cols)
    return [jax.ShapeDtypeStruct(shape, BF16) for shape in (along_y, along_y, (rows, cols))]


def edge_scratch(layers, comps, cols):
    return pltpu.VMEM((2, edge_rows(layers, comps), cols), F32)


def opening(field, mask, perm, diag, flux):
    layers, comps, rows, cols = field.shape
    hbm = pl.BlockSpec(memory_space=pltpu.HBM)
    vmem = pl.BlockSpec(memory_space=pltpu.VMEM)
    kept = [(array.shape, array.dtype) for array in (field, field, mask, perm)]
    kept.append(((cols, comps * cols), BF16))
    return pl.pallas_call(
        opening_kernel,
        in_specs=[hbm] * 5,
        out_specs=[vmem] * 8,
        out_shape=[*edge_shapes(*field.shape), *(pltpu.VMEM(*item) for item in kept)],
        scratch_shapes=[edge_scratch(layers, comps, cols), pltpu.SemaphoreType.DMA((3,))],
        compiler_params=params(16),
        cost_estimate=cost(4 * field.size, 8 * field.size),
    )(*(pltpu.with_memory_space_constraint(array, pltpu.HBM) for array in (field, mask, perm, diag, flux)))


def exchange(send_y_0, send_y_1, send_x):
    def swaps(axis, first, second):
        count = lax.axis_size(axis)
        results = []
        for start, array in ((0, first), (1, second)):
            pairs = [(i, i + 1) for i in range(start, count - 1, 2)]
            results.append(lax.ppermute(array, axis, pairs + [(j, i) for i, j in pairs]))
        return results

    return (*swaps("gx", send_x, send_x), *swaps("gy", send_y_0, send_y_1))


TILE = 16
WEIGHTS = 7


def reciprocal(value):
    guess = pl.reciprocal(value, approx=True)
    return guess * (2.0 - value * guess)


def weight(centre, beside):
    return 2.0 * centre * beside * reciprocal(centre + beside)


def tile_weights(k, y, perm_ref, edge_x, y_rows, comps):
    layers, rows, cols = perm_ref.shape
    here = slice(y, y + TILE)
    lane = lax.broadcasted_iota(jnp.int32, (TILE, cols), 1)
    is_first, is_last = lane == 0, lane == cols - 1
    at_low = 2 * (layers * comps + k)
    perm_low = pltpu.roll(edge_x[here], lax.rem(cols - at_low, cols), 1)
    perm_high = pltpu.roll(edge_x[here], lax.rem(2 * cols - at_low - 2, cols), 1)
    centre = perm_ref[k, here]
    low_y, high_y = beside_y(perm_ref, (k,), y, y_rows)
    to_left = weight(centre, jnp.where(is_first, perm_low, pltpu.roll(centre, 1, 1)))
    to_right = weight(centre, jnp.where(is_last, perm_high, pltpu.roll(centre, cols - 1, 1)))
    return [
        jnp.where(k < layers - 1, weight(centre, perm_ref[jnp.minimum(k + 1, layers - 1), here]), 0.0),
        jnp.where(k > 0, weight(centre, perm_ref[jnp.maximum(k - 1, 0), here]), 0.0),
        weight(centre, high_y),
        weight(centre, low_y),
        jnp.where(is_last, 0.0, to_right),
        jnp.where(is_first, 0.0, to_left),
        jnp.where(is_first, to_left, jnp.where(is_last, to_right, 0.0)),
    ]


def beside_y(ref, index, y, y_rows):
    rows, cols = ref.shape[-2:]
    row = lax.broadcasted_iota(jnp.int32, (TILE, cols), 0)
    if y > 0:
        low = ref[(*index, slice(y - 1, y - 1 + TILE))]
    else:
        low = jnp.where(row == 0, y_rows[0], pltpu.roll(ref[(*index, slice(0, TILE))], 1, 0))
    if y + TILE < rows:
        high = ref[(*index, slice(y + 1, y + 1 + TILE))]
    else:
        high = jnp.where(row == TILE - 1, y_rows[1], pltpu.roll(ref[(*index, slice(y, y + TILE))], TILE - 1, 0))
    return low, high


def apply_kernel(is_first_apply, is_inner, *refs):
    names = ["field", "masked", "mask", "place", "x_1", "x_0", "diag", "flux"]
    names += ["perm"] if is_first_apply else ["weights"]
    names += [] if is_inner else ["y_0", "y_1", "inner", "begun"]
    names += ["out"] if is_inner or is_first_apply else ["out_hbm"]
    names += ["begun"] if is_inner else []
    if is_first_apply:
        names += [] if is_inner else ["rounded"]
        names += ["weights"]
    names += ["edge_x", "turned", "beside_x"]
    names += [] if is_inner or is_first_apply else ["out", "sems"]
    ref = dict(zip(names, refs, strict=True))
    field_ref, masked_ref, edge_x, place = ref["field"], ref["masked"], ref["edge_x"], ref["place"]
    layers, comps, rows, cols = field_ref.shape
    diag_ref, flux_ref = ref["diag"], ref["flux"]
    tiles = list(range(TILE, rows - TILE, TILE)) if is_inner else [0, rows - TILE]
    here_rows = len(tiles) * TILE

    def out_copies(k):
        middle = slice(TILE, rows - TILE)
        pairs = [(ref["inner"].at[k], ref["out_hbm"].at[k, :, middle])]
        pairs += [
            (ref["out"].at[k, :, j * TILE : (j + 1) * TILE], ref["out_hbm"].at[k, :, y : y + TILE]) for j, y in enumerate(tiles)
        ]
        return [pltpu.make_async_copy(a, b, ref["sems"].at[j, k]) for j, (a, b) in enumerate(pairs)]

    lane = lax.broadcasted_iota(jnp.int32, (rows, cols), 1)
    even_x = lax.axis_index("gx") % 2 == 0
    even_y = lax.axis_index("gy") % 2 == 0
    edge_x[...] = jnp.where((lane % 2 == 0) == even_x, ref["x_1"][...].astype(F32), ref["x_0"][...].astype(F32))
    for k in range(layers):
        for j, y in enumerate(tiles):
            start = k * here_rows + j * TILE
            piece = pltpu.roll(edge_x[y : y + TILE], (cols - 2 * comps * k) % cols, 1)
            ref["turned"][start : start + TILE] = piece.astype(BF16)
    ref["beside_x"][...] = jnp.dot(ref["turned"][...], place[...], preferred_element_type=F32)

    def layer(k, carry):
        above = jnp.minimum(k + 1, layers - 1)
        below = jnp.maximum(k - 1, 0)
        rows_y, perm_y = None, None
        if not is_inner:
            odd = k % 2 == 1
            here = pl.ds(pl.multiple_of(16 * (k // 2), 16), 16)
            sides = [ref[name][here].astype(F32) for name in ("y_0", "y_1")]
            sides = [jnp.where(odd, side[comps:], side[:comps]) for side in sides]
            rows_y = (jnp.where(even_y, sides[1], sides[0]), jnp.where(even_y, sides[0], sides[1]))
        if is_first_apply and not is_inner:
            here = slice(layers * comps, layers * comps + 16)
            mine = lax.broadcasted_iota(jnp.int32, (16, cols), 0) == k
            sides = [
                jnp.sum(jnp.where(mine, ref[name][here].astype(F32), 0.0), axis=0, keepdims=True) for name in ("y_0", "y_1")
            ]
            perm_y = (jnp.where(even_y, sides[1], sides[0]), jnp.where(even_y, sides[0], sides[1]))
        for j, y in enumerate(tiles):
            here, local = slice(y, y + TILE), slice(j * TILE, (j + 1) * TILE)
            side_rows = pl.ds(pl.multiple_of(k * here_rows + j * TILE, TILE), TILE)
            if is_first_apply:
                weights = tile_weights(k, y, ref["perm"], edge_x, perm_y, comps)
                for number, value in enumerate(weights):
                    ref["weights"][k, number, local] = value
            else:
                weights = [ref["weights"][k, number, local] for number in range(WEIGHTS)]
            total = [None] * comps
            for r in range(comps):
                own = masked_ref[k, r, here]
                low, high = beside_y(masked_ref, (k, r), y, None if is_inner else [side[r : r + 1] for side in rows_y])
                summed = (
                    weights[0] * masked_ref[above, r, here]
                    + weights[1] * masked_ref[below, r, here]
                    + weights[2] * high
                    + weights[3] * low
                    + weights[4] * pltpu.roll(own, cols - 1, 1)
                    + weights[5] * pltpu.roll(own, 1, 1)
                    + weights[6] * ref["beside_x"][side_rows, r * cols : (r + 1) * cols]
                )
                for c in range(comps):
                    term = -flux_ref[k, r, c, here].astype(F32) * summed
                    if is_inner:
                        term = diag_ref[k, r, c, here].astype(F32) * own + term
                    total[c] = term if r == 0 else total[c] + term
            well = ref["mask"][here].astype(F32) if is_inner else None
            for c in range(comps):
                value = total[c] + (well * field_ref[k, c, here] if is_inner else ref["begun"][k, c, local])
                if is_first_apply and not is_inner:
                    ref["out"][k, c, here] = value
                    columns = pl.ds(pl.multiple_of(k * cols, cols), cols)
                    ref["rounded"][c * rows + y : c * rows + y + TILE, columns] = value.astype(BF16)
                else:
                    ref["out"][k, c, local] = value
        for j, y in enumerate([0, rows - TILE] if is_inner else []):
            here, local = slice(y, y + TILE), slice(j * TILE, (j + 1) * TILE)
            well = ref["mask"][here].astype(F32)
            total = [well * field_ref[k, c, here] for c in range(comps)]
            for r in range(comps):
                own = masked_ref[k, r, here]
                for c in range(comps):
                    total[c] += diag_ref[k, r, c, here].astype(F32) * own
            for c in range(comps):
                ref["begun"][k, c, local] = total[c]
        if is_first_apply and not is_inner:
            columns = pl.ds(pl.multiple_of(k * cols, cols), cols)
            for c in range(comps):
                value = ref["inner"][k, c]
                ref["out"][k, c, TILE : rows - TILE] = value
                ref["rounded"][c * rows + TILE : (c + 1) * rows - TILE, columns] = value.astype(BF16)
        if not is_first_apply and not is_inner:
            for copy in out_copies(k):
                copy.start()
        return carry

    unrolled(layers, 3, layer)
    if not is_first_apply and not is_inner:
        for k in range(layers):
            for copy in out_copies(k):
                copy.wait()


def apply_rows(is_first_apply, is_inner, field, masked, mask, place, halos, blocks, third, *inner):
    layers, comps, rows, cols = field.shape
    vmem = pl.BlockSpec(memory_space=pltpu.VMEM)
    hbm = pl.BlockSpec(memory_space=pltpu.HBM)
    here_rows = rows - 2 * TILE if is_inner else 2 * TILE
    here = (layers, comps, here_rows, cols)
    arrays = [field, masked, mask, place, halos[1], halos[0], *blocks, third]
    specs = [vmem] * 9
    if not is_inner:
        arrays += [*halos[2:], *inner]
        specs += [vmem] * 4
    if is_inner:
        begun = (layers, comps, 2 * TILE, cols)
        out_shape, out_specs = [pltpu.VMEM(here, F32), pltpu.VMEM(begun, F32)], [vmem] * 2
    else:
        out_shape = [jax.ShapeDtypeStruct(field.shape, F32)]
        out_specs = [vmem if is_first_apply else hbm]
    if is_first_apply:
        if not is_inner:
            out_shape.append(jax.ShapeDtypeStruct((comps * rows, layers * cols), BF16))
        out_shape.append(pltpu.VMEM((layers, WEIGHTS, here_rows, cols), F32))
        out_specs = [vmem] * len(out_shape)
    scratch = [
        pltpu.VMEM((rows, cols), F32),
        pltpu.VMEM((layers * here_rows, cols), BF16),
        pltpu.VMEM((layers * here_rows, comps * cols), F32),
    ]
    if not is_first_apply and not is_inner:
        scratch += [pltpu.VMEM(here, F32), pltpu.SemaphoreType.DMA((3, layers))]
    size = layers * comps * comps * here_rows * cols
    return pl.pallas_call(
        functools.partial(apply_kernel, is_first_apply, is_inner),
        in_specs=specs,
        out_specs=out_specs,
        out_shape=out_shape,
        scratch_shapes=scratch,
        compiler_params=params(16),
        cost_estimate=cost(8 * size, 4 * size + 8 * field.size),
    )(*arrays)


def split_cells(cells, rows, cols):
    layer = cells // (rows * cols)
    y = (cells // cols) % rows
    return layer * cols + cells % cols, y


def unrolled(count, together, body):
    def group(i, carry):
        for j in range(together):
            body(i * together + j, None)
        return carry

    together = math.gcd(count, together)
    if together == count:
        group(0, None)
    else:
        lax.fori_loop(0, count // together, group, 0)


def stretch(i, size):
    return pl.ds(i * size if isinstance(i, int) else pl.multiple_of(i * size, size), size)


def one_hot(column, count, slots):
    number = lax.broadcasted_iota(jnp.int32, (count, slots), 0)
    return jnp.where(number == column, 1.0, 0.0).astype(BF16)


def gather_kernel(rows, cols, helper_ref, count_ref, cells_ref, rounded_ref, sent_ref, kept_ref=None):
    chunks, _, slots = cells_ref.shape
    comps, width = sent_ref.shape[1:]
    per_chunk = slots // width
    row_number = lax.broadcasted_iota(jnp.int32, (rows, slots), 0)

    def one(i, carry):
        column, y = split_cells(cells_ref[i], rows, cols)
        chosen = one_hot(column, rounded_ref.shape[1], slots)
        if kept_ref is not None:
            kept_ref[:, stretch(i, slots)] = chosen
        found = jnp.dot(rounded_ref[...], chosen, preferred_element_type=F32)
        at_row = row_number == y
        values = [
            jnp.sum(jnp.where(at_row, found[c * rows : (c + 1) * rows], 0.0), axis=0, keepdims=True)
            for c in range(comps)
        ]
        values = jnp.concatenate(values, axis=0)
        for j in range(per_chunk):
            b = i * per_chunk + j
            live = jnp.where(b < count_ref[0, 0], 1.0, 0.0)
            sent_ref[helper_ref[0, 0, b]] = (values[:, j * width : (j + 1) * width] * live).astype(BF16)
        return carry

    unrolled(chunks, 8, one)


def gather(rounded, cells, helper, count, comps, rows, cols, width):
    blocks = helper.shape[-1]
    smem = pl.BlockSpec(memory_space=pltpu.SMEM)
    vmem = pl.BlockSpec(memory_space=pltpu.VMEM)
    out_shape = [jax.ShapeDtypeStruct((blocks, comps, width), BF16)]
    if rounded.shape[1] * cells.size * 2 <= KEPT_BYTES:
        out_shape.append(pltpu.VMEM((rounded.shape[1], cells.size), BF16))
    return pl.pallas_call(
        functools.partial(gather_kernel, rows, cols),
        in_specs=[smem, smem, vmem, vmem],
        out_specs=[vmem] * len(out_shape),
        out_shape=out_shape,
        compiler_params=params(16),
        cost_estimate=cost(2 * rounded.size * cells.size, 2 * rounded.size),
    )(helper, count, cells, rounded)


PARTS = 3


def helper_kernel(inverse_ref, coupling_ref, state_ref, picked_ref, reply_ref):
    blocks, comps = inverse_ref.shape[:2]
    width = inverse_ref.shape[-1]

    def transposed(block_ref, b, value):
        block = block_ref[b].astype(F32)
        total = block[0] * value[0:1]
        for r in range(1, comps):
            total += block[r] * value[r : r + 1]
        return total

    def one(b, totals):
        multiplier = transposed(inverse_ref, b, picked_ref[b].astype(F32))
        state = state_ref[b].astype(F32)
        part = multiplier * state
        correction = -transposed(coupling_ref, b, multiplier)
        reply_ref[b, 0:comps] = correction.astype(BF16)
        return tuple(totals[j] + part * state[j : j + 1] for j in range(comps))

    totals = lax.fori_loop(0, blocks, one, (jnp.zeros((comps, width), F32),) * comps)
    lane = lax.broadcasted_iota(jnp.int32, (comps, width), 1)
    rest = jnp.zeros((comps, width), F32)
    for j in range(comps):
        column = jnp.sum(totals[j], axis=1, keepdims=True)
        rest = jnp.where(lane % comps == j, column, rest)
    packed = jnp.zeros((comps, width), F32)
    for part in range(PARTS):
        rounded = rest.astype(BF16).astype(F32)
        packed = jnp.where(lane // comps == part, rounded, packed)
        rest = rest - rounded
    packed = packed.astype(BF16)
    for b in range(blocks):
        reply_ref[b, comps : 2 * comps] = packed


def at_helper(inverse, coupling, state, picked):
    blocks, comps, _, width = inverse.shape
    return pl.pallas_call(
        helper_kernel,
        out_shape=jax.ShapeDtypeStruct((blocks, 2 * comps, width), BF16),
        compiler_params=params(16),
        cost_estimate=cost(4 * inverse.size, 4 * inverse.size),
    )(inverse, coupling, state, picked)


def scatter_kernel(scale, has_kept, helper_ref, cells_ref, back_ref, first_ref, mask_ref, *refs):
    kept_ref = refs[0] if has_kept else None
    second_ref, masked_ref, *sends, grad_ref, added, side_y = refs[has_kept:]
    layers, comps, rows, cols = first_ref.shape
    chunks, _, slots = cells_ref.shape
    width = back_ref.shape[-1]
    per_chunk = slots // width
    row_number = lax.broadcasted_iota(jnp.int32, (rows, slots), 0)
    for k in range(layers):
        for c in range(comps):
            added[c * rows : (c + 1) * rows, k * cols : (k + 1) * cols] = first_ref[k, c]

    def one(i, carry):
        column, y = split_cells(cells_ref[i], rows, cols)
        if has_kept:
            chosen = kept_ref[:, stretch(i, slots)]
        else:
            chosen = one_hot(column, added.shape[1], slots)
        parts = [back_ref[helper_ref[0, 0, i * per_chunk + j]].astype(F32)[:comps] for j in range(per_chunk)]
        correction = jnp.concatenate(parts, axis=1)
        at_row = row_number == y
        spread = jnp.concatenate(
            [jnp.where(at_row, correction[c : c + 1], 0.0).astype(BF16) for c in range(comps)], axis=0
        )
        added[...] += lax.dot_general(spread, chosen, (((1,), (1,)), ((), ())), preferred_element_type=F32)
        return carry

    unrolled(chunks, 2, one)
    for k in range(layers):
        for c in range(comps):
            second_ref[k, c] = added[c * rows : (c + 1) * rows, k * cols : (k + 1) * cols]
    write_edges(second_ref, mask_ref, None, masked_ref, side_y, sends)
    total = back_ref[0].astype(F32)[comps:]
    for b in range(1, back_ref.shape[0]):
        total += back_ref[b].astype(F32)[comps:]
    whole = total
    for part in range(1, PARTS):
        whole += pltpu.roll(total, width - part * comps, 1)
    grad_ref[...] = (whole * scale)[:, :comps]


def scatter(first, back, helper, cells, mask, kept, scale):
    layers, comps, rows, cols = first.shape
    smem = pl.BlockSpec(memory_space=pltpu.SMEM)
    vmem = pl.BlockSpec(memory_space=pltpu.VMEM)
    edges = edge_shapes(*first.shape)
    return pl.pallas_call(
        functools.partial(scatter_kernel, scale, len(kept)),
        in_specs=[smem] + [vmem] * (4 + len(kept)),
        out_specs=[vmem] * (3 + len(edges)),
        out_shape=[
            pltpu.VMEM(first.shape, F32),
            pltpu.VMEM(first.shape, F32),
            *edges,
            jax.ShapeDtypeStruct((comps, comps), F32),
        ],
        scratch_shapes=[pltpu.VMEM((comps * rows, layers * cols), F32), edge_scratch(layers, comps, cols)],
        compiler_params=params(24),
        cost_estimate=cost(2 * first.size * cells.size, 8 * first.size),
    )(helper, cells, back, first, mask, *kept)


def shards(
    cotangent,
    permeability,
    well_mask,
    diag_block,
    flux_block,
    cell_list,
    block_count,
    helper_of,
    flash_inverse,
    flash_coupling,
    phase_state,
):
    layers, comps, rows, cols = cotangent.shape
    slots, width = helper_of.shape[-1], flash_inverse.shape[-1]
    inverse = flash_inverse.reshape(slots, comps, comps, width)
    coupling = flash_coupling.reshape(slots, comps, comps, width)
    state = phase_state.reshape(slots, comps, width)

    def cells(chunk):
        return cell_list.reshape(-1, 1, min(chunk, cell_list.shape[-1]))

    def to_partners(array):
        return lax.all_to_all(array, AXES, split_axis=0, concat_axis=0, tiled=True)

    *sides, masked, field, mask, perm, place = opening(cotangent, well_mask, permeability, diag_block, flux_block)
    halos = exchange(*sides)
    blocks = [pltpu.with_memory_space_constraint(block, pltpu.VMEM) for block in (diag_block, flux_block)]
    inner, begun, inner_weights = apply_rows(True, True, field, masked, mask, place, halos, blocks, perm)
    first, rounded, outer_weights = apply_rows(
        True, False, field, masked, mask, place, halos, blocks, perm, inner, begun
    )
    sent, *chosen = gather(rounded, cells(GATHER_CHUNK), helper_of, block_count, comps, rows, cols, width)
    reply = at_helper(inverse, coupling, state, to_partners(sent))
    devices = lax.axis_size("gx") * lax.axis_size("gy")
    scale = -1.0 / math.sqrt(width * devices * devices)
    second, masked, *sides, interaction_grad = scatter(
        first, to_partners(reply), helper_of, cells(SCATTER_CHUNK), mask, chosen, scale
    )
    halos = exchange(*sides)
    inner, begun = apply_rows(False, True, second, masked, mask, place, halos, blocks, inner_weights)
    (adjoint,) = apply_rows(False, False, second, masked, mask, place, halos, blocks, outer_weights, inner, begun)
    return (adjoint, interaction_grad)


def solution(mesh):
    return jax.shard_map(
        shards,
        mesh=mesh,
        in_specs=(
            P(None, None, "gy", "gx"),
            P(None, "gy", "gx"),
            P("gy", "gx"),
            P(None, None, None, "gy", "gx"),
            P(None, None, None, "gy", "gx"),
            P("gy", "gx", None),
            P("gy", "gx"),
            P("gy", "gx", None),
            P("gy", "gx", None, None, None, None),
            P("gy", "gx", None, None, None, None),
            P("gy", "gx", None, None, None),
        ),
        out_specs=(P(None, None, "gy", "gx"), P()),
        check_vma=False,
    )
```

```python
import functools
import math

import jax
import jax.numpy as jnp
from jax import lax
from jax.experimental import pallas as pl
from jax.experimental.pallas import tpu as pltpu
from jax.sharding import PartitionSpec as P

F32 = jnp.float32
BF16 = jnp.bfloat16
AXES = ("gx", "gy")
MIB = 1024 * 1024
GATHER_CHUNK, SCATTER_CHUNK = 512, 4096
KEPT_BYTES = 8 * MIB


def params(mib):
    return pltpu.CompilerParams(vmem_limit_bytes=mib * MIB)


def cost(flops, moved):
    return pl.CostEstimate(flops=int(flops), bytes_accessed=int(moved), transcendentals=0)


def round_up(number, step):
    return -(-number // step) * step


def write_edges(field_ref, mask_ref, perm_ref, masked_ref, side_y, sends):
    send_y_0, send_y_1, send_x = sends
    layers, comps, rows, cols = field_ref.shape
    with_perm = perm_ref is not None
    clear = 1.0 - mask_ref[...].astype(F32)
    lane = lax.broadcasted_iota(jnp.int32, (rows, cols), 1)
    pair = lane // 2
    along_x = jnp.zeros((rows, cols), F32)
    side_y[...] = jnp.zeros_like(side_y)
    for k in range(layers):
        for c in range(comps + with_perm):
            if c < comps:
                value, at = field_ref[k, c] * clear, k * comps + c
                masked_ref[k, c] = value
            else:
                value, at = perm_ref[k], layers * comps + k
            side_y[0, at : at + 1, :] = value[0:1]
            side_y[1, at : at + 1, :] = value[rows - 1 : rows]
            along_x = jnp.where(pair == at, pltpu.roll(value, (2 * at + 1) % cols, 1), along_x)
    even = lax.axis_index("gy") % 2 == 0
    send_x[...] = along_x.astype(BF16)
    low, high = side_y[0].astype(BF16), side_y[1].astype(BF16)
    send_y_0[...] = jnp.where(even, high, low)
    send_y_1[...] = jnp.where(even, low, high)


def write_place(place_ref):
    cols, width = place_ref.shape
    number = lax.broadcasted_iota(jnp.int32, (cols, cols), 0)
    spot = lax.broadcasted_iota(jnp.int32, (cols, cols), 1)
    for r in range(width // cols):
        taken = ((number == 2 * r) & (spot == 0)) | ((number == 2 * r + 1) & (spot == cols - 1))
        place_ref[:, r * cols : (r + 1) * cols] = jnp.where(taken, 1.0, 0.0).astype(BF16)


def opening_kernel(
    field_hbm, mask_hbm, perm_hbm, diag_hbm, flux_hbm,
    send_y_0, send_y_1, send_x, masked_ref, field_ref, mask_ref, perm_ref, place_ref,
    side_y, sems,
):
    pairs = [(mask_hbm, mask_ref), (perm_hbm, perm_ref)]
    pairs.append((field_hbm, field_ref))
    copies = [pltpu.make_async_copy(a, b, sems.at[i]) for i, (a, b) in enumerate(pairs)]
    for copy in copies:
        copy.start()
    write_place(place_ref)
    for copy in copies:
        copy.wait()
    write_edges(field_ref, mask_ref, perm_ref, masked_ref, side_y, (send_y_0, send_y_1, send_x))


def edge_rows(layers, comps):
    return round_up(layers * (comps + 1), 16)


def edge_shapes(layers, comps, rows, cols):
    along_y = (edge_rows(layers, comps), cols)
    return [jax.ShapeDtypeStruct(shape, BF16) for shape in (along_y, along_y, (rows, cols))]


def edge_scratch(layers, comps, cols):
    return pltpu.VMEM((2, edge_rows(layers, comps), cols), F32)


def opening(field, mask, perm, diag, flux):
    layers, comps, rows, cols = field.shape
    hbm = pl.BlockSpec(memory_space=pltpu.HBM)
    vmem = pl.BlockSpec(memory_space=pltpu.VMEM)
    kept = [(array.shape, array.dtype) for array in (field, field, mask, perm)]
    kept.append(((cols, comps * cols), BF16))
    return pl.pallas_call(
        opening_kernel,
        in_specs=[hbm] * 5,
        out_specs=[vmem] * 8,
        out_shape=[*edge_shapes(*field.shape), *(pltpu.VMEM(*item) for item in kept)],
        scratch_shapes=[edge_scratch(layers, comps, cols), pltpu.SemaphoreType.DMA((3,))],
        compiler_params=params(16),
        cost_estimate=cost(4 * field.size, 8 * field.size),
    )(*(pltpu.with_memory_space_constraint(array, pltpu.HBM) for array in (field, mask, perm, diag, flux)))


def exchange(send_y_0, send_y_1, send_x):
    def swaps(axis, first, second):
        count = lax.axis_size(axis)
        results = []
        for start, array in ((0, first), (1, second)):
            pairs = [(i, i + 1) for i in range(start, count - 1, 2)]
            results.append(lax.ppermute(array, axis, pairs + [(j, i) for i, j in pairs]))
        return results

    return (*swaps("gx", send_x, send_x), *swaps("gy", send_y_0, send_y_1))


TILE = 16
WEIGHTS = 7


def reciprocal(value):
    guess = pl.reciprocal(value, approx=True)
    return guess * (2.0 - value * guess)


def weight(centre, beside):
    return 2.0 * centre * beside * reciprocal(centre + beside)


def tile_weights(k, y, perm_ref, edge_x, y_rows, comps):
    layers, rows, cols = perm_ref.shape
    here = slice(y, y + TILE)
    lane = lax.broadcasted_iota(jnp.int32, (TILE, cols), 1)
    is_first, is_last = lane == 0, lane == cols - 1
    at_low = 2 * (layers * comps + k)
    perm_low = pltpu.roll(edge_x[here], lax.rem(cols - at_low, cols), 1)
    perm_high = pltpu.roll(edge_x[here], lax.rem(2 * cols - at_low - 2, cols), 1)
    centre = perm_ref[k, here]
    low_y, high_y = beside_y(perm_ref, (k,), y, y_rows)
    to_left = weight(centre, jnp.where(is_first, perm_low, pltpu.roll(centre, 1, 1)))
    to_right = weight(centre, jnp.where(is_last, perm_high, pltpu.roll(centre, cols - 1, 1)))
    return [
        jnp.where(k < layers - 1, weight(centre, perm_ref[jnp.minimum(k + 1, layers - 1), here]), 0.0),
        jnp.where(k > 0, weight(centre, perm_ref[jnp.maximum(k - 1, 0), here]), 0.0),
        weight(centre, high_y),
        weight(centre, low_y),
        jnp.where(is_last, 0.0, to_right),
        jnp.where(is_first, 0.0, to_left),
        jnp.where(is_first, to_left, jnp.where(is_last, to_right, 0.0)),
    ]


def beside_y(ref, index, y, y_rows):
    rows, cols = ref.shape[-2:]
    row = lax.broadcasted_iota(jnp.int32, (TILE, cols), 0)
    if y > 0:
        low = ref[(*index, slice(y - 1, y - 1 + TILE))]
    else:
        low = jnp.where(row == 0, y_rows[0], pltpu.roll(ref[(*index, slice(0, TILE))], 1, 0))
    if y + TILE < rows:
        high = ref[(*index, slice(y + 1, y + 1 + TILE))]
    else:
        high = jnp.where(row == TILE - 1, y_rows[1], pltpu.roll(ref[(*index, slice(y, y + TILE))], TILE - 1, 0))
    return low, high


def apply_kernel(is_first_apply, is_inner, *refs):
    names = ["field", "masked", "mask", "place", "x_1", "x_0", "diag", "flux"]
    names += ["perm"] if is_first_apply else ["weights"]
    names += [] if is_inner else ["y_0", "y_1", "inner", "begun"]
    names += ["out"] if is_inner or is_first_apply else ["out_hbm"]
    names += ["begun"] if is_inner else []
    if is_first_apply:
        names += [] if is_inner else ["rounded"]
        names += ["weights"]
    names += ["edge_x", "turned", "beside_x"]
    names += [] if is_inner or is_first_apply else ["out", "sems"]
    ref = dict(zip(names, refs, strict=True))
    field_ref, masked_ref, edge_x, place = ref["field"], ref["masked"], ref["edge_x"], ref["place"]
    layers, comps, rows, cols = field_ref.shape
    diag_ref, flux_ref = ref["diag"], ref["flux"]
    tiles = list(range(TILE, rows - TILE, TILE)) if is_inner else [0, rows - TILE]
    here_rows = len(tiles) * TILE

    def out_copies(k):
        middle = slice(TILE, rows - TILE)
        pairs = [(ref["inner"].at[k], ref["out_hbm"].at[k, :, middle])]
        pairs += [
            (ref["out"].at[k, :, j * TILE : (j + 1) * TILE], ref["out_hbm"].at[k, :, y : y + TILE]) for j, y in enumerate(tiles)
        ]
        return [pltpu.make_async_copy(a, b, ref["sems"].at[j, k]) for j, (a, b) in enumerate(pairs)]

    lane = lax.broadcasted_iota(jnp.int32, (rows, cols), 1)
    even_x = lax.axis_index("gx") % 2 == 0
    even_y = lax.axis_index("gy") % 2 == 0
    edge_x[...] = jnp.where((lane % 2 == 0) == even_x, ref["x_1"][...].astype(F32), ref["x_0"][...].astype(F32))
    for k in range(layers):
        for j, y in enumerate(tiles):
            start = k * here_rows + j * TILE
            piece = pltpu.roll(edge_x[y : y + TILE], (cols - 2 * comps * k) % cols, 1)
            ref["turned"][start : start + TILE] = piece.astype(BF16)
    ref["beside_x"][...] = jnp.dot(ref["turned"][...], place[...], preferred_element_type=F32)

    def layer(k, carry):
        above = jnp.minimum(k + 1, layers - 1)
        below = jnp.maximum(k - 1, 0)
        rows_y, perm_y = None, None
        if not is_inner:
            odd = k % 2 == 1
            here = pl.ds(pl.multiple_of(16 * (k // 2), 16), 16)
            sides = [ref[name][here].astype(F32) for name in ("y_0", "y_1")]
            sides = [jnp.where(odd, side[comps:], side[:comps]) for side in sides]
            rows_y = (jnp.where(even_y, sides[1], sides[0]), jnp.where(even_y, sides[0], sides[1]))
        if is_first_apply and not is_inner:
            here = slice(layers * comps, layers * comps + 16)
            mine = lax.broadcasted_iota(jnp.int32, (16, cols), 0) == k
            sides = [
                jnp.sum(jnp.where(mine, ref[name][here].astype(F32), 0.0), axis=0, keepdims=True) for name in ("y_0", "y_1")
            ]
            perm_y = (jnp.where(even_y, sides[1], sides[0]), jnp.where(even_y, sides[0], sides[1]))
        for j, y in enumerate(tiles):
            here, local = slice(y, y + TILE), slice(j * TILE, (j + 1) * TILE)
            side_rows = pl.ds(pl.multiple_of(k * here_rows + j * TILE, TILE), TILE)
            if is_first_apply:
                weights = tile_weights(k, y, ref["perm"], edge_x, perm_y, comps)
                for number, value in enumerate(weights):
                    ref["weights"][k, number, local] = value
            else:
                weights = [ref["weights"][k, number, local] for number in range(WEIGHTS)]
            total = [None] * comps
            for r in range(comps):
                own = masked_ref[k, r, here]
                low, high = beside_y(masked_ref, (k, r), y, None if is_inner else [side[r : r + 1] for side in rows_y])
                summed = (
                    weights[0] * masked_ref[above, r, here]
                    + weights[1] * masked_ref[below, r, here]
                    + weights[2] * high
                    + weights[3] * low
                    + weights[4] * pltpu.roll(own, cols - 1, 1)
                    + weights[5] * pltpu.roll(own, 1, 1)
                    + weights[6] * ref["beside_x"][side_rows, r * cols : (r + 1) * cols]
                )
                for c in range(comps):
                    term = -flux_ref[k, r, c, here].astype(F32) * summed
                    if is_inner:
                        term = diag_ref[k, r, c, here].astype(F32) * own + term
                    total[c] = term if r == 0 else total[c] + term
            well = ref["mask"][here].astype(F32) if is_inner else None
            for c in range(comps):
                value = total[c] + (well * field_ref[k, c, here] if is_inner else ref["begun"][k, c, local])
                if is_first_apply and not is_inner:
                    ref["out"][k, c, here] = value
                    columns = pl.ds(pl.multiple_of(k * cols, cols), cols)
                    ref["rounded"][c * rows + y : c * rows + y + TILE, columns] = value.astype(BF16)
                else:
                    ref["out"][k, c, local] = value
        for j, y in enumerate([0, rows - TILE] if is_inner else []):
            here, local = slice(y, y + TILE), slice(j * TILE, (j + 1) * TILE)
            well = ref["mask"][here].astype(F32)
            total = [well * field_ref[k, c, here] for c in range(comps)]
            for r in range(comps):
                own = masked_ref[k, r, here]
                for c in range(comps):
                    total[c] += diag_ref[k, r, c, here].astype(F32) * own
            for c in range(comps):
                ref["begun"][k, c, local] = total[c]
        if is_first_apply and not is_inner:
            columns = pl.ds(pl.multiple_of(k * cols, cols), cols)
            for c in range(comps):
                value = ref["inner"][k, c]
                ref["out"][k, c, TILE : rows - TILE] = value
                ref["rounded"][c * rows + TILE : (c + 1) * rows - TILE, columns] = value.astype(BF16)
        if not is_first_apply and not is_inner:
            for copy in out_copies(k)[1:]:
                copy.start()
        return carry

    if not is_first_apply and not is_inner:
        for k in range(layers):
            out_copies(k)[0].start()
    unrolled(layers, 3, layer)
    if not is_first_apply and not is_inner:
        for k in range(layers):
            for copy in out_copies(k):
                copy.wait()


def apply_rows(is_first_apply, is_inner, field, masked, mask, place, halos, blocks, third, *inner):
    layers, comps, rows, cols = field.shape
    vmem = pl.BlockSpec(memory_space=pltpu.VMEM)
    hbm = pl.BlockSpec(memory_space=pltpu.HBM)
    here_rows = rows - 2 * TILE if is_inner else 2 * TILE
    here = (layers, comps, here_rows, cols)
    arrays = [field, masked, mask, place, halos[1], halos[0], *blocks, third]
    specs = [vmem] * 9
    if not is_inner:
        arrays += [*halos[2:], *inner]
        specs += [vmem] * 4
    if is_inner:
        begun = (layers, comps, 2 * TILE, cols)
        out_shape, out_specs = [pltpu.VMEM(here, F32), pltpu.VMEM(begun, F32)], [vmem] * 2
    else:
        out_shape = [jax.ShapeDtypeStruct(field.shape, F32)]
        out_specs = [vmem if is_first_apply else hbm]
    if is_first_apply:
        if not is_inner:
            out_shape.append(jax.ShapeDtypeStruct((comps * rows, layers * cols), BF16))
        out_shape.append(pltpu.VMEM((layers, WEIGHTS, here_rows, cols), F32))
        out_specs = [vmem] * len(out_shape)
    scratch = [
        pltpu.VMEM((rows, cols), F32),
        pltpu.VMEM((layers * here_rows, cols), BF16),
        pltpu.VMEM((layers * here_rows, comps * cols), F32),
    ]
    if not is_first_apply and not is_inner:
        scratch += [pltpu.VMEM(here, F32), pltpu.SemaphoreType.DMA((3, layers))]
    size = layers * comps * comps * here_rows * cols
    return pl.pallas_call(
        functools.partial(apply_kernel, is_first_apply, is_inner),
        in_specs=specs,
        out_specs=out_specs,
        out_shape=out_shape,
        scratch_shapes=scratch,
        compiler_params=params(16),
        cost_estimate=cost(8 * size, 4 * size + 8 * field.size),
    )(*arrays)


def split_cells(cells, rows, cols):
    layer = cells // (rows * cols)
    y = (cells // cols) % rows
    return layer * cols + cells % cols, y


def unrolled(count, together, body):
    def group(i, carry):
        for j in range(together):
            body(i * together + j, None)
        return carry

    together = math.gcd(count, together)
    if together == count:
        group(0, None)
    else:
        lax.fori_loop(0, count // together, group, 0)


def stretch(i, size):
    return pl.ds(i * size if isinstance(i, int) else pl.multiple_of(i * size, size), size)


def one_hot(column, count, slots):
    number = lax.broadcasted_iota(jnp.int32, (count, slots), 0)
    return jnp.where(number == column, 1.0, 0.0).astype(BF16)


def gather_kernel(rows, cols, helper_ref, count_ref, cells_ref, rounded_ref, sent_ref, kept_ref=None):
    chunks, _, slots = cells_ref.shape
    comps, width = sent_ref.shape[1:]
    per_chunk = slots // width
    row_number = lax.broadcasted_iota(jnp.int32, (rows, slots), 0)

    def one(i, carry):
        column, y = split_cells(cells_ref[i], rows, cols)
        chosen = one_hot(column, rounded_ref.shape[1], slots)
        if kept_ref is not None:
            kept_ref[:, stretch(i, slots)] = chosen
        found = jnp.dot(rounded_ref[...], chosen, preferred_element_type=F32)
        at_row = row_number == y
        values = [
            jnp.sum(jnp.where(at_row, found[c * rows : (c + 1) * rows], 0.0), axis=0, keepdims=True)
            for c in range(comps)
        ]
        values = jnp.concatenate(values, axis=0)
        for j in range(per_chunk):
            b = i * per_chunk + j
            live = jnp.where(b < count_ref[0, 0], 1.0, 0.0)
            sent_ref[helper_ref[0, 0, b]] = (values[:, j * width : (j + 1) * width] * live).astype(BF16)
        return carry

    unrolled(chunks, 8, one)


def gather(rounded, cells, helper, count, comps, rows, cols, width):
    blocks = helper.shape[-1]
    smem = pl.BlockSpec(memory_space=pltpu.SMEM)
    vmem = pl.BlockSpec(memory_space=pltpu.VMEM)
    out_shape = [jax.ShapeDtypeStruct((blocks, comps, width), BF16)]
    if rounded.shape[1] * cells.size * 2 <= KEPT_BYTES:
        out_shape.append(pltpu.VMEM((rounded.shape[1], cells.size), BF16))
    return pl.pallas_call(
        functools.partial(gather_kernel, rows, cols),
        in_specs=[smem, smem, vmem, vmem],
        out_specs=[vmem] * len(out_shape),
        out_shape=out_shape,
        compiler_params=params(16),
        cost_estimate=cost(2 * rounded.size * cells.size, 2 * rounded.size),
    )(helper, count, cells, rounded)


PARTS = 3


def helper_kernel(inverse_ref, coupling_ref, state_ref, picked_ref, reply_ref):
    blocks, comps = inverse_ref.shape[:2]
    width = inverse_ref.shape[-1]

    def transposed(block_ref, b, value):
        block = block_ref[b].astype(F32)
        total = block[0] * value[0:1]
        for r in range(1, comps):
            total += block[r] * value[r : r + 1]
        return total

    def one(b, totals):
        multiplier = transposed(inverse_ref, b, picked_ref[b].astype(F32))
        state = state_ref[b].astype(F32)
        part = multiplier * state
        correction = -transposed(coupling_ref, b, multiplier)
        reply_ref[b, 0:comps] = correction.astype(BF16)
        return tuple(totals[j] + part * state[j : j + 1] for j in range(comps))

    totals = lax.fori_loop(0, blocks, one, (jnp.zeros((comps, width), F32),) * comps)
    lane = lax.broadcasted_iota(jnp.int32, (comps, width), 1)
    rest = jnp.zeros((comps, width), F32)
    for j in range(comps):
        column = jnp.sum(totals[j], axis=1, keepdims=True)
        rest = jnp.where(lane % comps == j, column, rest)
    packed = jnp.zeros((comps, width), F32)
    for part in range(PARTS):
        rounded = rest.astype(BF16).astype(F32)
        packed = jnp.where(lane // comps == part, rounded, packed)
        rest = rest - rounded
    packed = packed.astype(BF16)
    for b in range(blocks):
        reply_ref[b, comps : 2 * comps] = packed


def at_helper(inverse, coupling, state, picked):
    blocks, comps, _, width = inverse.shape
    return pl.pallas_call(
        helper_kernel,
        out_shape=jax.ShapeDtypeStruct((blocks, 2 * comps, width), BF16),
        compiler_params=params(16),
        cost_estimate=cost(4 * inverse.size, 4 * inverse.size),
    )(inverse, coupling, state, picked)


def scatter_kernel(scale, has_kept, helper_ref, cells_ref, back_ref, first_ref, mask_ref, *refs):
    kept_ref = refs[0] if has_kept else None
    second_ref, masked_ref, *sends, grad_ref, added, side_y = refs[has_kept:]
    layers, comps, rows, cols = first_ref.shape
    chunks, _, slots = cells_ref.shape
    width = back_ref.shape[-1]
    per_chunk = slots // width
    row_number = lax.broadcasted_iota(jnp.int32, (rows, slots), 0)
    if chunks > 1:
        added[...] = jnp.zeros_like(added)

    def one(i, carry):
        column, y = split_cells(cells_ref[i], rows, cols)
        if has_kept:
            chosen = kept_ref[:, stretch(i, slots)]
        else:
            chosen = one_hot(column, added.shape[1], slots)
        parts = [back_ref[helper_ref[0, 0, i * per_chunk + j]].astype(F32)[:comps] for j in range(per_chunk)]
        correction = jnp.concatenate(parts, axis=1)
        at_row = row_number == y
        spread = jnp.concatenate(
            [jnp.where(at_row, correction[c : c + 1], 0.0).astype(BF16) for c in range(comps)], axis=0
        )
        product = lax.dot_general(spread, chosen, (((1,), (1,)), ((), ())), preferred_element_type=F32)
        added[...] = product if chunks == 1 else added[...] + product
        return carry

    unrolled(chunks, 1, one)
    for k in range(layers):
        for c in range(comps):
            second_ref[k, c] = first_ref[k, c] + added[c * rows : (c + 1) * rows, k * cols : (k + 1) * cols]
    write_edges(second_ref, mask_ref, None, masked_ref, side_y, sends)
    total = back_ref[0].astype(F32)[comps:]
    for b in range(1, back_ref.shape[0]):
        total += back_ref[b].astype(F32)[comps:]
    whole = total
    for part in range(1, PARTS):
        whole += pltpu.roll(total, width - part * comps, 1)
    grad_ref[...] = (whole * scale)[:, :comps]


def scatter(first, back, helper, cells, mask, kept, scale):
    layers, comps, rows, cols = first.shape
    smem = pl.BlockSpec(memory_space=pltpu.SMEM)
    vmem = pl.BlockSpec(memory_space=pltpu.VMEM)
    edges = edge_shapes(*first.shape)
    return pl.pallas_call(
        functools.partial(scatter_kernel, scale, len(kept)),
        in_specs=[smem] + [vmem] * (4 + len(kept)),
        out_specs=[vmem] * (3 + len(edges)),
        out_shape=[
            pltpu.VMEM(first.shape, F32),
            pltpu.VMEM(first.shape, F32),
            *edges,
            jax.ShapeDtypeStruct((comps, comps), F32),
        ],
        scratch_shapes=[pltpu.VMEM((comps * rows, layers * cols), F32), edge_scratch(layers, comps, cols)],
        compiler_params=params(24),
        cost_estimate=cost(2 * first.size * cells.size, 8 * first.size),
    )(helper, cells, back, first, mask, *kept)


def shards(
    cotangent,
    permeability,
    well_mask,
    diag_block,
    flux_block,
    cell_list,
    block_count,
    helper_of,
    flash_inverse,
    flash_coupling,
    phase_state,
):
    layers, comps, rows, cols = cotangent.shape
    slots, width = helper_of.shape[-1], flash_inverse.shape[-1]
    inverse = flash_inverse.reshape(slots, comps, comps, width)
    coupling = flash_coupling.reshape(slots, comps, comps, width)
    state = phase_state.reshape(slots, comps, width)

    def cells(chunk):
        return cell_list.reshape(-1, 1, min(chunk, cell_list.shape[-1]))

    def to_partners(array):
        return lax.all_to_all(array, AXES, split_axis=0, concat_axis=0, tiled=True)

    *sides, masked, field, mask, perm, place = opening(cotangent, well_mask, permeability, diag_block, flux_block)
    halos = exchange(*sides)
    blocks = [pltpu.with_memory_space_constraint(block, pltpu.VMEM) for block in (diag_block, flux_block)]
    inner, begun, inner_weights = apply_rows(True, True, field, masked, mask, place, halos, blocks, perm)
    first, rounded, outer_weights = apply_rows(
        True, False, field, masked, mask, place, halos, blocks, perm, inner, begun
    )
    sent, *chosen = gather(rounded, cells(GATHER_CHUNK), helper_of, block_count, comps, rows, cols, width)
    reply = at_helper(inverse, coupling, state, to_partners(sent))
    devices = lax.axis_size("gx") * lax.axis_size("gy")
    scale = -1.0 / math.sqrt(width * devices * devices)
    second, masked, *sides, interaction_grad = scatter(
        first, to_partners(reply), helper_of, cells(SCATTER_CHUNK), mask, chosen, scale
    )
    halos = exchange(*sides)
    inner, begun = apply_rows(False, True, second, masked, mask, place, halos, blocks, inner_weights)
    (adjoint,) = apply_rows(False, False, second, masked, mask, place, halos, blocks, outer_weights, inner, begun)
    return (adjoint, interaction_grad)


def solution(mesh):
    return jax.shard_map(
        shards,
        mesh=mesh,
        in_specs=(
            P(None, None, "gy", "gx"),
            P(None, "gy", "gx"),
            P("gy", "gx"),
            P(None, None, None, "gy", "gx"),
            P(None, None, None, "gy", "gx"),
            P("gy", "gx", None),
            P("gy", "gx"),
            P("gy", "gx", None),
            P("gy", "gx", None, None, None, None),
            P("gy", "gx", None, None, None, None),
            P("gy", "gx", None, None, None),
        ),
        out_specs=(P(None, None, "gy", "gx"), P()),
        check_vma=False,
    )
```

```python
import functools
import math

import jax
import jax.numpy as jnp
from jax import lax
from jax.experimental import pallas as pl
from jax.experimental.pallas import tpu as pltpu
from jax.sharding import PartitionSpec as P

F32 = jnp.float32
BF16 = jnp.bfloat16
AXES = ("gx", "gy")
MIB = 1024 * 1024
GATHER_CHUNK, SCATTER_CHUNK = 1024, 4096
KEPT_BYTES = 8 * MIB


def params(mib):
    return pltpu.CompilerParams(vmem_limit_bytes=mib * MIB)


def cost(flops, moved):
    return pl.CostEstimate(flops=int(flops), bytes_accessed=int(moved), transcendentals=0)


def round_up(number, step):
    return -(-number // step) * step


def write_edges(field_ref, mask_ref, perm_ref, masked_ref, side_y, sends):
    send_y_0, send_y_1, send_x = sends
    layers, comps, rows, cols = field_ref.shape
    with_perm = perm_ref is not None
    clear = 1.0 - mask_ref[...].astype(F32)
    lane = lax.broadcasted_iota(jnp.int32, (rows, cols), 1)
    pair = lane // 2
    along_x = jnp.zeros((rows, cols), F32)
    side_y[...] = jnp.zeros_like(side_y)
    for k in range(layers):
        for c in range(comps + with_perm):
            if c < comps:
                value, at = field_ref[k, c] * clear, k * comps + c
                masked_ref[k, c] = value
            else:
                value, at = perm_ref[k], layers * comps + k
            side_y[0, at : at + 1, :] = value[0:1]
            side_y[1, at : at + 1, :] = value[rows - 1 : rows]
            along_x = jnp.where(pair == at, pltpu.roll(value, (2 * at + 1) % cols, 1), along_x)
    even = lax.axis_index("gy") % 2 == 0
    send_x[...] = along_x.astype(BF16)
    low, high = side_y[0].astype(BF16), side_y[1].astype(BF16)
    send_y_0[...] = jnp.where(even, high, low)
    send_y_1[...] = jnp.where(even, low, high)


def write_place(place_ref):
    cols, width = place_ref.shape
    number = lax.broadcasted_iota(jnp.int32, (cols, cols), 0)
    spot = lax.broadcasted_iota(jnp.int32, (cols, cols), 1)
    for r in range(width // cols):
        taken = ((number == 2 * r) & (spot == 0)) | ((number == 2 * r + 1) & (spot == cols - 1))
        place_ref[:, r * cols : (r + 1) * cols] = jnp.where(taken, 1.0, 0.0).astype(BF16)


def opening_kernel(
    field_hbm, mask_hbm, perm_hbm, diag_hbm, flux_hbm,
    send_y_0, send_y_1, send_x, masked_ref, field_ref, mask_ref, perm_ref, place_ref,
    side_y, sems,
):
    pairs = [(mask_hbm, mask_ref), (perm_hbm, perm_ref)]
    pairs.append((field_hbm, field_ref))
    copies = [pltpu.make_async_copy(a, b, sems.at[i]) for i, (a, b) in enumerate(pairs)]
    for copy in copies:
        copy.start()
    write_place(place_ref)
    for copy in copies:
        copy.wait()
    write_edges(field_ref, mask_ref, perm_ref, masked_ref, side_y, (send_y_0, send_y_1, send_x))


def edge_rows(layers, comps):
    return round_up(layers * (comps + 1), 16)


def edge_shapes(layers, comps, rows, cols):
    along_y = (edge_rows(layers, comps), cols)
    return [jax.ShapeDtypeStruct(shape, BF16) for shape in (along_y, along_y, (rows, cols))]


def edge_scratch(layers, comps, cols):
    return pltpu.VMEM((2, edge_rows(layers, comps), cols), F32)


def opening(field, mask, perm, diag, flux):
    layers, comps, rows, cols = field.shape
    hbm = pl.BlockSpec(memory_space=pltpu.HBM)
    vmem = pl.BlockSpec(memory_space=pltpu.VMEM)
    kept = [(array.shape, array.dtype) for array in (field, field, mask, perm)]
    kept.append(((cols, comps * cols), BF16))
    return pl.pallas_call(
        opening_kernel,
        in_specs=[hbm] * 5,
        out_specs=[vmem] * 8,
        out_shape=[*edge_shapes(*field.shape), *(pltpu.VMEM(*item) for item in kept)],
        scratch_shapes=[edge_scratch(layers, comps, cols), pltpu.SemaphoreType.DMA((3,))],
        compiler_params=params(16),
        cost_estimate=cost(4 * field.size, 8 * field.size),
    )(*(pltpu.with_memory_space_constraint(array, pltpu.HBM) for array in (field, mask, perm, diag, flux)))


def exchange(send_y_0, send_y_1, send_x):
    def swaps(axis, first, second):
        count = lax.axis_size(axis)
        results = []
        for start, array in ((0, first), (1, second)):
            pairs = [(i, i + 1) for i in range(start, count - 1, 2)]
            results.append(lax.ppermute(array, axis, pairs + [(j, i) for i, j in pairs]))
        return results

    return (*swaps("gx", send_x, send_x), *swaps("gy", send_y_0, send_y_1))


TILE = 16
WEIGHTS = 7


def reciprocal(value):
    guess = pl.reciprocal(value, approx=True)
    return guess * (2.0 - value * guess)


def weight(centre, beside):
    return 2.0 * centre * beside * reciprocal(centre + beside)


def tile_weights(k, y, perm_ref, edge_x, y_rows, comps):
    layers, rows, cols = perm_ref.shape
    here = slice(y, y + TILE)
    lane = lax.broadcasted_iota(jnp.int32, (TILE, cols), 1)
    is_first, is_last = lane == 0, lane == cols - 1
    at_low = 2 * (layers * comps + k)
    perm_low = pltpu.roll(edge_x[here], lax.rem(cols - at_low, cols), 1)
    perm_high = pltpu.roll(edge_x[here], lax.rem(2 * cols - at_low - 2, cols), 1)
    centre = perm_ref[k, here]
    low_y, high_y = beside_y(perm_ref, (k,), y, y_rows)
    to_left = weight(centre, jnp.where(is_first, perm_low, pltpu.roll(centre, 1, 1)))
    to_right = weight(centre, jnp.where(is_last, perm_high, pltpu.roll(centre, cols - 1, 1)))
    return [
        jnp.where(k < layers - 1, weight(centre, perm_ref[jnp.minimum(k + 1, layers - 1), here]), 0.0),
        jnp.where(k > 0, weight(centre, perm_ref[jnp.maximum(k - 1, 0), here]), 0.0),
        weight(centre, high_y),
        weight(centre, low_y),
        jnp.where(is_last, 0.0, to_right),
        jnp.where(is_first, 0.0, to_left),
        jnp.where(is_first, to_left, jnp.where(is_last, to_right, 0.0)),
    ]


def beside_y(ref, index, y, y_rows):
    rows, cols = ref.shape[-2:]
    row = lax.broadcasted_iota(jnp.int32, (TILE, cols), 0)
    if y > 0:
        low = ref[(*index, slice(y - 1, y - 1 + TILE))]
    else:
        low = jnp.where(row == 0, y_rows[0], pltpu.roll(ref[(*index, slice(0, TILE))], 1, 0))
    if y + TILE < rows:
        high = ref[(*index, slice(y + 1, y + 1 + TILE))]
    else:
        high = jnp.where(row == TILE - 1, y_rows[1], pltpu.roll(ref[(*index, slice(y, y + TILE))], TILE - 1, 0))
    return low, high


def apply_kernel(is_first_apply, is_inner, *refs):
    names = ["field", "masked", "mask", "place", "x_1", "x_0", "diag", "flux"]
    names += ["perm"] if is_first_apply else ["weights"]
    names += [] if is_inner else ["y_0", "y_1", "inner", "begun"]
    names += ["out"] if is_inner or is_first_apply else ["out_hbm"]
    names += ["begun"] if is_inner else []
    if is_first_apply:
        names += [] if is_inner else ["rounded"]
        names += ["weights"]
    names += ["edge_x", "turned", "beside_x"]
    names += [] if is_inner or is_first_apply else ["out", "sems"]
    ref = dict(zip(names, refs, strict=True))
    field_ref, masked_ref, edge_x, place = ref["field"], ref["masked"], ref["edge_x"], ref["place"]
    layers, comps, rows, cols = field_ref.shape
    diag_ref, flux_ref = ref["diag"], ref["flux"]
    tiles = list(range(TILE, rows - TILE, TILE)) if is_inner else [0, rows - TILE]
    here_rows = len(tiles) * TILE

    def out_copies(k):
        middle = slice(TILE, rows - TILE)
        pairs = [(ref["inner"].at[k], ref["out_hbm"].at[k, :, middle])]
        pairs += [
            (ref["out"].at[k, :, j * TILE : (j + 1) * TILE], ref["out_hbm"].at[k, :, y : y + TILE]) for j, y in enumerate(tiles)
        ]
        return [pltpu.make_async_copy(a, b, ref["sems"].at[j, k]) for j, (a, b) in enumerate(pairs)]

    lane = lax.broadcasted_iota(jnp.int32, (rows, cols), 1)
    even_x = lax.axis_index("gx") % 2 == 0
    even_y = lax.axis_index("gy") % 2 == 0
    edge_x[...] = jnp.where((lane % 2 == 0) == even_x, ref["x_1"][...].astype(F32), ref["x_0"][...].astype(F32))
    for k in range(layers):
        for j, y in enumerate(tiles):
            start = k * here_rows + j * TILE
            piece = pltpu.roll(edge_x[y : y + TILE], (cols - 2 * comps * k) % cols, 1)
            ref["turned"][start : start + TILE] = piece.astype(BF16)
    ref["beside_x"][...] = jnp.dot(ref["turned"][...], place[...], preferred_element_type=F32)

    def layer(k, carry):
        above = jnp.minimum(k + 1, layers - 1)
        below = jnp.maximum(k - 1, 0)
        rows_y, perm_y = None, None
        if not is_inner:
            odd = k % 2 == 1
            here = pl.ds(pl.multiple_of(16 * (k // 2), 16), 16)
            sides = [ref[name][here].astype(F32) for name in ("y_0", "y_1")]
            sides = [jnp.where(odd, side[comps:], side[:comps]) for side in sides]
            rows_y = (jnp.where(even_y, sides[1], sides[0]), jnp.where(even_y, sides[0], sides[1]))
        if is_first_apply and not is_inner:
            here = slice(layers * comps, layers * comps + 16)
            mine = lax.broadcasted_iota(jnp.int32, (16, cols), 0) == k
            sides = [
                jnp.sum(jnp.where(mine, ref[name][here].astype(F32), 0.0), axis=0, keepdims=True) for name in ("y_0", "y_1")
            ]
            perm_y = (jnp.where(even_y, sides[1], sides[0]), jnp.where(even_y, sides[0], sides[1]))
        for j, y in enumerate(tiles):
            here, local = slice(y, y + TILE), slice(j * TILE, (j + 1) * TILE)
            side_rows = pl.ds(pl.multiple_of(k * here_rows + j * TILE, TILE), TILE)
            if is_first_apply:
                weights = tile_weights(k, y, ref["perm"], edge_x, perm_y, comps)
                for number, value in enumerate(weights):
                    ref["weights"][k, number, local] = value
            else:
                weights = [ref["weights"][k, number, local] for number in range(WEIGHTS)]
            total = [None] * comps
            for r in range(comps):
                own = masked_ref[k, r, here]
                low, high = beside_y(masked_ref, (k, r), y, None if is_inner else [side[r : r + 1] for side in rows_y])
                summed = (
                    weights[0] * masked_ref[above, r, here]
                    + weights[1] * masked_ref[below, r, here]
                    + weights[2] * high
                    + weights[3] * low
                    + weights[4] * pltpu.roll(own, cols - 1, 1)
                    + weights[5] * pltpu.roll(own, 1, 1)
                    + weights[6] * ref["beside_x"][side_rows, r * cols : (r + 1) * cols]
                )
                for c in range(comps):
                    term = -flux_ref[k, r, c, here].astype(F32) * summed
                    if is_inner:
                        term = diag_ref[k, r, c, here].astype(F32) * own + term
                    total[c] = term if r == 0 else total[c] + term
            well = ref["mask"][here].astype(F32) if is_inner else None
            for c in range(comps):
                value = total[c] + (well * field_ref[k, c, here] if is_inner else ref["begun"][k, c, local])
                if is_first_apply and not is_inner:
                    ref["out"][k, c, here] = value
                    columns = pl.ds(pl.multiple_of(k * cols, cols), cols)
                    ref["rounded"][c * rows + y : c * rows + y + TILE, columns] = value.astype(BF16)
                else:
                    ref["out"][k, c, local] = value
        for j, y in enumerate([0, rows - TILE] if is_inner else []):
            here, local = slice(y, y + TILE), slice(j * TILE, (j + 1) * TILE)
            well = ref["mask"][here].astype(F32)
            total = [well * field_ref[k, c, here] for c in range(comps)]
            for r in range(comps):
                own = masked_ref[k, r, here]
                for c in range(comps):
                    total[c] += diag_ref[k, r, c, here].astype(F32) * own
            for c in range(comps):
                ref["begun"][k, c, local] = total[c]
        if is_first_apply and not is_inner:
            columns = pl.ds(pl.multiple_of(k * cols, cols), cols)
            for c in range(comps):
                value = ref["inner"][k, c]
                ref["out"][k, c, TILE : rows - TILE] = value
                ref["rounded"][c * rows + TILE : (c + 1) * rows - TILE, columns] = value.astype(BF16)
        if not is_first_apply and not is_inner:
            for copy in out_copies(k)[1:]:
                copy.start()
        return carry

    if not is_first_apply and not is_inner:
        for k in range(layers):
            out_copies(k)[0].start()
    unrolled(layers, 3, layer)
    if not is_first_apply and not is_inner:
        for k in range(layers):
            for copy in out_copies(k):
                copy.wait()


def apply_rows(is_first_apply, is_inner, field, masked, mask, place, halos, blocks, third, *inner):
    layers, comps, rows, cols = field.shape
    vmem = pl.BlockSpec(memory_space=pltpu.VMEM)
    hbm = pl.BlockSpec(memory_space=pltpu.HBM)
    here_rows = rows - 2 * TILE if is_inner else 2 * TILE
    here = (layers, comps, here_rows, cols)
    arrays = [field, masked, mask, place, halos[1], halos[0], *blocks, third]
    specs = [vmem] * 9
    if not is_inner:
        arrays += [*halos[2:], *inner]
        specs += [vmem] * 4
    if is_inner:
        begun = (layers, comps, 2 * TILE, cols)
        out_shape, out_specs = [pltpu.VMEM(here, F32), pltpu.VMEM(begun, F32)], [vmem] * 2
    else:
        out_shape = [jax.ShapeDtypeStruct(field.shape, F32)]
        out_specs = [vmem if is_first_apply else hbm]
    if is_first_apply:
        if not is_inner:
            out_shape.append(jax.ShapeDtypeStruct((comps * rows, layers * cols), BF16))
        out_shape.append(pltpu.VMEM((layers, WEIGHTS, here_rows, cols), F32))
        out_specs = [vmem] * len(out_shape)
    scratch = [
        pltpu.VMEM((rows, cols), F32),
        pltpu.VMEM((layers * here_rows, cols), BF16),
        pltpu.VMEM((layers * here_rows, comps * cols), F32),
    ]
    if not is_first_apply and not is_inner:
        scratch += [pltpu.VMEM(here, F32), pltpu.SemaphoreType.DMA((3, layers))]
    size = layers * comps * comps * here_rows * cols
    return pl.pallas_call(
        functools.partial(apply_kernel, is_first_apply, is_inner),
        in_specs=specs,
        out_specs=out_specs,
        out_shape=out_shape,
        scratch_shapes=scratch,
        compiler_params=params(16),
        cost_estimate=cost(8 * size, 4 * size + 8 * field.size),
    )(*arrays)


def split_cells(cells, rows, cols):
    layer = cells // (rows * cols)
    y = (cells // cols) % rows
    return layer * cols + cells % cols, y


def unrolled(count, together, body):
    def group(i, carry):
        for j in range(together):
            body(i * together + j, None)
        return carry

    together = math.gcd(count, together)
    if together == count:
        group(0, None)
    else:
        lax.fori_loop(0, count // together, group, 0)


def stretch(i, size):
    return pl.ds(i * size if isinstance(i, int) else pl.multiple_of(i * size, size), size)


def one_hot(column, count, slots):
    number = lax.broadcasted_iota(jnp.int32, (count, slots), 0)
    return jnp.where(number == column, 1.0, 0.0).astype(BF16)


def gather_kernel(rows, cols, helper_ref, count_ref, cells_ref, rounded_ref, sent_ref, kept_ref=None):
    chunks, _, slots = cells_ref.shape
    comps, width = sent_ref.shape[1:]
    per_chunk = slots // width
    row_number = lax.broadcasted_iota(jnp.int32, (rows, slots), 0)

    def one(i, carry):
        column, y = split_cells(cells_ref[i], rows, cols)
        chosen = one_hot(column, rounded_ref.shape[1], slots)
        if kept_ref is not None:
            kept_ref[:, stretch(i, slots)] = chosen
        found = jnp.dot(rounded_ref[...], chosen, preferred_element_type=F32)
        at_row = row_number == y
        values = [
            jnp.sum(jnp.where(at_row, found[c * rows : (c + 1) * rows], 0.0), axis=0, keepdims=True)
            for c in range(comps)
        ]
        values = jnp.concatenate(values, axis=0)
        for j in range(per_chunk):
            b = i * per_chunk + j
            live = jnp.where(b < count_ref[0, 0], 1.0, 0.0)
            sent_ref[helper_ref[0, 0, b]] = (values[:, j * width : (j + 1) * width] * live).astype(BF16)
        return carry

    unrolled(chunks, 8, one)


def gather(rounded, cells, helper, count, comps, rows, cols, width):
    blocks = helper.shape[-1]
    smem = pl.BlockSpec(memory_space=pltpu.SMEM)
    vmem = pl.BlockSpec(memory_space=pltpu.VMEM)
    out_shape = [jax.ShapeDtypeStruct((blocks, comps, width), BF16)]
    if rounded.shape[1] * cells.size * 2 <= KEPT_BYTES:
        out_shape.append(pltpu.VMEM((rounded.shape[1], cells.size), BF16))
    return pl.pallas_call(
        functools.partial(gather_kernel, rows, cols),
        in_specs=[smem, smem, vmem, vmem],
        out_specs=[vmem] * len(out_shape),
        out_shape=out_shape,
        compiler_params=params(16),
        cost_estimate=cost(2 * rounded.size * cells.size, 2 * rounded.size),
    )(helper, count, cells, rounded)


PARTS = 3


def helper_kernel(inverse_ref, coupling_ref, state_ref, picked_ref, reply_ref):
    blocks, comps = inverse_ref.shape[:2]
    width = inverse_ref.shape[-1]

    def transposed(block_ref, b, value):
        block = block_ref[b].astype(F32)
        total = block[0] * value[0:1]
        for r in range(1, comps):
            total += block[r] * value[r : r + 1]
        return total

    def one(b, totals):
        multiplier = transposed(inverse_ref, b, picked_ref[b].astype(F32))
        state = state_ref[b].astype(F32)
        part = multiplier * state
        correction = -transposed(coupling_ref, b, multiplier)
        reply_ref[b, 0:comps] = correction.astype(BF16)
        return tuple(totals[j] + part * state[j : j + 1] for j in range(comps))

    totals = lax.fori_loop(0, blocks, one, (jnp.zeros((comps, width), F32),) * comps)
    lane = lax.broadcasted_iota(jnp.int32, (comps, width), 1)
    rest = jnp.zeros((comps, width), F32)
    for j in range(comps):
        column = jnp.sum(totals[j], axis=1, keepdims=True)
        rest = jnp.where(lane % comps == j, column, rest)
    packed = jnp.zeros((comps, width), F32)
    for part in range(PARTS):
        rounded = rest.astype(BF16).astype(F32)
        packed = jnp.where(lane // comps == part, rounded, packed)
        rest = rest - rounded
    packed = packed.astype(BF16)
    for b in range(blocks):
        reply_ref[b, comps : 2 * comps] = packed


def at_helper(inverse, coupling, state, picked):
    blocks, comps, _, width = inverse.shape
    return pl.pallas_call(
        helper_kernel,
        out_shape=jax.ShapeDtypeStruct((blocks, 2 * comps, width), BF16),
        compiler_params=params(16),
        cost_estimate=cost(4 * inverse.size, 4 * inverse.size),
    )(inverse, coupling, state, picked)


def scatter_kernel(scale, has_kept, helper_ref, cells_ref, back_ref, first_ref, mask_ref, *refs):
    kept_ref = refs[0] if has_kept else None
    second_ref, masked_ref, *sends, grad_ref, added, side_y = refs[has_kept:]
    layers, comps, rows, cols = first_ref.shape
    chunks, _, slots = cells_ref.shape
    width = back_ref.shape[-1]
    per_chunk = slots // width
    row_number = lax.broadcasted_iota(jnp.int32, (rows, slots), 0)
    if chunks > 1:
        added[...] = jnp.zeros_like(added)

    def one(i, carry):
        column, y = split_cells(cells_ref[i], rows, cols)
        if has_kept:
            chosen = kept_ref[:, stretch(i, slots)]
        else:
            chosen = one_hot(column, added.shape[1], slots)
        parts = [back_ref[helper_ref[0, 0, i * per_chunk + j]].astype(F32)[:comps] for j in range(per_chunk)]
        correction = jnp.concatenate(parts, axis=1)
        at_row = row_number == y
        spread = jnp.concatenate(
            [jnp.where(at_row, correction[c : c + 1], 0.0).astype(BF16) for c in range(comps)], axis=0
        )
        product = lax.dot_general(spread, chosen, (((1,), (1,)), ((), ())), preferred_element_type=F32)
        added[...] = product if chunks == 1 else added[...] + product
        return carry

    unrolled(chunks, 1, one)
    for k in range(layers):
        for c in range(comps):
            second_ref[k, c] = first_ref[k, c] + added[c * rows : (c + 1) * rows, k * cols : (k + 1) * cols]
    write_edges(second_ref, mask_ref, None, masked_ref, side_y, sends)
    total = back_ref[0].astype(F32)[comps:]
    for b in range(1, back_ref.shape[0]):
        total += back_ref[b].astype(F32)[comps:]
    whole = total
    for part in range(1, PARTS):
        whole += pltpu.roll(total, width - part * comps, 1)
    grad_ref[...] = (whole * scale)[:, :comps]


def scatter(first, back, helper, cells, mask, kept, scale):
    layers, comps, rows, cols = first.shape
    smem = pl.BlockSpec(memory_space=pltpu.SMEM)
    vmem = pl.BlockSpec(memory_space=pltpu.VMEM)
    edges = edge_shapes(*first.shape)
    return pl.pallas_call(
        functools.partial(scatter_kernel, scale, len(kept)),
        in_specs=[smem] + [vmem] * (4 + len(kept)),
        out_specs=[vmem] * (3 + len(edges)),
        out_shape=[
            pltpu.VMEM(first.shape, F32),
            pltpu.VMEM(first.shape, F32),
            *edges,
            jax.ShapeDtypeStruct((comps, comps), F32),
        ],
        scratch_shapes=[pltpu.VMEM((comps * rows, layers * cols), F32), edge_scratch(layers, comps, cols)],
        compiler_params=params(24),
        cost_estimate=cost(2 * first.size * cells.size, 8 * first.size),
    )(helper, cells, back, first, mask, *kept)


def shards(
    cotangent,
    permeability,
    well_mask,
    diag_block,
    flux_block,
    cell_list,
    block_count,
    helper_of,
    flash_inverse,
    flash_coupling,
    phase_state,
):
    layers, comps, rows, cols = cotangent.shape
    slots, width = helper_of.shape[-1], flash_inverse.shape[-1]
    inverse = flash_inverse.reshape(slots, comps, comps, width)
    coupling = flash_coupling.reshape(slots, comps, comps, width)
    state = phase_state.reshape(slots, comps, width)

    def cells(chunk):
        return cell_list.reshape(-1, 1, min(chunk, cell_list.shape[-1]))

    def to_partners(array):
        return lax.all_to_all(array, AXES, split_axis=0, concat_axis=0, tiled=True)

    *sides, masked, field, mask, perm, place = opening(cotangent, well_mask, permeability, diag_block, flux_block)
    halos = exchange(*sides)
    blocks = [pltpu.with_memory_space_constraint(block, pltpu.VMEM) for block in (diag_block, flux_block)]
    inner, begun, inner_weights = apply_rows(True, True, field, masked, mask, place, halos, blocks, perm)
    first, rounded, outer_weights = apply_rows(
        True, False, field, masked, mask, place, halos, blocks, perm, inner, begun
    )
    sent, *chosen = gather(rounded, cells(GATHER_CHUNK), helper_of, block_count, comps, rows, cols, width)
    reply = at_helper(inverse, coupling, state, to_partners(sent))
    devices = lax.axis_size("gx") * lax.axis_size("gy")
    scale = -1.0 / math.sqrt(width * devices * devices)
    second, masked, *sides, interaction_grad = scatter(
        first, to_partners(reply), helper_of, cells(SCATTER_CHUNK), mask, chosen, scale
    )
    halos = exchange(*sides)
    inner, begun = apply_rows(False, True, second, masked, mask, place, halos, blocks, inner_weights)
    (adjoint,) = apply_rows(False, False, second, masked, mask, place, halos, blocks, outer_weights, inner, begun)
    return (adjoint, interaction_grad)


def solution(mesh):
    return jax.shard_map(
        shards,
        mesh=mesh,
        in_specs=(
            P(None, None, "gy", "gx"),
            P(None, "gy", "gx"),
            P("gy", "gx"),
            P(None, None, None, "gy", "gx"),
            P(None, None, None, "gy", "gx"),
            P("gy", "gx", None),
            P("gy", "gx"),
            P("gy", "gx", None),
            P("gy", "gx", None, None, None, None),
            P("gy", "gx", None, None, None, None),
            P("gy", "gx", None, None, None),
        ),
        out_specs=(P(None, None, "gy", "gx"), P()),
        check_vma=False,
    )
```
